32 devices in a mesh: ctx: 8 (over z, x), dp: 4 (over y, core).
Axes of the slice: x: 2, y: 2, z: 4, core: 2. Of those that a mesh axis runs over, the one named last changes fastest.
Arguments:
- query: bfloat16 [4, 1024, 1024], P('dp', 'ctx')
- key: bfloat16 [4, 1024, 1024], P('dp', 'ctx')
- value: bfloat16 [4, 1024, 1024], P('dp', 'ctx'), may hold values from -5 to 5
- dout: bfloat16 [4, 1024, 1024], P('dp', 'ctx'), may hold values from -5 to 5
- glob_keys: bfloat16 [4, 64, 1024], replicated, may hold values from -5 to 5
- glob_values: bfloat16 [4, 64, 1024], replicated, may hold values from -5 to 5
- glob_ids: int32 [4, 2], P('dp'), may hold values from 0 to 3, all different within a row
- rand_blocks: int32 [8, 16, 3], replicated, may hold values from 0 to 15, as said below
Outputs:
- d_query: bfloat16 [4, 1024, 1024], P('dp', 'ctx')
- d_key: bfloat16 [4, 1024, 1024], P('dp', 'ctx')
- d_value: bfloat16 [4, 1024, 1024], P('dp', 'ctx')
- d_global: float32 [2, 4, 64, 1024], replicated
The draws below stay inside these ranges and needn't reach their ends.
Inputs may be any that keep to these rules, and one draw needn't show every extreme that they name: With P = 8 and o_r = (r + 1) * P // 4, rand_blocks[h, i, r] lies in the span of blocks 2 * q to 2 * (q + 1) - 1, where q = (i // 2 + o_r) mod P.
All inputs are finite; a program needn't handle non-finite values.
Results may differ from the reference program's by a relative error of at most 0.015.
Values may be sent and summed in bfloat16 or wider, within the bound.
No kernel may reach another device: no remote copies, remote signals or barrier semaphores. Data moves between devices by JAX's collectives and lax.ppermute only.
A program may use at most 64 MiB of HBM per device.

```python
import math
import jax
import jax.numpy as jnp
from jax import lax

HEADS = 8
HS = 128
BLK = 64
RAND = 3
GTAB = 4
BLK_DEV = 2
HD = 1024
NBLK = 16
SEQ = 1024
BATCH = 4


def base_draw(key, salt):
    sub_key = jax.random.fold_in(key, salt)
    return jnp.clip(jax.random.normal(sub_key, (BATCH, SEQ, HD), jnp.float32), -4.0, 4.0)


def shared_keys(key):
    keys_base = base_draw(key, 11)
    return keys_base


def draw_key(key, part):
    return shared_keys(key).astype(jnp.bfloat16)


def draw_query(key, part):
    queries = base_draw(key, 12)
    return queries.astype(jnp.bfloat16)


def draw_rand_blocks(key, part):
    span_count = NBLK // BLK_DEV
    blocks = jnp.arange(NBLK, dtype=jnp.int32)
    owners = blocks // BLK_DEV
    slots = jnp.arange(RAND, dtype=jnp.int32)
    shifts = (slots + 1) * span_count // (RAND + 1)
    targets = (owners[:, None] + shifts[None, :]) % span_count
    inside = jax.random.randint(key, (HEADS, NBLK, RAND), 0, BLK_DEV)
    drawn = targets[None, :, :] * BLK_DEV + inside
    return drawn.astype(jnp.int32)


def block_scale(rng, dims, cuts, smallest, top_value):
    def one(dim, shards_of):
        draws = jax.random.uniform(jax.random.fold_in(jax.random.fold_in(rng, 6), dim), (shards_of,), jnp.float32, smallest / len(cuts), top_value / len(cuts))
        return jnp.repeat(jnp.exp(draws), dims[dim] // shards_of).reshape((-1,) + (1,) * (len(dims) - dim - 1))

    level = one(*cuts[0])
    for cut in cuts[1:]:
        level = level * one(*cut)
    return level


def distinct(own_key, rows, amount, top, lift):
    ranking = jax.random.permutation(jax.random.fold_in(own_key, 1), amount)
    boost = ranking
    for power in range(3):
        boost = boost * boost // amount
    boost = boost * lift // amount
    lots = jax.random.randint(jax.random.fold_in(own_key, 2), (rows, amount), 0, 4096) + boost
    sure = jax.random.permutation(jax.random.fold_in(own_key, 3), rows)[jnp.arange(amount) % rows]
    lots = jnp.where(jnp.arange(rows)[:, None] == sure[None, :], 1 << 14, lots)
    priority = lots * amount + jnp.arange(amount)
    return lax.top_k(priority.astype(jnp.int32), top)[1].astype(jnp.int32)


def bell_draw(rng, extent, spread, reach, cuts=(), kind=jnp.bfloat16):
    array = jax.random.normal(rng, extent, jnp.float32) * spread
    if len(cuts) > 0:
        array = block_scale(rng, extent, cuts, -0.22, 0.18) * array
    return jnp.clip(array, min=-reach, max=reach).astype(kind)


def setup_inputs(seed: int = 0) -> dict:
    splits = jax.random.split(jax.random.key(seed), 9)
    query = draw_query(jax.random.fold_in(splits[8], 71), 0)
    key = draw_key(jax.random.fold_in(splits[8], 71), 0)
    value = bell_draw(splits[2], (BATCH, SEQ, HD), 1.0, 5.0, ((0, 4), (1, 8)))
    dout = bell_draw(splits[3], (BATCH, SEQ, HD), 1.0, 5.0, ((0, 4), (1, 8)))
    glob_keys = bell_draw(splits[4], (GTAB, BLK, HD), 1.0, 5.0)
    glob_values = bell_draw(splits[5], (GTAB, BLK, HD), 1.0, 5.0)
    glob_ids = distinct(splits[6], BATCH, GTAB, 2, 0)
    rand_blocks = draw_rand_blocks(jax.random.fold_in(splits[8], 71), 0)
    return dict(query=query, key=key, value=value, dout=dout, glob_keys=glob_keys, glob_values=glob_values, glob_ids=glob_ids, rand_blocks=rand_blocks)


def rounded(values):
    return lax.optimization_barrier(values.astype(jnp.bfloat16)).astype(jnp.float32)

def attend(q_head, o_grad, k_head, v_head, gk_head, gv_head, key_index, key_valid):
    q_blocks = q_head.shape[0]
    head_size = q_head.shape[2]
    scaling = 1.0 / math.sqrt(head_size)
    local_lists = key_index.shape[1]
    keys_all = jnp.concatenate([jnp.take(k_head, key_index, axis=0), jnp.broadcast_to(gk_head[None], (q_blocks,) + gk_head.shape)], axis=1).reshape(q_blocks, -1, head_size)
    values_all = jnp.concatenate([jnp.take(v_head, key_index, axis=0), jnp.broadcast_to(gv_head[None], (q_blocks,) + gv_head.shape)], axis=1).reshape(q_blocks, -1, head_size)
    keep_mask = jnp.repeat(jnp.concatenate([key_valid, jnp.ones((q_blocks, 2), dtype=bool)], axis=1), BLK, axis=1)
    q_float = q_head.astype(jnp.float32)
    grad_float = o_grad.astype(jnp.float32)
    keys_float = keys_all.astype(jnp.float32)
    values_float = values_all.astype(jnp.float32)
    scores = jnp.einsum('nqd,nkd->nqk', q_float, keys_float) * scaling
    scores = jnp.where(keep_mask[:, None, :], scores, -1e+30)
    row_max = lax.optimization_barrier(jnp.max(scores, axis=-1, keepdims=True))
    exp_scores = jnp.exp(scores - row_max)
    weights = exp_scores / lax.optimization_barrier(jnp.sum(exp_scores, axis=-1, keepdims=True))
    weights_b = rounded(weights)
    attn_out = jnp.einsum('nqk,nkd->nqd', weights_b, values_float)
    row_dot = lax.optimization_barrier(jnp.sum(grad_float * attn_out, axis=-1, keepdims=True))
    prob_grad = jnp.einsum('nqd,nkd->nqk', grad_float, values_float)
    score_grad = rounded(weights * (prob_grad - row_dot) * scaling)
    q_grad = jnp.einsum('nqk,nkd->nqd', score_grad, keys_float)
    k_grad = jnp.einsum('nqk,nqd->nkd', score_grad, q_float).reshape(q_blocks, local_lists + 2, BLK, head_size)
    v_grad = jnp.einsum('nqk,nqd->nkd', weights_b, grad_float).reshape(q_blocks, local_lists + 2, BLK, head_size)
    flat_index = key_index.reshape(-1)
    k_local = jnp.zeros(k_head.shape, jnp.float32).at[flat_index].add(k_grad[:, :local_lists].reshape(-1, BLK, head_size))
    v_local = jnp.zeros(v_head.shape, jnp.float32).at[flat_index].add(v_grad[:, :local_lists].reshape(-1, BLK, head_size))
    return (q_grad, k_local, v_local, k_grad[:, local_lists:], v_grad[:, local_lists:])

def by_heads(row_array):
    block_total = row_array.shape[0] // BLK
    return row_array.reshape(block_total, BLK, HEADS, HS).transpose(2, 0, 1, 3)

def from_heads(head_array):
    return head_array.transpose(1, 2, 0, 3).reshape(-1, HEADS * HS)

def reference(query, key, value, dout, glob_keys, glob_values, glob_ids, rand_blocks):
    block_count = SEQ // BLK
    blocks = jnp.arange(block_count, dtype=jnp.int32)
    window = blocks[:, None] + jnp.arange(-1, 2, dtype=jnp.int32)[None, :]
    key_valid = jnp.concatenate([(window >= 0) & (window < block_count), jnp.ones((block_count, RAND), dtype=bool)], axis=1)
    table_grad = jnp.zeros((2, GTAB, BLK, HD), jnp.float32)
    q_grads = []
    k_grads = []
    v_grads = []
    for batch_row in range(BATCH):
        chosen = glob_ids[batch_row]
        gk_heads = jnp.take(glob_keys, chosen, axis=0).reshape(2, BLK, HEADS, HS).transpose(2, 0, 1, 3)
        gv_heads = jnp.take(glob_values, chosen, axis=0).reshape(2, BLK, HEADS, HS).transpose(2, 0, 1, 3)

        def per_head(pieces):
            q_head, o_grad, k_head, v_head, gk_head, gv_head, rand_head = pieces
            key_index = jnp.clip(jnp.concatenate([window, rand_head], axis=1), 0, block_count - 1).astype(jnp.int32)
            q_grad, k_local, v_local, gk_grad, gv_grad = attend(q_head, o_grad, k_head, v_head, gk_head, gv_head, key_index, key_valid)
            return (q_grad, k_local, v_local, lax.optimization_barrier(jnp.sum(gk_grad, axis=0)), lax.optimization_barrier(jnp.sum(gv_grad, axis=0)))
        results = lax.map(per_head, (by_heads(query[batch_row]), by_heads(dout[batch_row]), by_heads(key[batch_row]), by_heads(value[batch_row]), gk_heads, gv_heads, rand_blocks))
        q_grads.append(from_heads(results[0]).astype(jnp.bfloat16))
        k_grads.append(from_heads(results[1]).astype(jnp.bfloat16))
        v_grads.append(from_heads(results[2]).astype(jnp.bfloat16))
        gk_sum = results[3].transpose(1, 2, 0, 3).reshape(2, BLK, HD)
        gv_sum = results[4].transpose(1, 2, 0, 3).reshape(2, BLK, HD)
        table_grad = table_grad.at[0, chosen].add(gk_sum)
        table_grad = table_grad.at[1, chosen].add(gv_sum)
    return (jnp.stack(q_grads), jnp.stack(k_grads), jnp.stack(v_grads), table_grad)
```

```python
import functools
import math

import jax
import jax.numpy as jnp
from jax import lax
from jax.experimental import pallas as pl
from jax.experimental.pallas import tpu as pltpu
from jax.sharding import PartitionSpec as P

BLK = 64


def passed_along(shard, axis, by):
    length = lax.axis_size(axis)
    return lax.ppermute(shard, axis, [(i, (i + by) % length) for i in range(length)])


def padded(cells, sides, width):
    for axis, dim in sides:
        count = lax.axis_size(axis)
        ends = count - 1
        head = lax.slice_in_dim(cells, 0, width, axis=dim)
        tail = lax.slice_in_dim(cells, cells.shape[dim] - width, cells.shape[dim], axis=dim)
        cells = jnp.concatenate(
            [
                lax.ppermute(tail, axis, [(i, (i + 1) % count) for i in range(ends)]),
                cells,
                lax.ppermute(head, axis, [((i + 1) % count, i) for i in range(ends)]),
            ],
            axis=dim,
        )
    return cells


def passed_along_2(value, axis, steps):
    count = lax.axis_size(axis)
    leading, last = (max(0, -steps), min(count, count - steps))
    return lax.ppermute(value, axis, [(source, source + steps) for source in range(leading, last)])


def attend(
    q_head,
    o_grad,
    k_head,
    v_head,
    gk_head,
    gv_head,
    key_index,
    key_valid,
    scatter_count,
    rand_count,
):
    q_blocks = q_head.shape[0]
    head_size = q_head.shape[2]
    scaling = 1.0 / math.sqrt(head_size)
    local_lists = key_index.shape[1]
    keys_all = jnp.concatenate(
        [
            jnp.take(k_head, key_index, axis=0),
            jnp.broadcast_to(gk_head[None], (q_blocks,) + gk_head.shape),
        ],
        axis=1,
    ).reshape(q_blocks, -1, head_size)
    values_all = jnp.concatenate(
        [
            jnp.take(v_head, key_index, axis=0),
            jnp.broadcast_to(gv_head[None], (q_blocks,) + gv_head.shape),
        ],
        axis=1,
    ).reshape(q_blocks, -1, head_size)
    keep_mask = jnp.repeat(
        jnp.concatenate([key_valid, jnp.ones((q_blocks, 2), dtype=bool)], axis=1), BLK, axis=1
    )
    scores = (
        jnp.einsum("nqd,nkd->nqk", q_head, keys_all, preferred_element_type=jnp.float32) * scaling
    )
    scores = jnp.where(keep_mask[:, None, :], scores, -1e30)
    row_max = jnp.max(scores, axis=-1, keepdims=True)
    exp_scores = jnp.exp(scores - row_max)
    weights = exp_scores / jnp.sum(exp_scores, axis=-1, keepdims=True)
    weights_b = weights.astype(jnp.bfloat16)
    attn_out = jnp.einsum("nqk,nkd->nqd", weights_b, values_all, preferred_element_type=jnp.float32)
    row_dot = jnp.sum(o_grad.astype(jnp.float32) * attn_out, axis=-1, keepdims=True)
    prob_grad = jnp.einsum("nqd,nkd->nqk", o_grad, values_all, preferred_element_type=jnp.float32)
    score_grad = (weights * (prob_grad - row_dot) * scaling).astype(jnp.bfloat16)
    q_grad = jnp.einsum("nqk,nkd->nqd", score_grad, keys_all, preferred_element_type=jnp.float32)
    k_grad = jnp.einsum(
        "nqk,nqd->nkd", score_grad, q_head, preferred_element_type=jnp.float32
    ).reshape(q_blocks, local_lists + 2, BLK, head_size)
    v_grad = jnp.einsum(
        "nqk,nqd->nkd", weights_b, o_grad, preferred_element_type=jnp.float32
    ).reshape(q_blocks, local_lists + 2, BLK, head_size)
    flat_index = key_index.reshape(-1)
    k_local = (
        jnp.zeros(k_head.shape, jnp.float32)
        .at[flat_index]
        .add(k_grad[:, :scatter_count].reshape(-1, BLK, head_size))
    )
    v_local = (
        jnp.zeros(v_head.shape, jnp.float32)
        .at[flat_index]
        .add(v_grad[:, :scatter_count].reshape(-1, BLK, head_size))
    )
    grad_tiles = score_grad.reshape(q_blocks, BLK, local_lists + 2, BLK)[
        :, :, 3 : 3 + rand_count
    ].transpose(0, 2, 1, 3)
    prob_tiles = weights_b.reshape(q_blocks, BLK, local_lists + 2, BLK)[
        :, :, 3 : 3 + rand_count
    ].transpose(0, 2, 1, 3)
    return (
        q_grad,
        k_local,
        v_local,
        k_grad[:, local_lists:],
        v_grad[:, local_lists:],
        grad_tiles,
        prob_tiles,
    )


def by_heads(row_array, head_count):
    block_total = row_array.shape[0] // BLK
    return row_array.reshape(block_total, BLK, head_count, -1).transpose(2, 0, 1, 3)


def from_heads(head_array):
    head_count = head_array.shape[0]
    head_size = head_array.shape[3]
    return head_array.transpose(1, 2, 0, 3).reshape(-1, head_count * head_size)


def fetch_far(key_value, offset):
    return passed_along(key_value, "ctx", -offset)


def return_far(partials, offset):
    return passed_along(partials, "ctx", offset)


def on_ring(query, key, value, dout, glob_keys, glob_values, glob_ids, rand_blocks):
    row_count = query.shape[1]
    head_count = rand_blocks.shape[0]
    rand_count = rand_blocks.shape[2]
    head_size = query.shape[2] // head_count
    per_device = row_count // BLK
    span_count = lax.axis_size("ctx")
    device_pos = lax.axis_index("ctx")
    block_count = per_device * span_count
    offsets = [(slot + 1) * span_count // (rand_count + 1) for slot in range(rand_count)]
    key_value = jnp.stack([key[0], value[0]])
    extended = padded(key_value, (("ctx", 1),), row_count)
    far_spans = [fetch_far(key_value, offset) for offset in offsets]
    k_rows = jnp.concatenate([extended[0]] + [span[0] for span in far_spans], axis=0)
    v_rows = jnp.concatenate([extended[1]] + [span[1] for span in far_spans], axis=0)
    first_block = device_pos * per_device
    key_base = first_block - per_device
    query_ids = first_block + jnp.arange(per_device, dtype=jnp.int32)
    window = query_ids[:, None] + jnp.arange(-1, 2, dtype=jnp.int32)[None, :]
    key_valid = jnp.concatenate(
        [(window >= 0) & (window < block_count), jnp.ones((per_device, rand_count), dtype=bool)],
        axis=1,
    )
    window_local = jnp.clip(window - key_base, 0, 3 * per_device - 1)
    rand_rows = lax.dynamic_slice_in_dim(rand_blocks, first_block, per_device, 1)
    offset_table = jnp.array(offsets, dtype=jnp.int32)
    far_starts = (device_pos + offset_table) % span_count * per_device
    slot_base = (3 + jnp.arange(rand_count, dtype=jnp.int32)) * per_device
    rand_local = rand_rows - far_starts[None, None, :] + slot_base[None, None, :]
    all_lists = jnp.concatenate(
        [jnp.broadcast_to(window_local[None], (head_count,) + window_local.shape), rand_local],
        axis=2,
    )
    key_index = jnp.clip(all_lists, 0, (3 + rand_count) * per_device - 1)
    chosen = glob_ids[0]
    gk_heads = by_heads(jnp.take(glob_keys, chosen, axis=0).reshape(2 * BLK, -1), head_count)
    gv_heads = by_heads(jnp.take(glob_values, chosen, axis=0).reshape(2 * BLK, -1), head_count)
    scatter_count = 3 + rand_count

    def per_head(pieces):
        q_head, o_grad, k_head, v_head, gk_head, gv_head, index_head = pieces
        return attend(
            q_head,
            o_grad,
            k_head,
            v_head,
            gk_head,
            gv_head,
            index_head,
            key_valid,
            scatter_count,
            rand_count,
        )

    results = lax.map(
        per_head,
        (
            by_heads(query[0], head_count),
            by_heads(dout[0], head_count),
            by_heads(k_rows, head_count),
            by_heads(v_rows, head_count),
            gk_heads,
            gv_heads,
            key_index,
        ),
    )
    q_grad = results[0]
    kv_grads = jnp.stack([results[1], results[2]])
    lower_part = kv_grads[:, :, :per_device]
    upper_part = kv_grads[:, :, 2 * per_device : 3 * per_device]
    from_below = passed_along_2(upper_part.astype(jnp.bfloat16), "ctx", 1).astype(upper_part.dtype)
    from_above = passed_along_2(lower_part.astype(jnp.bfloat16), "ctx", -1).astype(lower_part.dtype)
    own_grads = kv_grads[:, :, per_device : 2 * per_device] + from_below + from_above
    for slot in range(rand_count):
        start = (3 + slot) * per_device
        own_grads = own_grads + return_far(
            kv_grads[:, :, start : start + per_device], offsets[slot]
        )
    global_part = jnp.stack([jnp.sum(results[3], axis=1), jnp.sum(results[4], axis=1)])
    global_part = global_part.transpose(0, 2, 3, 1, 4).reshape(2, 2, BLK, head_count * head_size)
    one_hot = (chosen[:, None] == jnp.arange(glob_keys.shape[0], dtype=jnp.int32)[None, :]).astype(
        jnp.float32
    )
    table_term = jnp.einsum("sg,ksbd->kgbd", one_hot, global_part, precision=lax.Precision.HIGHEST)
    table_grad = lax.psum(table_term, ("ctx", "dp"))
    d_query = from_heads(q_grad).astype(jnp.bfloat16)[None]
    d_key = from_heads(own_grads[0]).astype(jnp.bfloat16)[None]
    d_value = from_heads(own_grads[1]).astype(jnp.bfloat16)[None]
    return (d_query, d_key, d_value, table_grad)


VMEM_BYTES = 48 * 1024 * 1024
MASKED = -1e30


def dot(left, right, left_dim, right_dim):
    dims = (((left_dim,), (right_dim,)), ((), ()))
    return lax.dot_general(left, right, dims, preferred_element_type=jnp.float32)


def pack_kernel(q_ref, k_ref, v_ref, o_ref, out_ref):
    head_size = out_ref.shape[3]
    for head in range(out_ref.shape[0]):
        columns = slice(head * head_size, (head + 1) * head_size)
        for place, ref in enumerate((q_ref, k_ref, v_ref, o_ref)):
            out_ref[head, place] = ref[0, :, columns]


def pack(query, key, value, dout, head_count):
    _, rows, width = query.shape
    return pl.pallas_call(
        pack_kernel,
        out_shape=jax.ShapeDtypeStruct((head_count, 4, rows, width // head_count), query.dtype),
        compiler_params=pltpu.CompilerParams(vmem_limit_bytes=VMEM_BYTES),
        cost_estimate=pl.CostEstimate(flops=0, bytes_accessed=16 * rows * width, transcendentals=0),
        name="pack_heads",
    )(query, key, value, dout)


def head_kernel(
    place_ref,
    rand_ref,
    x_ref,
    gk0_ref,
    gk1_ref,
    gv0_ref,
    gv1_ref,
    send_ref,
    table_ref,
    k_all,
    v_all,
    dk_all,
    dv_all,
    dgk,
    dgv,
):
    spans, _, rows, head_size = x_ref.shape
    rand_count = rand_ref.shape[0] // (2 * spans)
    scaling = 1.0 / math.sqrt(head_size)
    top = BLK + spans * rows
    for pool in (k_all, v_all, dk_all, dv_all):
        pool[:BLK] = jnp.zeros((BLK, head_size), pool.dtype)
        pool[top:] = jnp.zeros((BLK, head_size), pool.dtype)
    for pool in (dk_all, dv_all):
        pool[BLK:top] = jnp.zeros((top - BLK, head_size), pool.dtype)
    for span in range(spans):
        at = BLK + span * rows
        k_all[at : at + rows] = x_ref[span, 1]
        v_all[at : at + rows] = x_ref[span, 2]
    gk = [gk0_ref[0], gk1_ref[0]]
    gv = [gv0_ref[0], gv1_ref[0]]
    shared = 4 * BLK
    own = (1 + rand_count) * BLK
    first = lax.broadcasted_iota(jnp.int32, (1, rows), 1) < BLK
    empty = jnp.zeros((BLK, head_size), x_ref.dtype)

    def split(block):
        return jnp.concatenate(
            [
                jnp.concatenate([block[:BLK], empty], axis=0),
                jnp.concatenate([empty, block[BLK:]], axis=0),
            ],
            axis=1,
        )

    for span in range(spans):
        at = span * rows
        q = x_ref[span, 0]
        o = x_ref[span, 3]
        q_split = split(q)
        o_split = split(o)
        places = [
            [
                pl.multiple_of((rand_ref[(2 * span + half) * rand_count + slot] + 1) * BLK, BLK)
                for slot in range(rand_count)
            ]
            for half in range(2)
        ]

        def gathered(pool, table):
            window = pool[at : at + 4 * BLK]
            lists = [
                jnp.concatenate([edge] + [pool[pl.ds(p, BLK)] for p in places[half]], axis=0)
                for half, edge in enumerate((window[:BLK], window[3 * BLK :]))
            ]
            both = jnp.concatenate([window[BLK : 3 * BLK]] + table, axis=0)
            return jnp.concatenate(lists, axis=1), both

        k_own, k_both = gathered(k_all, gk)
        v_own, v_both = gathered(v_all, gv)
        s_own = dot(k_own, q_split, 1, 1) * scaling
        s_both = dot(k_both, q, 1, 1) * scaling
        if span == 0 or span == spans - 1:
            row = lax.broadcasted_iota(jnp.int32, (own, 1), 0) < BLK
            outside = row & (first if span == 0 else jnp.logical_not(first))
            s_own = jnp.where(outside, MASKED, s_own)
        top_score = jnp.maximum(
            jnp.max(s_own, axis=0, keepdims=True), jnp.max(s_both, axis=0, keepdims=True)
        )
        e_own = jnp.exp(s_own - top_score)
        e_both = jnp.exp(s_both - top_score)
        total = jnp.sum(e_own, axis=0, keepdims=True) + jnp.sum(e_both, axis=0, keepdims=True)
        inverse = 1.0 / total
        p_own = e_own * inverse
        p_both = e_both * inverse
        pb_own = p_own.astype(jnp.bfloat16)
        pb_both = p_both.astype(jnp.bfloat16)
        g_own = dot(v_own, o_split, 1, 1)
        g_both = dot(v_both, o, 1, 1)
        row_dot = jnp.sum(pb_own.astype(jnp.float32) * g_own, axis=0, keepdims=True) + jnp.sum(
            pb_both.astype(jnp.float32) * g_both, axis=0, keepdims=True
        )
        ds_own = (p_own * (g_own - row_dot) * scaling).astype(jnp.bfloat16)
        ds_both = (p_both * (g_both - row_dot) * scaling).astype(jnp.bfloat16)
        wide = dot(ds_own, k_own, 0, 0)
        dq = jnp.concatenate([wide[:BLK, :head_size], wide[BLK:, head_size:]], axis=0)
        dq = dq + dot(ds_both, k_both, 0, 0)
        send_ref[span, 0] = dq.astype(jnp.bfloat16)
        for weights_own, weights_both, x_split, x, pool, table in (
            (ds_own, ds_both, q_split, q, dk_all, dgk),
            (pb_own, pb_both, o_split, o, dv_all, dgv),
        ):
            d_own = dot(weights_own, x_split, 1, 0)
            d_both = dot(weights_both, x, 1, 0)
            pool[at + BLK : at + 3 * BLK] += d_both[: 2 * BLK]
            if span == 0:
                table[...] = d_both[2 * BLK :]
            else:
                table[...] += d_both[2 * BLK :]
            pool[at : at + BLK] += d_own[:BLK, :head_size]
            pool[at + 3 * BLK : at + 4 * BLK] += d_own[:BLK, head_size:]
            for half in range(2):
                columns = slice(half * head_size, (half + 1) * head_size)
                for slot, p in enumerate(places[half]):
                    pool[pl.ds(p, BLK)] += d_own[(1 + slot) * BLK : (2 + slot) * BLK, columns]
    for span in range(spans):
        at = BLK + span * rows
        send_ref[span, 1] = dk_all[at : at + rows].astype(jnp.bfloat16)
        send_ref[span, 2] = dv_all[at : at + rows].astype(jnp.bfloat16)
    table_ref[...] = jnp.zeros(table_ref.shape, table_ref.dtype)
    for slot in range(2):
        for kind, table in enumerate((dgk, dgv)):
            table_ref[kind, place_ref[1 + slot]] = table[
                slot * BLK : (slot + 1) * BLK
            ].astype(table_ref.dtype)


def attend_head(x, glob_keys, glob_values, place, rand_head):
    spans, _, rows, head_size = x.shape
    table_size = glob_keys.shape[0]
    padded_rows = spans * rows + 2 * BLK
    block = (1, BLK, head_size)
    chosen = [
        pl.BlockSpec(block, lambda i, place, rand: (place[1], 0, place[0])),
        pl.BlockSpec(block, lambda i, place, rand: (place[2], 0, place[0])),
    ]
    whole = lambda *shape: pl.BlockSpec(shape, lambda i, place, rand: (0,) * len(shape))
    keys_each = spans * rows * 8 * BLK
    return pl.pallas_call(
        head_kernel,
        grid_spec=pltpu.PrefetchScalarGridSpec(
            num_scalar_prefetch=2,
            grid=(1,),
            in_specs=[whole(*x.shape)] + chosen + chosen,
            out_specs=[
                whole(spans, 3, rows, head_size),
                whole(2, table_size, BLK, head_size),
            ],
            scratch_shapes=[
                pltpu.VMEM((padded_rows, head_size), jnp.bfloat16),
                pltpu.VMEM((padded_rows, head_size), jnp.bfloat16),
                pltpu.VMEM((padded_rows, head_size), jnp.float32),
                pltpu.VMEM((padded_rows, head_size), jnp.float32),
                pltpu.VMEM((2 * BLK, head_size), jnp.float32),
                pltpu.VMEM((2 * BLK, head_size), jnp.float32),
            ],
        ),
        out_shape=[
            jax.ShapeDtypeStruct((spans, 3, rows, head_size), jnp.bfloat16),
            jax.ShapeDtypeStruct((2, table_size, BLK, head_size), jnp.bfloat16),
        ],
        compiler_params=pltpu.CompilerParams(vmem_limit_bytes=VMEM_BYTES),
        cost_estimate=pl.CostEstimate(
            flops=10 * keys_each * head_size,
            bytes_accessed=16 * spans * rows * head_size,
            transcendentals=keys_each,
        ),
        name="attend_head",
    )(place, rand_head, x, glob_keys, glob_keys, glob_values, glob_values)


def unpack_kernel(x_ref, dq_ref, dk_ref, dv_ref):
    head_size = x_ref.shape[3]
    for head in range(x_ref.shape[0]):
        columns = slice(head * head_size, (head + 1) * head_size)
        for place, ref in enumerate((dq_ref, dk_ref, dv_ref)):
            ref[0, :, columns] = x_ref[head, place]


def unpack(x):
    heads, _, rows, head_size = x.shape
    shape = jax.ShapeDtypeStruct((1, rows, heads * head_size), x.dtype)
    return pl.pallas_call(
        unpack_kernel,
        grid=(1,),
        in_specs=[pl.BlockSpec((heads, 3, rows, head_size), lambda i: (0, 0, 0, 0))],
        out_specs=[pl.BlockSpec(shape.shape, lambda i: (0, 0, 0))] * 3,
        out_shape=[shape] * 3,
        compiler_params=pltpu.CompilerParams(vmem_limit_bytes=VMEM_BYTES),
        cost_estimate=pl.CostEstimate(
            flops=0, bytes_accessed=12 * rows * heads * head_size, transcendentals=0
        ),
        name="unpack_heads",
    )(x)


def table_kernel(place_ref, *refs):
    parts, out_ref = refs[:-1], refs[-1]
    head_size = parts[0].shape[2]
    for flip, ref in enumerate(parts):
        at = place_ref[0] ^ flip
        for head in range(ref.shape[0]):
            columns = slice(head * head_size, (head + 1) * head_size)
            out_ref[at, :, columns] = ref[head].astype(out_ref.dtype)


def whole_table(me, parts):
    heads, rows, head_size = parts[0].shape
    shape = (len(parts), rows, heads * head_size)
    part = pl.BlockSpec(parts[0].shape, lambda i, me: (0, 0, 0))
    return pl.pallas_call(
        table_kernel,
        grid_spec=pltpu.PrefetchScalarGridSpec(
            num_scalar_prefetch=1,
            grid=(1,),
            in_specs=[part] * len(parts),
            out_specs=pl.BlockSpec(shape, lambda i, me: (0, 0, 0)),
        ),
        out_shape=jax.ShapeDtypeStruct(shape, jnp.float32),
        compiler_params=pltpu.CompilerParams(vmem_limit_bytes=VMEM_BYTES),
        name="whole_table",
    )(me, *parts)


def flipped(array, axis, bits):
    length = lax.axis_size(axis)
    return lax.ppermute(array, axis, [(i, i ^ bits) for i in range(length)])


def on_heads(query, key, value, dout, glob_keys, glob_values, glob_ids, rand_blocks):
    head_count, block_count, _ = rand_blocks.shape
    rows = query.shape[1]
    head_size = query.shape[2] // head_count
    table_size = glob_keys.shape[0]
    dp_count = lax.axis_size("dp")
    head = lax.axis_index("ctx")
    place = jnp.concatenate([head[None].astype(jnp.int32), glob_ids[0]])
    rand_head = lax.dynamic_index_in_dim(rand_blocks, head, 0, keepdims=False).reshape(-1)
    rand_head = jnp.clip(rand_head, 0, block_count - 1)
    packed = pack(query, key, value, dout, head_count)
    arrived = lax.all_to_all(packed, "ctx", 0, 0)
    grads, table = attend_head(arrived, glob_keys, glob_values, place, rand_head)
    shares = table.reshape(dp_count, -1, head_size)
    shares = lax.all_to_all(shares, "dp", 0, 0)
    share = jnp.sum(shares.astype(jnp.float32), axis=0).astype(jnp.bfloat16)
    share = jnp.broadcast_to(share.reshape(1, -1, rows, head_size), (head_count, 1, rows, head_size))
    back = lax.all_to_all(jnp.concatenate([grads, share], axis=1), "ctx", 0, 0)
    d_query, d_key, d_value = unpack(back)
    quarter = back[:, 3]
    beside = flipped(quarter, "dp", 1)
    across = flipped(quarter, "dp", 2)
    corner = flipped(across, "dp", 1)
    me = lax.axis_index("dp").astype(jnp.int32)[None]
    d_table = whole_table(me, [quarter, beside, across, corner])
    return (d_query, d_key, d_value, d_table.reshape((2,) + glob_keys.shape))


def on_device(query, key, value, dout, glob_keys, glob_values, glob_ids, rand_blocks):
    head_count = rand_blocks.shape[0]
    rows = query.shape[1]
    one_head_each = lax.axis_size("ctx") == head_count and rows == 2 * BLK
    shared_table = 2 * glob_keys.shape[0] * BLK == lax.axis_size("dp") * rows
    if one_head_each and shared_table and lax.axis_size("dp") == 4:
        plan = on_heads
    else:
        plan = on_ring
    return plan(query, key, value, dout, glob_keys, glob_values, glob_ids, rand_blocks)


def solution(mesh):
    placed = (
        P("dp", "ctx", None),
        P("dp", "ctx", None),
        P("dp", "ctx", None),
        P("dp", "ctx", None),
        P(),
        P(),
        P("dp", None),
        P(),
    )
    return jax.shard_map(
        on_device,
        mesh=mesh,
        in_specs=placed,
        out_specs=(P("dp", "ctx", None), P("dp", "ctx", None), P("dp", "ctx", None), P()),
        check_vma=False,
    )
```

```python
import functools
import math

import jax
import jax.numpy as jnp
from jax import lax
from jax.experimental import pallas as pl
from jax.experimental.pallas import tpu as pltpu
from jax.sharding import PartitionSpec as P

BLK = 64


def passed_along(shard, axis, by):
    length = lax.axis_size(axis)
    return lax.ppermute(shard, axis, [(i, (i + by) % length) for i in range(length)])


def padded(cells, sides, width):
    for axis, dim in sides:
        count = lax.axis_size(axis)
        ends = count - 1
        head = lax.slice_in_dim(cells, 0, width, axis=dim)
        tail = lax.slice_in_dim(cells, cells.shape[dim] - width, cells.shape[dim], axis=dim)
        cells = jnp.concatenate(
            [
                lax.ppermute(tail, axis, [(i, (i + 1) % count) for i in range(ends)]),
                cells,
                lax.ppermute(head, axis, [((i + 1) % count, i) for i in range(ends)]),
            ],
            axis=dim,
        )
    return cells


def passed_along_2(value, axis, steps):
    count = lax.axis_size(axis)
    leading, last = (max(0, -steps), min(count, count - steps))
    return lax.ppermute(value, axis, [(source, source + steps) for source in range(leading, last)])


def attend(
    q_head,
    o_grad,
    k_head,
    v_head,
    gk_head,
    gv_head,
    key_index,
    key_valid,
    scatter_count,
    rand_count,
):
    q_blocks = q_head.shape[0]
    head_size = q_head.shape[2]
    scaling = 1.0 / math.sqrt(head_size)
    local_lists = key_index.shape[1]
    keys_all = jnp.concatenate(
        [
            jnp.take(k_head, key_index, axis=0),
            jnp.broadcast_to(gk_head[None], (q_blocks,) + gk_head.shape),
        ],
        axis=1,
    ).reshape(q_blocks, -1, head_size)
    values_all = jnp.concatenate(
        [
            jnp.take(v_head, key_index, axis=0),
            jnp.broadcast_to(gv_head[None], (q_blocks,) + gv_head.shape),
        ],
        axis=1,
    ).reshape(q_blocks, -1, head_size)
    keep_mask = jnp.repeat(
        jnp.concatenate([key_valid, jnp.ones((q_blocks, 2), dtype=bool)], axis=1), BLK, axis=1
    )
    scores = (
        jnp.einsum("nqd,nkd->nqk", q_head, keys_all, preferred_element_type=jnp.float32) * scaling
    )
    scores = jnp.where(keep_mask[:, None, :], scores, -1e30)
    row_max = jnp.max(scores, axis=-1, keepdims=True)
    exp_scores = jnp.exp(scores - row_max)
    weights = exp_scores / jnp.sum(exp_scores, axis=-1, keepdims=True)
    weights_b = weights.astype(jnp.bfloat16)
    attn_out = jnp.einsum("nqk,nkd->nqd", weights_b, values_all, preferred_element_type=jnp.float32)
    row_dot = jnp.sum(o_grad.astype(jnp.float32) * attn_out, axis=-1, keepdims=True)
    prob_grad = jnp.einsum("nqd,nkd->nqk", o_grad, values_all, preferred_element_type=jnp.float32)
    score_grad = (weights * (prob_grad - row_dot) * scaling).astype(jnp.bfloat16)
    q_grad = jnp.einsum("nqk,nkd->nqd", score_grad, keys_all, preferred_element_type=jnp.float32)
    k_grad = jnp.einsum(
        "nqk,nqd->nkd", score_grad, q_head, preferred_element_type=jnp.float32
    ).reshape(q_blocks, local_lists + 2, BLK, head_size)
    v_grad = jnp.einsum(
        "nqk,nqd->nkd", weights_b, o_grad, preferred_element_type=jnp.float32
    ).reshape(q_blocks, local_lists + 2, BLK, head_size)
    flat_index = key_index.reshape(-1)
    k_local = (
        jnp.zeros(k_head.shape, jnp.float32)
        .at[flat_index]
        .add(k_grad[:, :scatter_count].reshape(-1, BLK, head_size))
    )
    v_local = (
        jnp.zeros(v_head.shape, jnp.float32)
        .at[flat_index]
        .add(v_grad[:, :scatter_count].reshape(-1, BLK, head_size))
    )
    grad_tiles = score_grad.reshape(q_blocks, BLK, local_lists + 2, BLK)[
        :, :, 3 : 3 + rand_count
    ].transpose(0, 2, 1, 3)
    prob_tiles = weights_b.reshape(q_blocks, BLK, local_lists + 2, BLK)[
        :, :, 3 : 3 + rand_count
    ].transpose(0, 2, 1, 3)
    return (
        q_grad,
        k_local,
        v_local,
        k_grad[:, local_lists:],
        v_grad[:, local_lists:],
        grad_tiles,
        prob_tiles,
    )


def by_heads(row_array, head_count):
    block_total = row_array.shape[0] // BLK
    return row_array.reshape(block_total, BLK, head_count, -1).transpose(2, 0, 1, 3)


def from_heads(head_array):
    head_count = head_array.shape[0]
    head_size = head_array.shape[3]
    return head_array.transpose(1, 2, 0, 3).reshape(-1, head_count * head_size)


def fetch_far(key_value, offset):
    return passed_along(key_value, "ctx", -offset)


def return_far(partials, offset):
    return passed_along(partials, "ctx", offset)


def on_ring(query, key, value, dout, glob_keys, glob_values, glob_ids, rand_blocks):
    row_count = query.shape[1]
    head_count = rand_blocks.shape[0]
    rand_count = rand_blocks.shape[2]
    head_size = query.shape[2] // head_count
    per_device = row_count // BLK
    span_count = lax.axis_size("ctx")
    device_pos = lax.axis_index("ctx")
    block_count = per_device * span_count
    offsets = [(slot + 1) * span_count // (rand_count + 1) for slot in range(rand_count)]
    key_value = jnp.stack([key[0], value[0]])
    extended = padded(key_value, (("ctx", 1),), row_count)
    far_spans = [fetch_far(key_value, offset) for offset in offsets]
    k_rows = jnp.concatenate([extended[0]] + [span[0] for span in far_spans], axis=0)
    v_rows = jnp.concatenate([extended[1]] + [span[1] for span in far_spans], axis=0)
    first_block = device_pos * per_device
    key_base = first_block - per_device
    query_ids = first_block + jnp.arange(per_device, dtype=jnp.int32)
    window = query_ids[:, None] + jnp.arange(-1, 2, dtype=jnp.int32)[None, :]
    key_valid = jnp.concatenate(
        [(window >= 0) & (window < block_count), jnp.ones((per_device, rand_count), dtype=bool)],
        axis=1,
    )
    window_local = jnp.clip(window - key_base, 0, 3 * per_device - 1)
    rand_rows = lax.dynamic_slice_in_dim(rand_blocks, first_block, per_device, 1)
    offset_table = jnp.array(offsets, dtype=jnp.int32)
    far_starts = (device_pos + offset_table) % span_count * per_device
    slot_base = (3 + jnp.arange(rand_count, dtype=jnp.int32)) * per_device
    rand_local = rand_rows - far_starts[None, None, :] + slot_base[None, None, :]
    all_lists = jnp.concatenate(
        [jnp.broadcast_to(window_local[None], (head_count,) + window_local.shape), rand_local],
        axis=2,
    )
    key_index = jnp.clip(all_lists, 0, (3 + rand_count) * per_device - 1)
    chosen = glob_ids[0]
    gk_heads = by_heads(jnp.take(glob_keys, chosen, axis=0).reshape(2 * BLK, -1), head_count)
    gv_heads = by_heads(jnp.take(glob_values, chosen, axis=0).reshape(2 * BLK, -1), head_count)
    scatter_count = 3 + rand_count

    def per_head(pieces):
        q_head, o_grad, k_head, v_head, gk_head, gv_head, index_head = pieces
        return attend(
            q_head,
            o_grad,
            k_head,
            v_head,
            gk_head,
            gv_head,
            index_head,
            key_valid,
            scatter_count,
            rand_count,
        )

    results = lax.map(
        per_head,
        (
            by_heads(query[0], head_count),
            by_heads(dout[0], head_count),
            by_heads(k_rows, head_count),
            by_heads(v_rows, head_count),
            gk_heads,
            gv_heads,
            key_index,
        ),
    )
    q_grad = results[0]
    kv_grads = jnp.stack([results[1], results[2]])
    lower_part = kv_grads[:, :, :per_device]
    upper_part = kv_grads[:, :, 2 * per_device : 3 * per_device]
    from_below = passed_along_2(upper_part.astype(jnp.bfloat16), "ctx", 1).astype(upper_part.dtype)
    from_above = passed_along_2(lower_part.astype(jnp.bfloat16), "ctx", -1).astype(lower_part.dtype)
    own_grads = kv_grads[:, :, per_device : 2 * per_device] + from_below + from_above
    for slot in range(rand_count):
        start = (3 + slot) * per_device
        own_grads = own_grads + return_far(
            kv_grads[:, :, start : start + per_device], offsets[slot]
        )
    global_part = jnp.stack([jnp.sum(results[3], axis=1), jnp.sum(results[4], axis=1)])
    global_part = global_part.transpose(0, 2, 3, 1, 4).reshape(2, 2, BLK, head_count * head_size)
    one_hot = (chosen[:, None] == jnp.arange(glob_keys.shape[0], dtype=jnp.int32)[None, :]).astype(
        jnp.float32
    )
    table_term = jnp.einsum("sg,ksbd->kgbd", one_hot, global_part, precision=lax.Precision.HIGHEST)
    table_grad = lax.psum(table_term, ("ctx", "dp"))
    d_query = from_heads(q_grad).astype(jnp.bfloat16)[None]
    d_key = from_heads(own_grads[0]).astype(jnp.bfloat16)[None]
    d_value = from_heads(own_grads[1]).astype(jnp.bfloat16)[None]
    return (d_query, d_key, d_value, table_grad)


VMEM_BYTES = 24 * 1024 * 1024
SMALL_VMEM_BYTES = 4 * 1024 * 1024
LARGE_VMEM_BYTES = 60 * 1024 * 1024
MASKED = -1e30
ORDER = (0, 2, 4, 5, 3, 6, 7, 1)
HEADS_ORDER = (0, 2, 4, 6, 1, 3, 5, 7)


def dot(left, right, left_dim, right_dim):
    dims = (((left_dim,), (right_dim,)), ((), ()))
    return lax.dot_general(left, right, dims, preferred_element_type=jnp.float32)


def in_vmem(count):
    return [pl.BlockSpec(memory_space=pltpu.VMEM)] * count


def pack_kernel(count, *refs):
    ins, outs = refs[:4], refs[4 : 4 + count]
    held, made, in_sems, out_sems = refs[4 + count :]
    head_size = made.shape[3]
    me = lax.axis_index("ctx")
    loads = [
        pltpu.make_async_copy(ref.at[0], held.at[place], in_sems.at[place])
        for place, ref in enumerate(ins)
    ]
    for load in loads:
        load.start()
    for load in loads:
        load.wait()
    stores = []
    for flip in ORDER:
        at = pl.multiple_of((me ^ flip) * head_size, head_size)
        made[flip] = held[:, :, pl.ds(at, head_size)]
        store = pltpu.make_async_copy(made.at[flip], outs[flip], out_sems.at[flip])
        store.start()
        stores.append(store)
    for store in stores:
        store.wait()


def pack(query, key, value, dout, head_count):
    _, rows, width = query.shape
    chunk = (4, rows, width // head_count)
    in_hbm = pl.BlockSpec(memory_space=pltpu.HBM)
    return pl.pallas_call(
        functools.partial(pack_kernel, head_count),
        in_specs=[in_hbm] * 4,
        out_specs=[in_hbm] * head_count,
        out_shape=[jax.ShapeDtypeStruct(chunk, query.dtype)] * head_count,
        scratch_shapes=[
            pltpu.VMEM((4, rows, width), query.dtype),
            pltpu.VMEM((head_count,) + chunk, query.dtype),
            pltpu.SemaphoreType.DMA((4,)),
            pltpu.SemaphoreType.DMA((head_count,)),
        ],
        compiler_params=pltpu.CompilerParams(vmem_limit_bytes=LARGE_VMEM_BYTES),
        cost_estimate=pl.CostEstimate(flops=0, bytes_accessed=16 * rows * width, transcendentals=0),
        name="pack_heads",
    )(query, key, value, dout)


def choose_kernel(place_ref, gk_ref, gv_ref, out_ref, sems):
    head_size = out_ref.shape[2]
    columns = pl.ds(pl.multiple_of(place_ref[0] * head_size, head_size), head_size)
    copies = [
        pltpu.make_async_copy(
            ref.at[place_ref[2 + slot], :, columns],
            out_ref.at[2 * kind + slot],
            sems.at[2 * kind + slot],
        )
        for kind, ref in enumerate((gk_ref, gv_ref))
        for slot in range(2)
    ]
    for copy in copies:
        copy.start()
    for copy in copies:
        copy.wait()


def choose(place, glob_keys, glob_values, head_size):
    return pl.pallas_call(
        choose_kernel,
        in_specs=[pl.BlockSpec(memory_space=pltpu.SMEM)]
        + [pl.BlockSpec(memory_space=pltpu.HBM)] * 2,
        out_specs=pl.BlockSpec(memory_space=pltpu.VMEM),
        out_shape=jax.ShapeDtypeStruct((4, BLK, head_size), glob_keys.dtype),
        scratch_shapes=[pltpu.SemaphoreType.DMA((4,))],
        compiler_params=pltpu.CompilerParams(vmem_limit_bytes=SMALL_VMEM_BYTES),
        cost_estimate=pl.CostEstimate(
            flops=0, bytes_accessed=16 * BLK * head_size, transcendentals=0
        ),
        name="choose_blocks",
    )(place, glob_keys, glob_values)


def head_kernel(spans, shares, place_ref, rand_ref, *refs):
    x_refs, g_ref, send_ref = refs[:spans], refs[spans], refs[spans + 1]
    share_refs = refs[spans + 2 : spans + 2 + shares]
    q_all, k_all, v_all, o_all, dk_all, dv_all, dgk, dgv, table = refs[
        spans + 2 + shares :
    ]
    _, rows, head_size = x_refs[0].shape
    rand_count = rand_ref.shape[0] // (2 * spans)
    scaling = 1.0 / math.sqrt(head_size)
    me = place_ref[0]
    top = BLK + spans * rows
    for pool in (k_all, v_all, dk_all, dv_all):
        pool[:BLK] = jnp.zeros((BLK, head_size), pool.dtype)
        pool[top:] = jnp.zeros((BLK, head_size), pool.dtype)
    for pool in (dk_all, dv_all):
        pool[BLK:top] = jnp.zeros((top - BLK, head_size), pool.dtype)
    starts = [pl.multiple_of((me ^ flip) * rows, rows) for flip in ORDER]
    for at, ref in zip(starts, x_refs):
        q_all[pl.ds(at, rows)] = ref[0]
        k_all[pl.ds(pl.multiple_of(at + BLK, BLK), rows)] = ref[1]
        v_all[pl.ds(pl.multiple_of(at + BLK, BLK), rows)] = ref[2]
        o_all[pl.ds(at, rows)] = ref[3]
    gk = [g_ref[0], g_ref[1]]
    gv = [g_ref[2], g_ref[3]]
    own = (1 + rand_count) * BLK
    first = lax.broadcasted_iota(jnp.int32, (1, rows), 1) < BLK
    empty = jnp.zeros((BLK, head_size), jnp.bfloat16)

    def split(block):
        return jnp.concatenate(
            [
                jnp.concatenate([block[:BLK], empty], axis=0),
                jnp.concatenate([empty, block[BLK:]], axis=0),
            ],
            axis=1,
        )

    for span in range(spans):
        at = span * rows
        q = q_all[at : at + rows]
        o = o_all[at : at + rows]
        q_split = split(q)
        o_split = split(o)
        places = [
            [
                pl.multiple_of((rand_ref[(2 * span + half) * rand_count + slot] + 1) * BLK, BLK)
                for slot in range(rand_count)
            ]
            for half in range(2)
        ]

        def gathered(pool, table_blocks):
            window = pool[at : at + 4 * BLK]
            lists = [
                jnp.concatenate([edge] + [pool[pl.ds(p, BLK)] for p in places[half]], axis=0)
                for half, edge in enumerate((window[:BLK], window[3 * BLK :]))
            ]
            both = jnp.concatenate([window[BLK : 3 * BLK]] + table_blocks, axis=0)
            return jnp.concatenate(lists, axis=1), both

        k_own, k_both = gathered(k_all, gk)
        v_own, v_both = gathered(v_all, gv)
        s_own = dot(k_own, q_split, 1, 1) * scaling
        s_both = dot(k_both, q, 1, 1) * scaling
        if span == 0 or span == spans - 1:
            row = lax.broadcasted_iota(jnp.int32, (own, 1), 0) < BLK
            outside = row & (first if span == 0 else jnp.logical_not(first))
            s_own = jnp.where(outside, MASKED, s_own)
        top_score = jnp.maximum(
            jnp.max(s_own, axis=0, keepdims=True), jnp.max(s_both, axis=0, keepdims=True)
        )
        e_own = jnp.exp(s_own - top_score)
        e_both = jnp.exp(s_both - top_score)
        total = jnp.sum(e_own, axis=0, keepdims=True) + jnp.sum(e_both, axis=0, keepdims=True)
        inverse = 1.0 / total
        p_own = e_own * inverse
        p_both = e_both * inverse
        pb_own = p_own.astype(jnp.bfloat16)
        pb_both = p_both.astype(jnp.bfloat16)
        g_own = dot(v_own, o_split, 1, 1)
        g_both = dot(v_both, o, 1, 1)
        row_dot = jnp.sum(pb_own.astype(jnp.float32) * g_own, axis=0, keepdims=True) + jnp.sum(
            pb_both.astype(jnp.float32) * g_both, axis=0, keepdims=True
        )
        ds_own = (p_own * (g_own - row_dot) * scaling).astype(jnp.bfloat16)
        ds_both = (p_both * (g_both - row_dot) * scaling).astype(jnp.bfloat16)
        wide = dot(ds_own, k_own, 0, 0)
        dq = jnp.concatenate([wide[:BLK, :head_size], wide[BLK:, head_size:]], axis=0)
        send_ref[span, 0] = (dq + dot(ds_both, k_both, 0, 0)).astype(jnp.bfloat16)
        for weights_own, weights_both, x_split, x, pool, shared in (
            (ds_own, ds_both, q_split, q, dk_all, dgk),
            (pb_own, pb_both, o_split, o, dv_all, dgv),
        ):
            d_own = dot(weights_own, x_split, 1, 0)
            d_both = dot(weights_both, x, 1, 0)
            pool[at + BLK : at + 3 * BLK] += d_both[: 2 * BLK]
            if span == 0:
                shared[...] = d_both[2 * BLK :]
            else:
                shared[...] += d_both[2 * BLK :]
            pool[at : at + BLK] += d_own[:BLK, :head_size]
            pool[at + 3 * BLK : at + 4 * BLK] += d_own[:BLK, head_size:]
            for half in range(2):
                columns = slice(half * head_size, (half + 1) * head_size)
                for slot, p in enumerate(places[half]):
                    pool[pl.ds(p, BLK)] += d_own[(1 + slot) * BLK : (2 + slot) * BLK, columns]
    for span in range(spans):
        at = BLK + span * rows
        send_ref[span, 1] = dk_all[at : at + rows].astype(jnp.bfloat16)
        send_ref[span, 2] = dv_all[at : at + rows].astype(jnp.bfloat16)
    table[...] = jnp.zeros(table.shape, table.dtype)
    kinds = table.shape[0] // 2
    for slot in range(2):
        for kind, shared in enumerate((dgk, dgv)):
            block = shared[slot * BLK : (slot + 1) * BLK]
            table[kind * kinds + place_ref[2 + slot]] = block
    for flip, ref in enumerate(share_refs):
        count = table.shape[0] // shares
        start = (place_ref[1] ^ flip) * count
        ref[...] = table[pl.ds(start, count)].astype(ref.dtype)


def attend_head(chunks, chosen, place, rand_head, table_size, shares):
    spans = len(chunks)
    _, rows, head_size = chunks[0].shape
    padded_rows = spans * rows + 2 * BLK
    keys_each = spans * rows * 8 * BLK
    share = jax.ShapeDtypeStruct((2 * table_size // shares, BLK, head_size), jnp.bfloat16)
    outs = [jax.ShapeDtypeStruct((spans, 3, rows, head_size), jnp.bfloat16)] + [share] * shares
    results = pl.pallas_call(
        functools.partial(head_kernel, spans, shares),
        in_specs=[pl.BlockSpec(memory_space=pltpu.SMEM)] * 2 + in_vmem(spans + 1),
        out_specs=in_vmem(len(outs)),
        out_shape=outs,
        scratch_shapes=[
            pltpu.VMEM((spans * rows, head_size), jnp.bfloat16),
            pltpu.VMEM((padded_rows, head_size), jnp.bfloat16),
            pltpu.VMEM((padded_rows, head_size), jnp.bfloat16),
            pltpu.VMEM((spans * rows, head_size), jnp.bfloat16),
            pltpu.VMEM((padded_rows, head_size), jnp.float32),
            pltpu.VMEM((padded_rows, head_size), jnp.float32),
            pltpu.VMEM((2 * BLK, head_size), jnp.float32),
            pltpu.VMEM((2 * BLK, head_size), jnp.float32),
            pltpu.VMEM((2 * table_size, BLK, head_size), jnp.float32),
        ],
        compiler_params=pltpu.CompilerParams(vmem_limit_bytes=VMEM_BYTES),
        cost_estimate=pl.CostEstimate(
            flops=10 * keys_each * head_size,
            bytes_accessed=16 * spans * rows * head_size,
            transcendentals=keys_each,
        ),
        name="attend_head",
    )(place, rand_head, *chunks, chosen)
    return results[0], results[1:]


def unpack_kernel(x_ref, dq_ref, dk_ref, dv_ref):
    head_size = x_ref.shape[3]
    for head in range(x_ref.shape[0]):
        columns = slice(head * head_size, (head + 1) * head_size)
        for place, ref in enumerate((dq_ref, dk_ref, dv_ref)):
            ref[0, :, columns] = x_ref[head, place]


def unpack(x):
    heads, _, rows, head_size = x.shape
    shape = jax.ShapeDtypeStruct((1, rows, heads * head_size), x.dtype)
    return pl.pallas_call(
        unpack_kernel,
        grid=(1,),
        in_specs=[pl.BlockSpec((heads, 3, rows, head_size), lambda i: (0, 0, 0, 0))],
        out_specs=[pl.BlockSpec(shape.shape, lambda i: (0, 0, 0))] * 3,
        out_shape=[shape] * 3,
        compiler_params=pltpu.CompilerParams(vmem_limit_bytes=VMEM_BYTES),
        cost_estimate=pl.CostEstimate(
            flops=0, bytes_accessed=12 * rows * heads * head_size, transcendentals=0
        ),
        name="unpack_heads",
    )(x)


def table_kernel(*refs):
    parts, out_ref = refs[:-1], refs[-1]
    _, count, _, head_size = parts[0].shape
    head = lax.axis_index("ctx")
    share = lax.axis_index("dp")
    for bits, ref in enumerate(parts):
        for place, flip in enumerate(HEADS_ORDER):
            columns = pl.ds(pl.multiple_of((head ^ flip) * head_size, head_size), head_size)
            for block in range(count):
                out_ref[(share ^ bits) * count + block, :, columns] = ref[place, block].astype(
                    out_ref.dtype
                )


def whole_table(parts):
    heads, blocks, rows, head_size = parts[0].shape
    shape = (len(parts) * blocks, rows, heads * head_size)
    return pl.pallas_call(
        table_kernel,
        grid=(1,),
        in_specs=[pl.BlockSpec(parts[0].shape, lambda i: (0, 0, 0, 0))] * len(parts),
        out_specs=pl.BlockSpec(shape, lambda i: (0, 0, 0)),
        out_shape=jax.ShapeDtypeStruct(shape, jnp.float32),
        compiler_params=pltpu.CompilerParams(vmem_limit_bytes=VMEM_BYTES),
        name="whole_table",
    )(*parts)


def flipped(array, axis, bits):
    if bits == 0:
        return array
    return lax.ppermute(array, axis, [(i, i ^ bits) for i in range(lax.axis_size(axis))])


def on_heads(query, key, value, dout, glob_keys, glob_values, glob_ids, rand_blocks):
    head_count, block_count, _ = rand_blocks.shape
    head_size = query.shape[2] // head_count
    table_size = glob_keys.shape[0]
    shares = lax.axis_size("dp")
    head = lax.axis_index("ctx").astype(jnp.int32)
    sequence = lax.axis_index("dp").astype(jnp.int32)
    packed = pack(query, key, value, dout, head_count)
    chunks = [flipped(packed[flip], "ctx", flip) for flip in ORDER]
    place = jnp.concatenate([head[None], sequence[None], glob_ids[0]])
    rand_head = lax.dynamic_index_in_dim(rand_blocks, head, 0, keepdims=False).reshape(-1)
    rand_head = jnp.clip(rand_head, 0, block_count - 1)
    chosen = choose(place, glob_keys, glob_values, head_size)
    grads, terms = attend_head(chunks, chosen, place, rand_head, table_size, shares)
    terms = [flipped(terms[bits], "dp", bits) for bits in range(shares)]
    share = sum(term.astype(jnp.float32) for term in terms).astype(jnp.bfloat16)
    column = jnp.stack([flipped(share, "ctx", flip) for flip in HEADS_ORDER[:4]])
    quarter = jnp.concatenate([column, flipped(column, "ctx", 1)])
    across = flipped(quarter, "dp", 2)
    beside = flipped(quarter, "dp", 1)
    corner = flipped(across, "dp", 1)
    d_table = whole_table([quarter, beside, across, corner])
    back = lax.all_to_all(grads, "ctx", 0, 0)
    d_query, d_key, d_value = unpack(back)
    return (d_query, d_key, d_value, d_table.reshape((2,) + glob_keys.shape))


def on_device(query, key, value, dout, glob_keys, glob_values, glob_ids, rand_blocks):
    head_count = rand_blocks.shape[0]
    one_head_each = lax.axis_size("ctx") == head_count == 8 and query.shape[1] == 2 * BLK
    if one_head_each and lax.axis_size("dp") == 4 and glob_keys.shape[0] % 2 == 0:
        plan = on_heads
    else:
        plan = on_ring
    return plan(query, key, value, dout, glob_keys, glob_values, glob_ids, rand_blocks)


def solution(mesh):
    placed = (
        P("dp", "ctx", None),
        P("dp", "ctx", None),
        P("dp", "ctx", None),
        P("dp", "ctx", None),
        P(),
        P(),
        P("dp", None),
        P(),
    )
    return jax.shard_map(
        on_device,
        mesh=mesh,
        in_specs=placed,
        out_specs=(P("dp", "ctx", None), P("dp", "ctx", None), P("dp", "ctx", None), P()),
        check_vma=False,
    )
```

```python
import functools
import math

import jax
import jax.numpy as jnp
from jax import lax
from jax.experimental import pallas as pl
from jax.experimental.pallas import tpu as pltpu
from jax.sharding import PartitionSpec as P

BLK = 64


def passed_along(shard, axis, by):
    length = lax.axis_size(axis)
    return lax.ppermute(shard, axis, [(i, (i + by) % length) for i in range(length)])


def padded(cells, sides, width):
    for axis, dim in sides:
        count = lax.axis_size(axis)
        ends = count - 1
        head = lax.slice_in_dim(cells, 0, width, axis=dim)
        tail = lax.slice_in_dim(cells, cells.shape[dim] - width, cells.shape[dim], axis=dim)
        cells = jnp.concatenate(
            [
                lax.ppermute(tail, axis, [(i, (i + 1) % count) for i in range(ends)]),
                cells,
                lax.ppermute(head, axis, [((i + 1) % count, i) for i in range(ends)]),
            ],
            axis=dim,
        )
    return cells


def passed_along_2(value, axis, steps):
    count = lax.axis_size(axis)
    leading, last = (max(0, -steps), min(count, count - steps))
    return lax.ppermute(value, axis, [(source, source + steps) for source in range(leading, last)])


def attend(
    q_head,
    o_grad,
    k_head,
    v_head,
    gk_head,
    gv_head,
    key_index,
    key_valid,
    scatter_count,
    rand_count,
):
    q_blocks = q_head.shape[0]
    head_size = q_head.shape[2]
    scaling = 1.0 / math.sqrt(head_size)
    local_lists = key_index.shape[1]
    keys_all = jnp.concatenate(
        [
            jnp.take(k_head, key_index, axis=0),
            jnp.broadcast_to(gk_head[None], (q_blocks,) + gk_head.shape),
        ],
        axis=1,
    ).reshape(q_blocks, -1, head_size)
    values_all = jnp.concatenate(
        [
            jnp.take(v_head, key_index, axis=0),
            jnp.broadcast_to(gv_head[None], (q_blocks,) + gv_head.shape),
        ],
        axis=1,
    ).reshape(q_blocks, -1, head_size)
    keep_mask = jnp.repeat(
        jnp.concatenate([key_valid, jnp.ones((q_blocks, 2), dtype=bool)], axis=1), BLK, axis=1
    )
    scores = (
        jnp.einsum("nqd,nkd->nqk", q_head, keys_all, preferred_element_type=jnp.float32) * scaling
    )
    scores = jnp.where(keep_mask[:, None, :], scores, -1e30)
    row_max = jnp.max(scores, axis=-1, keepdims=True)
    exp_scores = jnp.exp(scores - row_max)
    weights = exp_scores / jnp.sum(exp_scores, axis=-1, keepdims=True)
    weights_b = weights.astype(jnp.bfloat16)
    attn_out = jnp.einsum("nqk,nkd->nqd", weights_b, values_all, preferred_element_type=jnp.float32)
    row_dot = jnp.sum(o_grad.astype(jnp.float32) * attn_out, axis=-1, keepdims=True)
    prob_grad = jnp.einsum("nqd,nkd->nqk", o_grad, values_all, preferred_element_type=jnp.float32)
    score_grad = (weights * (prob_grad - row_dot) * scaling).astype(jnp.bfloat16)
    q_grad = jnp.einsum("nqk,nkd->nqd", score_grad, keys_all, preferred_element_type=jnp.float32)
    k_grad = jnp.einsum(
        "nqk,nqd->nkd", score_grad, q_head, preferred_element_type=jnp.float32
    ).reshape(q_blocks, local_lists + 2, BLK, head_size)
    v_grad = jnp.einsum(
        "nqk,nqd->nkd", weights_b, o_grad, preferred_element_type=jnp.float32
    ).reshape(q_blocks, local_lists + 2, BLK, head_size)
    flat_index = key_index.reshape(-1)
    k_local = (
        jnp.zeros(k_head.shape, jnp.float32)
        .at[flat_index]
        .add(k_grad[:, :scatter_count].reshape(-1, BLK, head_size))
    )
    v_local = (
        jnp.zeros(v_head.shape, jnp.float32)
        .at[flat_index]
        .add(v_grad[:, :scatter_count].reshape(-1, BLK, head_size))
    )
    grad_tiles = score_grad.reshape(q_blocks, BLK, local_lists + 2, BLK)[
        :, :, 3 : 3 + rand_count
    ].transpose(0, 2, 1, 3)
    prob_tiles = weights_b.reshape(q_blocks, BLK, local_lists + 2, BLK)[
        :, :, 3 : 3 + rand_count
    ].transpose(0, 2, 1, 3)
    return (
        q_grad,
        k_local,
        v_local,
        k_grad[:, local_lists:],
        v_grad[:, local_lists:],
        grad_tiles,
        prob_tiles,
    )


def by_heads(row_array, head_count):
    block_total = row_array.shape[0] // BLK
    return row_array.reshape(block_total, BLK, head_count, -1).transpose(2, 0, 1, 3)


def from_heads(head_array):
    head_count = head_array.shape[0]
    head_size = head_array.shape[3]
    return head_array.transpose(1, 2, 0, 3).reshape(-1, head_count * head_size)


def fetch_far(key_value, offset):
    return passed_along(key_value, "ctx", -offset)


def return_far(partials, offset):
    return passed_along(partials, "ctx", offset)


def on_ring(query, key, value, dout, glob_keys, glob_values, glob_ids, rand_blocks):
    row_count = query.shape[1]
    head_count = rand_blocks.shape[0]
    rand_count = rand_blocks.shape[2]
    head_size = query.shape[2] // head_count
    per_device = row_count // BLK
    span_count = lax.axis_size("ctx")
    device_pos = lax.axis_index("ctx")
    block_count = per_device * span_count
    offsets = [(slot + 1) * span_count // (rand_count + 1) for slot in range(rand_count)]
    key_value = jnp.stack([key[0], value[0]])
    extended = padded(key_value, (("ctx", 1),), row_count)
    far_spans = [fetch_far(key_value, offset) for offset in offsets]
    k_rows = jnp.concatenate([extended[0]] + [span[0] for span in far_spans], axis=0)
    v_rows = jnp.concatenate([extended[1]] + [span[1] for span in far_spans], axis=0)
    first_block = device_pos * per_device
    key_base = first_block - per_device
    query_ids = first_block + jnp.arange(per_device, dtype=jnp.int32)
    window = query_ids[:, None] + jnp.arange(-1, 2, dtype=jnp.int32)[None, :]
    key_valid = jnp.concatenate(
        [(window >= 0) & (window < block_count), jnp.ones((per_device, rand_count), dtype=bool)],
        axis=1,
    )
    window_local = jnp.clip(window - key_base, 0, 3 * per_device - 1)
    rand_rows = lax.dynamic_slice_in_dim(rand_blocks, first_block, per_device, 1)
    offset_table = jnp.array(offsets, dtype=jnp.int32)
    far_starts = (device_pos + offset_table) % span_count * per_device
    slot_base = (3 + jnp.arange(rand_count, dtype=jnp.int32)) * per_device
    rand_local = rand_rows - far_starts[None, None, :] + slot_base[None, None, :]
    all_lists = jnp.concatenate(
        [jnp.broadcast_to(window_local[None], (head_count,) + window_local.shape), rand_local],
        axis=2,
    )
    key_index = jnp.clip(all_lists, 0, (3 + rand_count) * per_device - 1)
    chosen = glob_ids[0]
    gk_heads = by_heads(jnp.take(glob_keys, chosen, axis=0).reshape(2 * BLK, -1), head_count)
    gv_heads = by_heads(jnp.take(glob_values, chosen, axis=0).reshape(2 * BLK, -1), head_count)
    scatter_count = 3 + rand_count

    def per_head(pieces):
        q_head, o_grad, k_head, v_head, gk_head, gv_head, index_head = pieces
        return attend(
            q_head,
            o_grad,
            k_head,
            v_head,
            gk_head,
            gv_head,
            index_head,
            key_valid,
            scatter_count,
            rand_count,
        )

    results = lax.map(
        per_head,
        (
            by_heads(query[0], head_count),
            by_heads(dout[0], head_count),
            by_heads(k_rows, head_count),
            by_heads(v_rows, head_count),
            gk_heads,
            gv_heads,
            key_index,
        ),
    )
    q_grad = results[0]
    kv_grads = jnp.stack([results[1], results[2]])
    lower_part = kv_grads[:, :, :per_device]
    upper_part = kv_grads[:, :, 2 * per_device : 3 * per_device]
    from_below = passed_along_2(upper_part.astype(jnp.bfloat16), "ctx", 1).astype(upper_part.dtype)
    from_above = passed_along_2(lower_part.astype(jnp.bfloat16), "ctx", -1).astype(lower_part.dtype)
    own_grads = kv_grads[:, :, per_device : 2 * per_device] + from_below + from_above
    for slot in range(rand_count):
        start = (3 + slot) * per_device
        own_grads = own_grads + return_far(
            kv_grads[:, :, start : start + per_device], offsets[slot]
        )
    global_part = jnp.stack([jnp.sum(results[3], axis=1), jnp.sum(results[4], axis=1)])
    global_part = global_part.transpose(0, 2, 3, 1, 4).reshape(2, 2, BLK, head_count * head_size)
    one_hot = (chosen[:, None] == jnp.arange(glob_keys.shape[0], dtype=jnp.int32)[None, :]).astype(
        jnp.float32
    )
    table_term = jnp.einsum("sg,ksbd->kgbd", one_hot, global_part, precision=lax.Precision.HIGHEST)
    table_grad = lax.psum(table_term, ("ctx", "dp"))
    d_query = from_heads(q_grad).astype(jnp.bfloat16)[None]
    d_key = from_heads(own_grads[0]).astype(jnp.bfloat16)[None]
    d_value = from_heads(own_grads[1]).astype(jnp.bfloat16)[None]
    return (d_query, d_key, d_value, table_grad)


VMEM_BYTES = 24 * 1024 * 1024
SMALL_VMEM_BYTES = 4 * 1024 * 1024
LARGE_VMEM_BYTES = 60 * 1024 * 1024
MASKED = -1e30
ORDER = (0, 4, 2, 5, 3, 6, 7, 1)
HEADS_ORDER = (0, 2, 4, 6, 1, 3, 5, 7)


def dot(left, right, left_dim, right_dim):
    dims = (((left_dim,), (right_dim,)), ((), ()))
    return lax.dot_general(left, right, dims, preferred_element_type=jnp.float32)


def in_vmem(count):
    return [pl.BlockSpec(memory_space=pltpu.VMEM)] * count


def pack_kernel(count, *refs):
    ins, outs = refs[:4], refs[4 : 4 + count]
    held, made, in_sems, out_sems = refs[4 + count :]
    head_size = made.shape[3]
    me = lax.axis_index("ctx")
    loads = [
        pltpu.make_async_copy(ref.at[0], held.at[place], in_sems.at[place])
        for place, ref in enumerate(ins)
    ]
    for load in loads:
        load.start()
    for load in loads:
        load.wait()
    stores = []
    for flip in ORDER:
        at = pl.multiple_of((me ^ flip) * head_size, head_size)
        made[flip] = held[:, :, pl.ds(at, head_size)]
        store = pltpu.make_async_copy(made.at[flip], outs[flip], out_sems.at[flip])
        store.start()
        stores.append(store)
    for store in stores:
        store.wait()


def pack(query, key, value, dout, head_count):
    _, rows, width = query.shape
    chunk = (4, rows, width // head_count)
    in_hbm = pl.BlockSpec(memory_space=pltpu.HBM)
    return pl.pallas_call(
        functools.partial(pack_kernel, head_count),
        in_specs=[in_hbm] * 4,
        out_specs=[in_hbm] * head_count,
        out_shape=[jax.ShapeDtypeStruct(chunk, query.dtype)] * head_count,
        scratch_shapes=[
            pltpu.VMEM((4, rows, width), query.dtype),
            pltpu.VMEM((head_count,) + chunk, query.dtype),
            pltpu.SemaphoreType.DMA((4,)),
            pltpu.SemaphoreType.DMA((head_count,)),
        ],
        compiler_params=pltpu.CompilerParams(vmem_limit_bytes=LARGE_VMEM_BYTES),
        cost_estimate=pl.CostEstimate(flops=0, bytes_accessed=16 * rows * width, transcendentals=0),
        name="pack_heads",
    )(query, key, value, dout)


def choose_kernel(place_ref, gk_ref, gv_ref, own_ref, out_ref, held_ref, sems):
    head_size = out_ref.shape[2]
    columns = pl.ds(pl.multiple_of(place_ref[0] * head_size, head_size), head_size)
    copies = [
        pltpu.make_async_copy(
            ref.at[place_ref[2 + slot], :, columns],
            out_ref.at[2 * kind + slot],
            sems.at[2 * kind + slot],
        )
        for kind, ref in enumerate((gk_ref, gv_ref))
        for slot in range(2)
    ]
    copies.append(pltpu.make_async_copy(own_ref, held_ref, sems.at[4]))
    for copy in copies:
        copy.start()
    for copy in copies:
        copy.wait()


def choose(place, glob_keys, glob_values, own):
    head_size = own.shape[2]
    return pl.pallas_call(
        choose_kernel,
        in_specs=[pl.BlockSpec(memory_space=pltpu.SMEM)]
        + [pl.BlockSpec(memory_space=pltpu.HBM)] * 3,
        out_specs=in_vmem(2),
        out_shape=[
            jax.ShapeDtypeStruct((4, BLK, head_size), glob_keys.dtype),
            jax.ShapeDtypeStruct(own.shape, own.dtype),
        ],
        scratch_shapes=[pltpu.SemaphoreType.DMA((5,))],
        compiler_params=pltpu.CompilerParams(vmem_limit_bytes=SMALL_VMEM_BYTES),
        cost_estimate=pl.CostEstimate(
            flops=0, bytes_accessed=16 * BLK * head_size, transcendentals=0
        ),
        name="choose_blocks",
    )(place, glob_keys, glob_values, own)


def split_rows(block):
    empty = jnp.zeros((BLK, block.shape[1]), block.dtype)
    return jnp.concatenate(
        [
            jnp.concatenate([block[:BLK], empty], axis=0),
            jnp.concatenate([empty, block[BLK:]], axis=0),
        ],
        axis=1,
    )


def list_places(rand_ref, span, rand_count):
    return [
        [
            pl.multiple_of((rand_ref[(2 * span + half) * rand_count + slot] + 1) * BLK, BLK)
            for slot in range(rand_count)
        ]
        for half in range(2)
    ]


def gathered(pool, at, places, table_blocks):
    window = pool[at : at + 4 * BLK]
    lists = [
        jnp.concatenate([edge] + [pool[pl.ds(p, BLK)] for p in places[half]], axis=0)
        for half, edge in enumerate((window[:BLK], window[3 * BLK :]))
    ]
    both = jnp.concatenate([window[BLK : 3 * BLK]] + table_blocks, axis=0)
    return jnp.concatenate(lists, axis=1), both


def score_kernel(spans, shares, place_ref, rand_ref, *refs):
    x_refs, g_ref = refs[:spans], refs[spans]
    q_all, k_all, o_all, p_all, ds_all = refs[spans + 1 : spans + 6]
    share_refs = refs[spans + 6 : spans + 6 + shares]
    v_all, dgk, dgv, table = refs[spans + 6 + shares :]
    _, rows, head_size = x_refs[0].shape
    rand_count = rand_ref.shape[0] // (2 * spans)
    scaling = 1.0 / math.sqrt(head_size)
    me = place_ref[0]
    top = BLK + spans * rows
    for pool in (k_all, v_all):
        pool[:BLK] = jnp.zeros((BLK, head_size), pool.dtype)
        pool[top:] = jnp.zeros((BLK, head_size), pool.dtype)
    starts = [pl.multiple_of((me ^ flip) * rows, rows) for flip in ORDER]
    for at, ref in zip(starts, x_refs):
        q_all[pl.ds(at, rows)] = ref[0]
        k_all[pl.ds(pl.multiple_of(at + BLK, BLK), rows)] = ref[1]
        v_all[pl.ds(pl.multiple_of(at + BLK, BLK), rows)] = ref[2]
        o_all[pl.ds(at, rows)] = ref[3]
    gk = [g_ref[0], g_ref[1]]
    gv = [g_ref[2], g_ref[3]]
    own = (1 + rand_count) * BLK
    first = lax.broadcasted_iota(jnp.int32, (1, rows), 1) < BLK
    for span in range(spans):
        at = span * rows
        q = q_all[at : at + rows]
        o = o_all[at : at + rows]
        places = list_places(rand_ref, span, rand_count)
        k_own, k_both = gathered(k_all, at, places, gk)
        v_own, v_both = gathered(v_all, at, places, gv)
        s_own = dot(k_own, split_rows(q), 1, 1) * scaling
        s_both = dot(k_both, q, 1, 1) * scaling
        if span == 0 or span == spans - 1:
            row = lax.broadcasted_iota(jnp.int32, (own, 1), 0) < BLK
            outside = row & (first if span == 0 else jnp.logical_not(first))
            s_own = jnp.where(outside, MASKED, s_own)
        top_score = jnp.maximum(
            jnp.max(s_own, axis=0, keepdims=True), jnp.max(s_both, axis=0, keepdims=True)
        )
        e_own = jnp.exp(s_own - top_score)
        e_both = jnp.exp(s_both - top_score)
        total = jnp.sum(e_own, axis=0, keepdims=True) + jnp.sum(e_both, axis=0, keepdims=True)
        inverse = 1.0 / total
        p_own = e_own * inverse
        p_both = e_both * inverse
        pb_own = p_own.astype(jnp.bfloat16)
        pb_both = p_both.astype(jnp.bfloat16)
        g_own = dot(v_own, split_rows(o), 1, 1)
        g_both = dot(v_both, o, 1, 1)
        row_dot = jnp.sum(pb_own.astype(jnp.float32) * g_own, axis=0, keepdims=True) + jnp.sum(
            pb_both.astype(jnp.float32) * g_both, axis=0, keepdims=True
        )
        ds_own = (p_own * (g_own - row_dot) * scaling).astype(jnp.bfloat16)
        ds_both = (p_both * (g_both - row_dot) * scaling).astype(jnp.bfloat16)
        p_all[span, :own] = pb_own
        p_all[span, own:] = pb_both
        ds_all[span, :own] = ds_own
        ds_all[span, own:] = ds_both
        for weights, x, shared in ((ds_both, q, dgk), (pb_both, o, dgv)):
            term = dot(weights[2 * BLK :], x, 1, 0)
            if span == 0:
                shared[...] = term
            else:
                shared[...] += term
    table[...] = jnp.zeros(table.shape, table.dtype)
    kinds = table.shape[0] // 2
    for slot in range(2):
        for kind, shared in enumerate((dgk, dgv)):
            block = shared[slot * BLK : (slot + 1) * BLK]
            table[kind * kinds + place_ref[2 + slot]] = block
    for flip, ref in enumerate(share_refs):
        count = table.shape[0] // shares
        start = (place_ref[1] ^ flip) * count
        ref[...] = table[pl.ds(start, count)].astype(ref.dtype)


def scores(chunks, chosen, place, rand_head, table_size, shares):
    spans = len(chunks)
    _, rows, head_size = chunks[0].shape
    keys = 8 * BLK
    padded_rows = spans * rows + 2 * BLK
    keys_each = spans * rows * keys
    half = lambda *shape: jax.ShapeDtypeStruct(shape, jnp.bfloat16)
    outs = [
        half(spans * rows, head_size),
        half(padded_rows, head_size),
        half(spans * rows, head_size),
        half(spans, keys, rows),
        half(spans, keys, rows),
    ] + [half(2 * table_size // shares, BLK, head_size)] * shares
    results = pl.pallas_call(
        functools.partial(score_kernel, spans, shares),
        in_specs=[pl.BlockSpec(memory_space=pltpu.SMEM)] * 2 + in_vmem(spans + 1),
        out_specs=in_vmem(len(outs)),
        out_shape=outs,
        scratch_shapes=[
            pltpu.VMEM((padded_rows, head_size), jnp.bfloat16),
            pltpu.VMEM((2 * BLK, head_size), jnp.float32),
            pltpu.VMEM((2 * BLK, head_size), jnp.float32),
            pltpu.VMEM((2 * table_size, BLK, head_size), jnp.float32),
        ],
        compiler_params=pltpu.CompilerParams(vmem_limit_bytes=VMEM_BYTES),
        cost_estimate=pl.CostEstimate(
            flops=4 * keys_each * head_size,
            bytes_accessed=8 * spans * rows * head_size,
            transcendentals=keys_each,
        ),
        name="scores",
    )(place, rand_head, *chunks, chosen)
    return results[:5], results[5:]


def grad_kernel(rand_ref, g_ref, q_all, k_all, o_all, p_all, ds_all, send_ref, dk_all, dv_all):
    spans, _, rows, head_size = send_ref.shape
    rand_count = rand_ref.shape[0] // (2 * spans)
    own = (1 + rand_count) * BLK
    for pool in (dk_all, dv_all):
        pool[...] = jnp.zeros(pool.shape, pool.dtype)
    gk = [g_ref[0], g_ref[1]]
    for span in range(spans):
        at = span * rows
        q = q_all[at : at + rows]
        o = o_all[at : at + rows]
        places = list_places(rand_ref, span, rand_count)
        k_own, k_both = gathered(k_all, at, places, gk)
        wide = dot(ds_all[span, :own], k_own, 0, 0)
        dq = jnp.concatenate([wide[:BLK, :head_size], wide[BLK:, head_size:]], axis=0)
        dq = dq + dot(ds_all[span, own:], k_both, 0, 0)
        send_ref[span, 0] = dq.astype(send_ref.dtype)
        for weights, x, pool in ((ds_all, q, dk_all), (p_all, o, dv_all)):
            d_own = dot(weights[span, :own], split_rows(x), 1, 0)
            d_both = dot(weights[span, own : own + 2 * BLK], x, 1, 0)
            pool[at + BLK : at + 3 * BLK] += d_both
            pool[at : at + BLK] += d_own[:BLK, :head_size]
            pool[at + 3 * BLK : at + 4 * BLK] += d_own[:BLK, head_size:]
            for half in range(2):
                columns = slice(half * head_size, (half + 1) * head_size)
                for slot, p in enumerate(places[half]):
                    pool[pl.ds(p, BLK)] += d_own[(1 + slot) * BLK : (2 + slot) * BLK, columns]
    for span in range(spans):
        at = BLK + span * rows
        send_ref[span, 1] = dk_all[at : at + rows].astype(send_ref.dtype)
        send_ref[span, 2] = dv_all[at : at + rows].astype(send_ref.dtype)


def grads(rand_head, chosen, held):
    spans, keys, rows = held[3].shape
    padded_rows, head_size = held[1].shape
    keys_each = spans * keys * rows
    return pl.pallas_call(
        grad_kernel,
        in_specs=[pl.BlockSpec(memory_space=pltpu.SMEM)] + in_vmem(1 + len(held)),
        out_specs=pl.BlockSpec(memory_space=pltpu.VMEM),
        out_shape=jax.ShapeDtypeStruct((spans, 3, rows, head_size), jnp.bfloat16),
        scratch_shapes=[pltpu.VMEM((padded_rows, head_size), jnp.float32)] * 2,
        compiler_params=pltpu.CompilerParams(vmem_limit_bytes=VMEM_BYTES),
        cost_estimate=pl.CostEstimate(
            flops=6 * keys_each * head_size,
            bytes_accessed=8 * spans * rows * head_size,
            transcendentals=0,
        ),
        name="grads",
    )(rand_head, chosen, *held)


def unpack_kernel(x_ref, *out_refs):
    heads, _, _, head_size = x_ref.shape
    for head in range(heads):
        columns = slice(head * head_size, (head + 1) * head_size)
        for place, ref in enumerate(out_refs):
            ref[0, :, columns] = x_ref[head, place]


def unpack(x):
    heads, count, rows, head_size = x.shape
    shape = jax.ShapeDtypeStruct((1, rows, heads * head_size), x.dtype)
    return pl.pallas_call(
        unpack_kernel,
        grid=(1,),
        in_specs=[pl.BlockSpec(x.shape, lambda i: (0, 0, 0, 0))],
        out_specs=[pl.BlockSpec(shape.shape, lambda i: (0, 0, 0))] * count,
        out_shape=[shape] * count,
        compiler_params=pltpu.CompilerParams(vmem_limit_bytes=VMEM_BYTES),
        cost_estimate=pl.CostEstimate(
            flops=0, bytes_accessed=4 * count * rows * heads * head_size, transcendentals=0
        ),
        name="unpack_heads",
    )(x)


def table_kernel(*refs):
    parts, out_ref = refs[:-1], refs[-1]
    _, count, _, head_size = parts[0].shape
    head = lax.axis_index("ctx")
    share = lax.axis_index("dp")
    for bits, ref in enumerate(parts):
        for place, flip in enumerate(HEADS_ORDER):
            columns = pl.ds(pl.multiple_of((head ^ flip) * head_size, head_size), head_size)
            for block in range(count):
                out_ref[(share ^ bits) * count + block, :, columns] = ref[place, block].astype(
                    out_ref.dtype
                )


def whole_table(parts):
    heads, blocks, rows, head_size = parts[0].shape
    shape = (len(parts) * blocks, rows, heads * head_size)
    return pl.pallas_call(
        table_kernel,
        grid=(1,),
        in_specs=[pl.BlockSpec(parts[0].shape, lambda i: (0, 0, 0, 0))] * len(parts),
        out_specs=pl.BlockSpec(shape, lambda i: (0, 0, 0)),
        out_shape=jax.ShapeDtypeStruct(shape, jnp.float32),
        compiler_params=pltpu.CompilerParams(vmem_limit_bytes=VMEM_BYTES),
        name="whole_table",
    )(*parts)


def flipped(array, axis, bits):
    if bits == 0:
        return array
    return lax.ppermute(array, axis, [(i, i ^ bits) for i in range(lax.axis_size(axis))])


def on_heads(query, key, value, dout, glob_keys, glob_values, glob_ids, rand_blocks):
    head_count, block_count, _ = rand_blocks.shape
    head_size = query.shape[2] // head_count
    table_size = glob_keys.shape[0]
    shares = lax.axis_size("dp")
    head = lax.axis_index("ctx").astype(jnp.int32)
    sequence = lax.axis_index("dp").astype(jnp.int32)
    packed = pack(query, key, value, dout, head_count)
    chunks = [flipped(packed[flip], "ctx", flip) for flip in ORDER]
    place = jnp.concatenate([head[None], sequence[None], glob_ids[0]])
    rand_head = lax.dynamic_index_in_dim(rand_blocks, head, 0, keepdims=False).reshape(-1)
    rand_head = jnp.clip(rand_head, 0, block_count - 1)
    chosen, chunks[0] = choose(place, glob_keys, glob_values, packed[0])
    held, terms = scores(chunks, chosen, place, rand_head, table_size, shares)
    sent = grads(rand_head, chosen, held)
    terms = [flipped(terms[bits], "dp", bits) for bits in range(shares)]
    *terms, sent = lax.optimization_barrier((*terms, sent))
    back = lax.all_to_all(sent, "ctx", 0, 0)
    share = sum(term.astype(jnp.float32) for term in terms).astype(jnp.bfloat16)
    column = jnp.stack([flipped(share, "ctx", flip) for flip in HEADS_ORDER[:4]])
    quarter = jnp.concatenate([column, flipped(column, "ctx", 1)])
    across = flipped(quarter, "dp", 2)
    beside = flipped(quarter, "dp", 1)
    corner = flipped(across, "dp", 1)
    d_table = whole_table([quarter, beside, across, corner])
    d_query, d_key, d_value = unpack(back)
    return (d_query, d_key, d_value, d_table.reshape((2,) + glob_keys.shape))


def on_device(query, key, value, dout, glob_keys, glob_values, glob_ids, rand_blocks):
    head_count = rand_blocks.shape[0]
    one_head_each = lax.axis_size("ctx") == head_count == 8 and query.shape[1] == 2 * BLK
    if one_head_each and lax.axis_size("dp") == 4 and glob_keys.shape[0] % 2 == 0:
        plan = on_heads
    else:
        plan = on_ring
    return plan(query, key, value, dout, glob_keys, glob_values, glob_ids, rand_blocks)


def solution(mesh):
    placed = (
        P("dp", "ctx", None),
        P("dp", "ctx", None),
        P("dp", "ctx", None),
        P("dp", "ctx", None),
        P(),
        P(),
        P("dp", None),
        P(),
    )
    return jax.shard_map(
        on_device,
        mesh=mesh,
        in_specs=placed,
        out_specs=(P("dp", "ctx", None), P("dp", "ctx", None), P("dp", "ctx", None), P()),
        check_vma=False,
    )
```

```python
import functools
import math

import jax
import jax.numpy as jnp
from jax import lax
from jax.experimental import pallas as pl
from jax.experimental.pallas import tpu as pltpu
from jax.sharding import PartitionSpec as P

BLK = 64


def passed_along(shard, axis, by):
    length = lax.axis_size(axis)
    return lax.ppermute(shard, axis, [(i, (i + by) % length) for i in range(length)])


def padded(cells, sides, width):
    for axis, dim in sides:
        count = lax.axis_size(axis)
        ends = count - 1
        head = lax.slice_in_dim(cells, 0, width, axis=dim)
        tail = lax.slice_in_dim(cells, cells.shape[dim] - width, cells.shape[dim], axis=dim)
        cells = jnp.concatenate(
            [
                lax.ppermute(tail, axis, [(i, (i + 1) % count) for i in range(ends)]),
                cells,
                lax.ppermute(head, axis, [((i + 1) % count, i) for i in range(ends)]),
            ],
            axis=dim,
        )
    return cells


def passed_along_2(value, axis, steps):
    count = lax.axis_size(axis)
    leading, last = (max(0, -steps), min(count, count - steps))
    return lax.ppermute(value, axis, [(source, source + steps) for source in range(leading, last)])


def attend(
    q_head,
    o_grad,
    k_head,
    v_head,
    gk_head,
    gv_head,
    key_index,
    key_valid,
    scatter_count,
    rand_count,
):
    q_blocks = q_head.shape[0]
    head_size = q_head.shape[2]
    scaling = 1.0 / math.sqrt(head_size)
    local_lists = key_index.shape[1]
    keys_all = jnp.concatenate(
        [
            jnp.take(k_head, key_index, axis=0),
            jnp.broadcast_to(gk_head[None], (q_blocks,) + gk_head.shape),
        ],
        axis=1,
    ).reshape(q_blocks, -1, head_size)
    values_all = jnp.concatenate(
        [
            jnp.take(v_head, key_index, axis=0),
            jnp.broadcast_to(gv_head[None], (q_blocks,) + gv_head.shape),
        ],
        axis=1,
    ).reshape(q_blocks, -1, head_size)
    keep_mask = jnp.repeat(
        jnp.concatenate([key_valid, jnp.ones((q_blocks, 2), dtype=bool)], axis=1), BLK, axis=1
    )
    scores = (
        jnp.einsum("nqd,nkd->nqk", q_head, keys_all, preferred_element_type=jnp.float32) * scaling
    )
    scores = jnp.where(keep_mask[:, None, :], scores, -1e30)
    row_max = jnp.max(scores, axis=-1, keepdims=True)
    exp_scores = jnp.exp(scores - row_max)
    weights = exp_scores / jnp.sum(exp_scores, axis=-1, keepdims=True)
    weights_b = weights.astype(jnp.bfloat16)
    attn_out = jnp.einsum("nqk,nkd->nqd", weights_b, values_all, preferred_element_type=jnp.float32)
    row_dot = jnp.sum(o_grad.astype(jnp.float32) * attn_out, axis=-1, keepdims=True)
    prob_grad = jnp.einsum("nqd,nkd->nqk", o_grad, values_all, preferred_element_type=jnp.float32)
    score_grad = (weights * (prob_grad - row_dot) * scaling).astype(jnp.bfloat16)
    q_grad = jnp.einsum("nqk,nkd->nqd", score_grad, keys_all, preferred_element_type=jnp.float32)
    k_grad = jnp.einsum(
        "nqk,nqd->nkd", score_grad, q_head, preferred_element_type=jnp.float32
    ).reshape(q_blocks, local_lists + 2, BLK, head_size)
    v_grad = jnp.einsum(
        "nqk,nqd->nkd", weights_b, o_grad, preferred_element_type=jnp.float32
    ).reshape(q_blocks, local_lists + 2, BLK, head_size)
    flat_index = key_index.reshape(-1)
    k_local = (
        jnp.zeros(k_head.shape, jnp.float32)
        .at[flat_index]
        .add(k_grad[:, :scatter_count].reshape(-1, BLK, head_size))
    )
    v_local = (
        jnp.zeros(v_head.shape, jnp.float32)
        .at[flat_index]
        .add(v_grad[:, :scatter_count].reshape(-1, BLK, head_size))
    )
    grad_tiles = score_grad.reshape(q_blocks, BLK, local_lists + 2, BLK)[
        :, :, 3 : 3 + rand_count
    ].transpose(0, 2, 1, 3)
    prob_tiles = weights_b.reshape(q_blocks, BLK, local_lists + 2, BLK)[
        :, :, 3 : 3 + rand_count
    ].transpose(0, 2, 1, 3)
    return (
        q_grad,
        k_local,
        v_local,
        k_grad[:, local_lists:],
        v_grad[:, local_lists:],
        grad_tiles,
        prob_tiles,
    )


def by_heads(row_array, head_count):
    block_total = row_array.shape[0] // BLK
    return row_array.reshape(block_total, BLK, head_count, -1).transpose(2, 0, 1, 3)


def from_heads(head_array):
    head_count = head_array.shape[0]
    head_size = head_array.shape[3]
    return head_array.transpose(1, 2, 0, 3).reshape(-1, head_count * head_size)


def fetch_far(key_value, offset):
    return passed_along(key_value, "ctx", -offset)


def return_far(partials, offset):
    return passed_along(partials, "ctx", offset)


def on_ring(query, key, value, dout, glob_keys, glob_values, glob_ids, rand_blocks):
    row_count = query.shape[1]
    head_count = rand_blocks.shape[0]
    rand_count = rand_blocks.shape[2]
    head_size = query.shape[2] // head_count
    per_device = row_count // BLK
    span_count = lax.axis_size("ctx")
    device_pos = lax.axis_index("ctx")
    block_count = per_device * span_count
    offsets = [(slot + 1) * span_count // (rand_count + 1) for slot in range(rand_count)]
    key_value = jnp.stack([key[0], value[0]])
    extended = padded(key_value, (("ctx", 1),), row_count)
    far_spans = [fetch_far(key_value, offset) for offset in offsets]
    k_rows = jnp.concatenate([extended[0]] + [span[0] for span in far_spans], axis=0)
    v_rows = jnp.concatenate([extended[1]] + [span[1] for span in far_spans], axis=0)
    first_block = device_pos * per_device
    key_base = first_block - per_device
    query_ids = first_block + jnp.arange(per_device, dtype=jnp.int32)
    window = query_ids[:, None] + jnp.arange(-1, 2, dtype=jnp.int32)[None, :]
    key_valid = jnp.concatenate(
        [(window >= 0) & (window < block_count), jnp.ones((per_device, rand_count), dtype=bool)],
        axis=1,
    )
    window_local = jnp.clip(window - key_base, 0, 3 * per_device - 1)
    rand_rows = lax.dynamic_slice_in_dim(rand_blocks, first_block, per_device, 1)
    offset_table = jnp.array(offsets, dtype=jnp.int32)
    far_starts = (device_pos + offset_table) % span_count * per_device
    slot_base = (3 + jnp.arange(rand_count, dtype=jnp.int32)) * per_device
    rand_local = rand_rows - far_starts[None, None, :] + slot_base[None, None, :]
    all_lists = jnp.concatenate(
        [jnp.broadcast_to(window_local[None], (head_count,) + window_local.shape), rand_local],
        axis=2,
    )
    key_index = jnp.clip(all_lists, 0, (3 + rand_count) * per_device - 1)
    chosen = glob_ids[0]
    gk_heads = by_heads(jnp.take(glob_keys, chosen, axis=0).reshape(2 * BLK, -1), head_count)
    gv_heads = by_heads(jnp.take(glob_values, chosen, axis=0).reshape(2 * BLK, -1), head_count)
    scatter_count = 3 + rand_count

    def per_head(pieces):
        q_head, o_grad, k_head, v_head, gk_head, gv_head, index_head = pieces
        return attend(
            q_head,
            o_grad,
            k_head,
            v_head,
            gk_head,
            gv_head,
            index_head,
            key_valid,
            scatter_count,
            rand_count,
        )

    results = lax.map(
        per_head,
        (
            by_heads(query[0], head_count),
            by_heads(dout[0], head_count),
            by_heads(k_rows, head_count),
            by_heads(v_rows, head_count),
            gk_heads,
            gv_heads,
            key_index,
        ),
    )
    q_grad = results[0]
    kv_grads = jnp.stack([results[1], results[2]])
    lower_part = kv_grads[:, :, :per_device]
    upper_part = kv_grads[:, :, 2 * per_device : 3 * per_device]
    from_below = passed_along_2(upper_part.astype(jnp.bfloat16), "ctx", 1).astype(upper_part.dtype)
    from_above = passed_along_2(lower_part.astype(jnp.bfloat16), "ctx", -1).astype(lower_part.dtype)
    own_grads = kv_grads[:, :, per_device : 2 * per_device] + from_below + from_above
    for slot in range(rand_count):
        start = (3 + slot) * per_device
        own_grads = own_grads + return_far(
            kv_grads[:, :, start : start + per_device], offsets[slot]
        )
    global_part = jnp.stack([jnp.sum(results[3], axis=1), jnp.sum(results[4], axis=1)])
    global_part = global_part.transpose(0, 2, 3, 1, 4).reshape(2, 2, BLK, head_count * head_size)
    one_hot = (chosen[:, None] == jnp.arange(glob_keys.shape[0], dtype=jnp.int32)[None, :]).astype(
        jnp.float32
    )
    table_term = jnp.einsum("sg,ksbd->kgbd", one_hot, global_part, precision=lax.Precision.HIGHEST)
    table_grad = lax.psum(table_term, ("ctx", "dp"))
    d_query = from_heads(q_grad).astype(jnp.bfloat16)[None]
    d_key = from_heads(own_grads[0]).astype(jnp.bfloat16)[None]
    d_value = from_heads(own_grads[1]).astype(jnp.bfloat16)[None]
    return (d_query, d_key, d_value, table_grad)


VMEM_BYTES = 24 * 1024 * 1024
SMALL_VMEM_BYTES = 4 * 1024 * 1024
LARGE_VMEM_BYTES = 60 * 1024 * 1024
FINISH_VMEM_BYTES = 24 * 1024 * 1024
MASKED = -1e30
EARLY_FLOPS = 5 * 10**9
GROUP = 8
ORDER = (0, 4, 2, 5, 3, 6, 7, 1)
COLUMN = (0, 2, 4, 6)


def dot(left, right, left_dim, right_dim):
    dims = (((left_dim,), (right_dim,)), ((), ()))
    return lax.dot_general(left, right, dims, preferred_element_type=jnp.float32)


def in_vmem(count):
    return [pl.BlockSpec(memory_space=pltpu.VMEM)] * count


def pack_kernel(count, *refs):
    ins, outs = refs[:4], refs[4 : 4 + count]
    held, made, in_sems, out_sems = refs[4 + count :]
    head_size = made.shape[3]
    me = lax.axis_index("ctx")
    loads = [
        pltpu.make_async_copy(ref.at[0], held.at[place], in_sems.at[place])
        for place, ref in enumerate(ins)
    ]
    for load in loads:
        load.start()
    for load in loads:
        load.wait()
    stores = []
    for flip in ORDER:
        at = pl.multiple_of((me ^ flip) * head_size, head_size)
        made[flip] = held[:, :, pl.ds(at, head_size)]
        store = pltpu.make_async_copy(made.at[flip], outs[flip], out_sems.at[flip])
        store.start()
        stores.append(store)
    for store in stores:
        store.wait()


def pack(query, key, value, dout, head_count):
    _, rows, width = query.shape
    chunk = (4, rows, width // head_count)
    in_hbm = pl.BlockSpec(memory_space=pltpu.HBM)
    return pl.pallas_call(
        functools.partial(pack_kernel, head_count),
        in_specs=[in_hbm] * 4,
        out_specs=[in_hbm] * head_count,
        out_shape=[jax.ShapeDtypeStruct(chunk, query.dtype)] * head_count,
        scratch_shapes=[
            pltpu.VMEM((4, rows, width), query.dtype),
            pltpu.VMEM((head_count,) + chunk, query.dtype),
            pltpu.SemaphoreType.DMA((4,)),
            pltpu.SemaphoreType.DMA((head_count,)),
        ],
        compiler_params=pltpu.CompilerParams(vmem_limit_bytes=LARGE_VMEM_BYTES),
        cost_estimate=pl.CostEstimate(flops=0, bytes_accessed=16 * rows * width, transcendentals=0),
        name="pack_heads",
    )(query, key, value, dout)


def choose_kernel(place_ref, gk_ref, gv_ref, own_ref, out_ref, held_ref, sems):
    head_size = out_ref.shape[2]
    columns = pl.ds(pl.multiple_of(place_ref[0] * head_size, head_size), head_size)
    copies = [
        pltpu.make_async_copy(
            ref.at[place_ref[2 + slot], :, columns],
            out_ref.at[2 * kind + slot],
            sems.at[2 * kind + slot],
        )
        for kind, ref in enumerate((gk_ref, gv_ref))
        for slot in range(2)
    ]
    copies.append(pltpu.make_async_copy(own_ref, held_ref, sems.at[4]))
    for copy in copies:
        copy.start()
    for copy in copies:
        copy.wait()


def choose(place, glob_keys, glob_values, own):
    head_size = own.shape[2]
    return pl.pallas_call(
        choose_kernel,
        in_specs=[pl.BlockSpec(memory_space=pltpu.SMEM)]
        + [pl.BlockSpec(memory_space=pltpu.HBM)] * 3,
        out_specs=in_vmem(2),
        out_shape=[
            jax.ShapeDtypeStruct((4, BLK, head_size), glob_keys.dtype),
            jax.ShapeDtypeStruct(own.shape, own.dtype),
        ],
        scratch_shapes=[pltpu.SemaphoreType.DMA((5,))],
        compiler_params=pltpu.CompilerParams(vmem_limit_bytes=SMALL_VMEM_BYTES),
        cost_estimate=pl.CostEstimate(
            flops=0, bytes_accessed=16 * BLK * head_size, transcendentals=0
        ),
        name="choose_blocks",
    )(place, glob_keys, glob_values, own)


def split_rows(block):
    empty = jnp.zeros((BLK, block.shape[1]), block.dtype)
    return jnp.concatenate(
        [
            jnp.concatenate([block[:BLK], empty], axis=0),
            jnp.concatenate([empty, block[BLK:]], axis=0),
        ],
        axis=1,
    )


def list_places(rand_ref, span, rand_count):
    return [
        [
            pl.multiple_of((rand_ref[(2 * span + half) * rand_count + slot] + 1) * BLK, BLK)
            for slot in range(rand_count)
        ]
        for half in range(2)
    ]


def gathered(pool, at, places, table_blocks):
    window = pool[at : at + 4 * BLK]
    lists = [
        jnp.concatenate([edge] + [pool[pl.ds(p, BLK)] for p in places[half]], axis=0)
        for half, edge in enumerate((window[:BLK], window[3 * BLK :]))
    ]
    both = jnp.concatenate([window[BLK : 3 * BLK]] + table_blocks, axis=0)
    return jnp.concatenate(lists, axis=1), both


def score_kernel(spans, shares, place_ref, rand_ref, *refs):
    x_refs, g_ref = refs[:spans], refs[spans]
    q_all, k_all, o_all, p_all, ds_all = refs[spans + 1 : spans + 6]
    share_refs = refs[spans + 6 : spans + 6 + shares]
    v_all, table = refs[spans + 6 + shares :]
    _, rows, head_size = x_refs[0].shape
    rand_count = rand_ref.shape[0] // (2 * spans)
    scaling = 1.0 / math.sqrt(head_size)
    me = place_ref[0]
    top = BLK + spans * rows
    for pool in (k_all, v_all):
        pool[:BLK] = jnp.zeros((BLK, head_size), pool.dtype)
        pool[top:] = jnp.zeros((BLK, head_size), pool.dtype)
    starts = [pl.multiple_of((me ^ flip) * rows, rows) for flip in ORDER]
    for at, ref in zip(starts, x_refs):
        q_all[pl.ds(at, rows)] = ref[0]
        k_all[pl.ds(pl.multiple_of(at + BLK, BLK), rows)] = ref[1]
        v_all[pl.ds(pl.multiple_of(at + BLK, BLK), rows)] = ref[2]
        o_all[pl.ds(at, rows)] = ref[3]
    gk = [g_ref[0], g_ref[1]]
    gv = [g_ref[2], g_ref[3]]
    own = (1 + rand_count) * BLK
    first = lax.broadcasted_iota(jnp.int32, (1, rows), 1) < BLK
    table_terms = [None, None]
    for group in range(0, spans, GROUP):
        members = range(group, min(group + GROUP, spans))
        made = []
        for span in members:
            at = span * rows
            q = q_all[at : at + rows]
            o = o_all[at : at + rows]
            places = list_places(rand_ref, span, rand_count)
            k_own, k_both = gathered(k_all, at, places, gk)
            v_own, v_both = gathered(v_all, at, places, gv)
            s_own = dot(k_own, split_rows(q), 1, 1) * scaling
            s_both = dot(k_both, q, 1, 1) * scaling
            g_own = dot(v_own, split_rows(o), 1, 1)
            g_both = dot(v_both, o, 1, 1)
            if span == 0 or span == spans - 1:
                row = lax.broadcasted_iota(jnp.int32, (own, 1), 0) < BLK
                outside = row & (first if span == 0 else jnp.logical_not(first))
                s_own = jnp.where(outside, MASKED, s_own)
            made.append((q, o, s_own, s_both, g_own, g_both))
        tops = [
            jnp.maximum(
                jnp.max(s_own, axis=0, keepdims=True), jnp.max(s_both, axis=0, keepdims=True)
            )
            for _, _, s_own, s_both, _, _ in made
        ]
        powers = [
            (jnp.exp(s_own - top_score), jnp.exp(s_both - top_score))
            for top_score, (_, _, s_own, s_both, _, _) in zip(tops, made)
        ]
        inverses = [
            1.0 / (jnp.sum(e_own, axis=0, keepdims=True) + jnp.sum(e_both, axis=0, keepdims=True))
            for e_own, e_both in powers
        ]
        weights = []
        for (e_own, e_both), inverse, (_, _, _, _, g_own, g_both) in zip(powers, inverses, made):
            p_own = e_own * inverse
            p_both = e_both * inverse
            pb_own = p_own.astype(jnp.bfloat16)
            pb_both = p_both.astype(jnp.bfloat16)
            row_dot = jnp.sum(
                pb_own.astype(jnp.float32) * g_own, axis=0, keepdims=True
            ) + jnp.sum(pb_both.astype(jnp.float32) * g_both, axis=0, keepdims=True)
            weights.append((p_own, p_both, pb_own, pb_both, row_dot))
        for span, (q, o, _, _, g_own, g_both), (p_own, p_both, pb_own, pb_both, row_dot) in zip(
            members, made, weights
        ):
            ds_own = (p_own * (g_own - row_dot) * scaling).astype(jnp.bfloat16)
            ds_both = (p_both * (g_both - row_dot) * scaling).astype(jnp.bfloat16)
            p_all[span, :own] = pb_own
            p_all[span, own:] = pb_both
            ds_all[span, :own] = ds_own
            ds_all[span, own:] = ds_both
            for kind, (weight, x) in enumerate(((ds_both, q), (pb_both, o))):
                term = dot(weight[2 * BLK :], x, 1, 0)
                so_far = table_terms[kind]
                table_terms[kind] = term if so_far is None else so_far + term
    table[...] = jnp.zeros(table.shape, table.dtype)
    kinds = table.shape[0] // 2
    for slot in range(2):
        for kind, shared in enumerate(table_terms):
            block = shared[slot * BLK : (slot + 1) * BLK]
            table[kind * kinds + place_ref[2 + slot]] = block
    for flip, ref in enumerate(share_refs):
        count = table.shape[0] // shares
        start = (place_ref[1] ^ flip) * count
        ref[...] = table[pl.ds(start, count)].astype(ref.dtype)


def scores(chunks, chosen, place, rand_head, table_size, shares):
    spans = len(chunks)
    _, rows, head_size = chunks[0].shape
    keys = 8 * BLK
    padded_rows = spans * rows + 2 * BLK
    keys_each = spans * rows * keys
    half = lambda *shape: jax.ShapeDtypeStruct(shape, jnp.bfloat16)
    outs = [
        half(spans * rows, head_size),
        half(padded_rows, head_size),
        half(spans * rows, head_size),
        half(spans, keys, rows),
        half(spans, keys, rows),
    ] + [half(2 * table_size // shares, BLK, head_size)] * shares
    results = pl.pallas_call(
        functools.partial(score_kernel, spans, shares),
        in_specs=[pl.BlockSpec(memory_space=pltpu.SMEM)] * 2 + in_vmem(spans + 1),
        out_specs=in_vmem(len(outs)),
        out_shape=outs,
        scratch_shapes=[
            pltpu.VMEM((padded_rows, head_size), jnp.bfloat16),
            pltpu.VMEM((2 * table_size, BLK, head_size), jnp.float32),
        ],
        compiler_params=pltpu.CompilerParams(vmem_limit_bytes=VMEM_BYTES),
        cost_estimate=pl.CostEstimate(
            flops=4 * keys_each * head_size,
            bytes_accessed=8 * spans * rows * head_size,
            transcendentals=keys_each,
        ),
        name="scores",
    )(place, rand_head, *chunks, chosen)
    return results[:5], results[5:]


def far_spans(spans, rand_count):
    return [(slot + 1) * spans // (rand_count + 1) for slot in range(rand_count)]


def grad_kernel(
    rand_ref, g_ref, q_all, k_all, o_all, p_all, ds_all, out_ref, made, sems
):
    spans, _, rows, head_size = made.shape
    rand_count = rand_ref.shape[0] // (2 * spans)
    own = (1 + rand_count) * BLK
    gk = [g_ref[0], g_ref[1]]
    offsets = far_spans(spans, rand_count)
    first = lax.broadcasted_iota(jnp.int32, (1, rows), 1) < BLK
    terms = []
    for span in range(spans):
        at = span * rows
        q = q_all[at : at + rows]
        o = o_all[at : at + rows]
        k_own, k_both = gathered(k_all, at, list_places(rand_ref, span, rand_count), gk)
        wide = dot(ds_all[span, :own], k_own, 0, 0)
        dq = jnp.concatenate([wide[:BLK, :head_size], wide[BLK:, head_size:]], axis=0)
        dq = dq + dot(ds_all[span, own:], k_both, 0, 0)
        made[span, 0] = dq.astype(made.dtype)
        keeps = [first]
        for slot, offset in enumerate(offsets):
            lower = [
                rand_ref[(2 * span + half) * rand_count + slot] == 2 * ((span + offset) % spans)
                for half in range(2)
            ]
            keeps.append((first & lower[0]) | (jnp.logical_not(first) & lower[1]))
        keeps = [jnp.where(keep, 1.0, 0.0).astype(made.dtype) for keep in keeps]
        pair = []
        for weights, x in ((ds_all, q), (p_all, o)):
            parts = [weights[span, own : own + 2 * BLK]]
            for place, keep in enumerate(keeps):
                block = weights[span, place * BLK : (place + 1) * BLK]
                lower = block * keep
                parts += [lower, block - lower]
            pair.append(dot(jnp.concatenate(parts, axis=0), x, 1, 0))
        terms.append(pair)
    copies = []
    for span in range(spans):
        for kind in range(2):
            part = lambda source, start, count: terms[source][kind][start : start + count]
            edges = [
                part(span - 1, 3 * BLK, BLK) if span > 0 else None,
                part(span + 1, 2 * BLK, BLK) if span < spans - 1 else None,
            ]
            edges = [jnp.zeros((BLK, head_size), jnp.float32) if e is None else e for e in edges]
            total = part(span, 0, 2 * BLK) + jnp.concatenate(edges, axis=0)
            for slot, offset in enumerate(offsets):
                total = total + part((span - offset) % spans, (4 + 2 * slot) * BLK, 2 * BLK)
            made[span, 1 + kind] = total.astype(made.dtype)
        copy = pltpu.make_async_copy(made.at[span], out_ref.at[span], sems.at[span])
        copy.start()
        copies.append(copy)
    for copy in copies:
        copy.wait()


def grads(rand_head, chosen, held):
    spans, keys, rows = held[3].shape
    head_size = held[1].shape[1]
    keys_each = spans * keys * rows
    shape = (spans, 3, rows, head_size)
    return pl.pallas_call(
        grad_kernel,
        in_specs=[pl.BlockSpec(memory_space=pltpu.SMEM)] + in_vmem(1 + len(held)),
        out_specs=pl.BlockSpec(memory_space=pltpu.HBM),
        out_shape=jax.ShapeDtypeStruct(shape, jnp.bfloat16),
        scratch_shapes=[
            pltpu.VMEM(shape, jnp.bfloat16),
            pltpu.SemaphoreType.DMA((spans,)),
        ],
        compiler_params=pltpu.CompilerParams(vmem_limit_bytes=VMEM_BYTES),
        cost_estimate=pl.CostEstimate(
            flops=6 * keys_each * head_size,
            bytes_accessed=8 * spans * rows * head_size,
            transcendentals=0,
        ),
        name="grads",
    )(rand_head, chosen, *held)


def early_kernel(sides, *refs):
    parts, out_ref = refs[:-1], refs[-1]
    head_size = parts[0].shape[2]
    head = lax.axis_index("ctx")
    share = lax.axis_index("dp")
    for side, ref in zip(sides, parts):
        for place in range(ref.shape[0]):
            bits = side[place // len(COLUMN)]
            flip = COLUMN[place % len(COLUMN)]
            columns = pl.ds(pl.multiple_of((head ^ flip) * head_size, head_size), head_size)
            out_ref[share ^ bits, :, columns] = ref[place].astype(out_ref.dtype)


def early_table(shares, head_count, sides, parts):
    _, rows, head_size = parts[0].shape
    shape = (shares, rows, head_count * head_size)
    return pl.pallas_call(
        functools.partial(early_kernel, sides),
        in_specs=in_vmem(len(parts)),
        out_specs=pl.BlockSpec(memory_space=pltpu.VMEM),
        out_shape=jax.ShapeDtypeStruct(shape, jnp.float32),
        compiler_params=pltpu.CompilerParams(vmem_limit_bytes=VMEM_BYTES),
        cost_estimate=pl.CostEstimate(
            flops=EARLY_FLOPS, bytes_accessed=2**21, transcendentals=0
        ),
        name="early_table",
    )(*parts)


def finish_kernel(sides, *refs):
    count = len(sides)
    parts, x_ref = refs[:count], refs[count]
    grad_refs, table_ref = refs[count + 2 : count + 5], refs[count + 5]
    x_held, grad_made, table_made, x_sem, grad_sems, table_sems = refs[count + 6 :]
    heads, _, _, head_size = x_held.shape
    load = pltpu.make_async_copy(x_ref, x_held, x_sem)
    load.start()
    me = lax.axis_index("ctx")
    share = lax.axis_index("dp")
    stores = []
    for side, ref in zip(sides, parts):
        for place in range(ref.shape[0]):
            at = len(stores)
            bits = side[place // len(COLUMN)]
            flip = COLUMN[place % len(COLUMN)] ^ 1
            columns = pl.ds(pl.multiple_of((me ^ flip) * head_size, head_size), head_size)
            table_made[at] = ref[place].astype(table_made.dtype)
            store = pltpu.make_async_copy(
                table_made.at[at], table_ref.at[share ^ bits, :, columns], table_sems.at[at]
            )
            store.start()
            stores.append(store)
    load.wait()
    for place, ref in enumerate(grad_refs):
        for head in range(heads):
            columns = slice(head * head_size, (head + 1) * head_size)
            grad_made[place, :, columns] = x_held[head, place]
        store = pltpu.make_async_copy(grad_made.at[place], ref.at[0], grad_sems.at[place])
        store.start()
        stores.append(store)
    for store in stores:
        store.wait()


def finish(x, table, sides, parts):
    heads, kinds, rows, head_size = x.shape
    blocks = sum(part.shape[0] for part in parts)
    in_hbm = pl.BlockSpec(memory_space=pltpu.HBM)
    grad = jax.ShapeDtypeStruct((1, rows, heads * head_size), x.dtype)
    return pl.pallas_call(
        functools.partial(finish_kernel, sides),
        in_specs=in_vmem(len(parts)) + [in_hbm] * 2,
        out_specs=[in_hbm] * (kinds + 1),
        out_shape=[grad] * kinds + [jax.ShapeDtypeStruct(table.shape, table.dtype)],
        scratch_shapes=[
            pltpu.VMEM(x.shape, x.dtype),
            pltpu.VMEM((kinds, rows, heads * head_size), x.dtype),
            pltpu.VMEM((blocks, rows, head_size), table.dtype),
            pltpu.SemaphoreType.DMA,
            pltpu.SemaphoreType.DMA((kinds,)),
            pltpu.SemaphoreType.DMA((blocks,)),
        ],
        input_output_aliases={len(parts) + 1: kinds},
        compiler_params=pltpu.CompilerParams(vmem_limit_bytes=FINISH_VMEM_BYTES),
        cost_estimate=pl.CostEstimate(flops=0, bytes_accessed=2**21, transcendentals=0),
        name="finish",
    )(*parts, x, table)


def flipped(array, axis, bits):
    if bits == 0:
        return array
    return lax.ppermute(array, axis, [(i, i ^ bits) for i in range(lax.axis_size(axis))])


def on_heads(query, key, value, dout, glob_keys, glob_values, glob_ids, rand_blocks):
    head_count, block_count, _ = rand_blocks.shape
    head_size = query.shape[2] // head_count
    table_size = glob_keys.shape[0]
    shares = lax.axis_size("dp")
    head = lax.axis_index("ctx").astype(jnp.int32)
    sequence = lax.axis_index("dp").astype(jnp.int32)
    packed = pack(query, key, value, dout, head_count)
    chunks = [flipped(packed[flip], "ctx", flip) for flip in ORDER]
    place = jnp.concatenate([head[None], sequence[None], glob_ids[0]])
    rand_head = lax.dynamic_index_in_dim(rand_blocks, head, 0, keepdims=False).reshape(-1)
    rand_head = jnp.clip(rand_head, 0, block_count - 1)
    chosen, chunks[0] = choose(place, glob_keys, glob_values, packed[0])
    held, terms = scores(chunks, chosen, place, rand_head, table_size, shares)
    sent = grads(rand_head, chosen, held)
    terms = [flipped(terms[bits], "dp", bits) for bits in range(shares)]
    *terms, sent = lax.optimization_barrier((*terms, sent))
    back = lax.all_to_all(sent, "ctx", 0, 0)
    share = sum(term.astype(jnp.float32) for term in terms).astype(jnp.bfloat16)
    share = share.reshape(1, -1, head_size)
    column = jnp.concatenate([flipped(share, "ctx", flip) for flip in COLUMN])
    even = jnp.concatenate([column, flipped(column, "dp", 2)])
    odd = flipped(even, "ctx", 1)
    beside_even = flipped(even, "dp", 1)
    beside_odd = flipped(odd, "dp", 1)
    d_table = early_table(shares, head_count, ((0, 2), (1, 3)), [even, beside_even])
    d_query, d_key, d_value, d_table = finish(
        back, d_table, ((0, 2), (1, 3)), [odd, beside_odd]
    )
    return (d_query, d_key, d_value, d_table.reshape((2,) + glob_keys.shape))


def on_device(query, key, value, dout, glob_keys, glob_values, glob_ids, rand_blocks):
    head_count = rand_blocks.shape[0]
    one_head_each = lax.axis_size("ctx") == head_count == 8 and query.shape[1] == 2 * BLK
    if one_head_each and lax.axis_size("dp") == 4 and glob_keys.shape[0] % 2 == 0:
        plan = on_heads
    else:
        plan = on_ring
    return plan(query, key, value, dout, glob_keys, glob_values, glob_ids, rand_blocks)


def solution(mesh):
    placed = (
        P("dp", "ctx", None),
        P("dp", "ctx", None),
        P("dp", "ctx", None),
        P("dp", "ctx", None),
        P(),
        P(),
        P("dp", None),
        P(),
    )
    return jax.shard_map(
        on_device,
        mesh=mesh,
        in_specs=placed,
        out_specs=(P("dp", "ctx", None), P("dp", "ctx", None), P("dp", "ctx", None), P()),
        check_vma=False,
    )
```

```python
import functools
import math

import jax
import jax.numpy as jnp
from jax import lax
from jax.experimental import pallas as pl
from jax.experimental.pallas import tpu as pltpu
from jax.sharding import PartitionSpec as P

BLK = 64


def passed_along(shard, axis, by):
    length = lax.axis_size(axis)
    return lax.ppermute(shard, axis, [(i, (i + by) % length) for i in range(length)])


def padded(cells, sides, width):
    for axis, dim in sides:
        count = lax.axis_size(axis)
        ends = count - 1
        head = lax.slice_in_dim(cells, 0, width, axis=dim)
        tail = lax.slice_in_dim(cells, cells.shape[dim] - width, cells.shape[dim], axis=dim)
        cells = jnp.concatenate(
            [
                lax.ppermute(tail, axis, [(i, (i + 1) % count) for i in range(ends)]),
                cells,
                lax.ppermute(head, axis, [((i + 1) % count, i) for i in range(ends)]),
            ],
            axis=dim,
        )
    return cells


def passed_along_2(value, axis, steps):
    count = lax.axis_size(axis)
    leading, last = (max(0, -steps), min(count, count - steps))
    return lax.ppermute(value, axis, [(source, source + steps) for source in range(leading, last)])


def attend(
    q_head,
    o_grad,
    k_head,
    v_head,
    gk_head,
    gv_head,
    key_index,
    key_valid,
    scatter_count,
    rand_count,
):
    q_blocks = q_head.shape[0]
    head_size = q_head.shape[2]
    scaling = 1.0 / math.sqrt(head_size)
    local_lists = key_index.shape[1]
    keys_all = jnp.concatenate(
        [
            jnp.take(k_head, key_index, axis=0),
            jnp.broadcast_to(gk_head[None], (q_blocks,) + gk_head.shape),
        ],
        axis=1,
    ).reshape(q_blocks, -1, head_size)
    values_all = jnp.concatenate(
        [
            jnp.take(v_head, key_index, axis=0),
            jnp.broadcast_to(gv_head[None], (q_blocks,) + gv_head.shape),
        ],
        axis=1,
    ).reshape(q_blocks, -1, head_size)
    keep_mask = jnp.repeat(
        jnp.concatenate([key_valid, jnp.ones((q_blocks, 2), dtype=bool)], axis=1), BLK, axis=1
    )
    scores = (
        jnp.einsum("nqd,nkd->nqk", q_head, keys_all, preferred_element_type=jnp.float32) * scaling
    )
    scores = jnp.where(keep_mask[:, None, :], scores, -1e30)
    row_max = jnp.max(scores, axis=-1, keepdims=True)
    exp_scores = jnp.exp(scores - row_max)
    weights = exp_scores / jnp.sum(exp_scores, axis=-1, keepdims=True)
    weights_b = weights.astype(jnp.bfloat16)
    attn_out = jnp.einsum("nqk,nkd->nqd", weights_b, values_all, preferred_element_type=jnp.float32)
    row_dot = jnp.sum(o_grad.astype(jnp.float32) * attn_out, axis=-1, keepdims=True)
    prob_grad = jnp.einsum("nqd,nkd->nqk", o_grad, values_all, preferred_element_type=jnp.float32)
    score_grad = (weights * (prob_grad - row_dot) * scaling).astype(jnp.bfloat16)
    q_grad = jnp.einsum("nqk,nkd->nqd", score_grad, keys_all, preferred_element_type=jnp.float32)
    k_grad = jnp.einsum(
        "nqk,nqd->nkd", score_grad, q_head, preferred_element_type=jnp.float32
    ).reshape(q_blocks, local_lists + 2, BLK, head_size)
    v_grad = jnp.einsum(
        "nqk,nqd->nkd", weights_b, o_grad, preferred_element_type=jnp.float32
    ).reshape(q_blocks, local_lists + 2, BLK, head_size)
    flat_index = key_index.reshape(-1)
    k_local = (
        jnp.zeros(k_head.shape, jnp.float32)
        .at[flat_index]
        .add(k_grad[:, :scatter_count].reshape(-1, BLK, head_size))
    )
    v_local = (
        jnp.zeros(v_head.shape, jnp.float32)
        .at[flat_index]
        .add(v_grad[:, :scatter_count].reshape(-1, BLK, head_size))
    )
    grad_tiles = score_grad.reshape(q_blocks, BLK, local_lists + 2, BLK)[
        :, :, 3 : 3 + rand_count
    ].transpose(0, 2, 1, 3)
    prob_tiles = weights_b.reshape(q_blocks, BLK, local_lists + 2, BLK)[
        :, :, 3 : 3 + rand_count
    ].transpose(0, 2, 1, 3)
    return (
        q_grad,
        k_local,
        v_local,
        k_grad[:, local_lists:],
        v_grad[:, local_lists:],
        grad_tiles,
        prob_tiles,
    )


def by_heads(row_array, head_count):
    block_total = row_array.shape[0] // BLK
    return row_array.reshape(block_total, BLK, head_count, -1).transpose(2, 0, 1, 3)


def from_heads(head_array):
    head_count = head_array.shape[0]
    head_size = head_array.shape[3]
    return head_array.transpose(1, 2, 0, 3).reshape(-1, head_count * head_size)


def fetch_far(key_value, offset):
    return passed_along(key_value, "ctx", -offset)


def return_far(partials, offset):
    return passed_along(partials, "ctx", offset)


def on_ring(query, key, value, dout, glob_keys, glob_values, glob_ids, rand_blocks):
    row_count = query.shape[1]
    head_count = rand_blocks.shape[0]
    rand_count = rand_blocks.shape[2]
    head_size = query.shape[2] // head_count
    per_device = row_count // BLK
    span_count = lax.axis_size("ctx")
    device_pos = lax.axis_index("ctx")
    block_count = per_device * span_count
    offsets = [(slot + 1) * span_count // (rand_count + 1) for slot in range(rand_count)]
    key_value = jnp.stack([key[0], value[0]])
    extended = padded(key_value, (("ctx", 1),), row_count)
    far_spans = [fetch_far(key_value, offset) for offset in offsets]
    k_rows = jnp.concatenate([extended[0]] + [span[0] for span in far_spans], axis=0)
    v_rows = jnp.concatenate([extended[1]] + [span[1] for span in far_spans], axis=0)
    first_block = device_pos * per_device
    key_base = first_block - per_device
    query_ids = first_block + jnp.arange(per_device, dtype=jnp.int32)
    window = query_ids[:, None] + jnp.arange(-1, 2, dtype=jnp.int32)[None, :]
    key_valid = jnp.concatenate(
        [(window >= 0) & (window < block_count), jnp.ones((per_device, rand_count), dtype=bool)],
        axis=1,
    )
    window_local = jnp.clip(window - key_base, 0, 3 * per_device - 1)
    rand_rows = lax.dynamic_slice_in_dim(rand_blocks, first_block, per_device, 1)
    offset_table = jnp.array(offsets, dtype=jnp.int32)
    far_starts = (device_pos + offset_table) % span_count * per_device
    slot_base = (3 + jnp.arange(rand_count, dtype=jnp.int32)) * per_device
    rand_local = rand_rows - far_starts[None, None, :] + slot_base[None, None, :]
    all_lists = jnp.concatenate(
        [jnp.broadcast_to(window_local[None], (head_count,) + window_local.shape), rand_local],
        axis=2,
    )
    key_index = jnp.clip(all_lists, 0, (3 + rand_count) * per_device - 1)
    chosen = glob_ids[0]
    gk_heads = by_heads(jnp.take(glob_keys, chosen, axis=0).reshape(2 * BLK, -1), head_count)
    gv_heads = by_heads(jnp.take(glob_values, chosen, axis=0).reshape(2 * BLK, -1), head_count)
    scatter_count = 3 + rand_count

    def per_head(pieces):
        q_head, o_grad, k_head, v_head, gk_head, gv_head, index_head = pieces
        return attend(
            q_head,
            o_grad,
            k_head,
            v_head,
            gk_head,
            gv_head,
            index_head,
            key_valid,
            scatter_count,
            rand_count,
        )

    results = lax.map(
        per_head,
        (
            by_heads(query[0], head_count),
            by_heads(dout[0], head_count),
            by_heads(k_rows, head_count),
            by_heads(v_rows, head_count),
            gk_heads,
            gv_heads,
            key_index,
        ),
    )
    q_grad = results[0]
    kv_grads = jnp.stack([results[1], results[2]])
    lower_part = kv_grads[:, :, :per_device]
    upper_part = kv_grads[:, :, 2 * per_device : 3 * per_device]
    from_below = passed_along_2(upper_part.astype(jnp.bfloat16), "ctx", 1).astype(upper_part.dtype)
    from_above = passed_along_2(lower_part.astype(jnp.bfloat16), "ctx", -1).astype(lower_part.dtype)
    own_grads = kv_grads[:, :, per_device : 2 * per_device] + from_below + from_above
    for slot in range(rand_count):
        start = (3 + slot) * per_device
        own_grads = own_grads + return_far(
            kv_grads[:, :, start : start + per_device], offsets[slot]
        )
    global_part = jnp.stack([jnp.sum(results[3], axis=1), jnp.sum(results[4], axis=1)])
    global_part = global_part.transpose(0, 2, 3, 1, 4).reshape(2, 2, BLK, head_count * head_size)
    one_hot = (chosen[:, None] == jnp.arange(glob_keys.shape[0], dtype=jnp.int32)[None, :]).astype(
        jnp.float32
    )
    table_term = jnp.einsum("sg,ksbd->kgbd", one_hot, global_part, precision=lax.Precision.HIGHEST)
    table_grad = lax.psum(table_term, ("ctx", "dp"))
    d_query = from_heads(q_grad).astype(jnp.bfloat16)[None]
    d_key = from_heads(own_grads[0]).astype(jnp.bfloat16)[None]
    d_value = from_heads(own_grads[1]).astype(jnp.bfloat16)[None]
    return (d_query, d_key, d_value, table_grad)


VMEM_BYTES = 24 * 1024 * 1024
SMALL_VMEM_BYTES = 4 * 1024 * 1024
LARGE_VMEM_BYTES = 60 * 1024 * 1024
FINISH_VMEM_BYTES = 24 * 1024 * 1024
MASKED = -1e30
PACK_FLOPS = 2 * 10**9
EARLY_FLOPS = 5 * 10**9
GROUP = 8
ORDER = (0, 4, 2, 5, 3, 6, 7, 1)
COLUMN = (0, 2, 4, 6)


def dot(left, right, left_dim, right_dim):
    dims = (((left_dim,), (right_dim,)), ((), ()))
    return lax.dot_general(left, right, dims, preferred_element_type=jnp.float32)


def in_vmem(count):
    return [pl.BlockSpec(memory_space=pltpu.VMEM)] * count


def first_kernel(q_ref, k_ref, v_ref, o_ref, out_ref, held, sems, out_sem):
    head_size = out_ref.shape[2]
    at = pl.multiple_of((lax.axis_index("ctx") ^ ORDER[1]) * head_size, head_size)
    copies = [
        pltpu.make_async_copy(
            ref.at[0, :, pl.ds(at, head_size)], held.at[place], sems.at[place]
        )
        for place, ref in enumerate((q_ref, k_ref, v_ref, o_ref))
    ]
    for copy in copies:
        copy.start()
    for copy in copies:
        copy.wait()
    store = pltpu.make_async_copy(held, out_ref, out_sem)
    store.start()
    store.wait()


def pack_kernel(count, *refs):
    ins, outs = refs[:4], refs[5 : 5 + count]
    held, made, in_sems, out_sems = refs[5 + count :]
    head_size = made.shape[3]
    me = lax.axis_index("ctx")
    loads = [
        pltpu.make_async_copy(ref.at[0], held.at[place], in_sems.at[place])
        for place, ref in enumerate(ins)
    ]
    for load in loads:
        load.start()
    for load in loads:
        load.wait()
    stores = []
    for place, flip in enumerate(ORDER[2:] + ORDER[:1]):
        at = pl.multiple_of((me ^ flip) * head_size, head_size)
        made[place] = held[:, :, pl.ds(at, head_size)]
        store = pltpu.make_async_copy(made.at[place], outs[place], out_sems.at[place])
        store.start()
        stores.append(store)
    for store in stores:
        store.wait()


def pack(query, key, value, dout, head_count):
    _, rows, width = query.shape
    arrays = (query, key, value, dout)
    chunk = (4, rows, width // head_count)
    shape = jax.ShapeDtypeStruct(chunk, query.dtype)
    in_hbm = pl.BlockSpec(memory_space=pltpu.HBM)
    first = pl.pallas_call(
        first_kernel,
        in_specs=[in_hbm] * 4,
        out_specs=in_hbm,
        out_shape=shape,
        scratch_shapes=[
            pltpu.VMEM(chunk, query.dtype),
            pltpu.SemaphoreType.DMA((4,)),
            pltpu.SemaphoreType.DMA,
        ],
        compiler_params=pltpu.CompilerParams(vmem_limit_bytes=LARGE_VMEM_BYTES),
        cost_estimate=pl.CostEstimate(flops=0, bytes_accessed=2 * rows * width, transcendentals=0),
        name="pack_first",
    )(*arrays)
    others = pl.pallas_call(
        functools.partial(pack_kernel, head_count - 1),
        in_specs=[in_hbm] * 5,
        out_specs=[in_hbm] * (head_count - 1),
        out_shape=[shape] * (head_count - 1),
        scratch_shapes=[
            pltpu.VMEM((4, rows, width), query.dtype),
            pltpu.VMEM((head_count - 1,) + chunk, query.dtype),
            pltpu.SemaphoreType.DMA((4,)),
            pltpu.SemaphoreType.DMA((head_count - 1,)),
        ],
        compiler_params=pltpu.CompilerParams(vmem_limit_bytes=LARGE_VMEM_BYTES),
        cost_estimate=pl.CostEstimate(
            flops=PACK_FLOPS, bytes_accessed=16 * rows * width, transcendentals=0
        ),
        name="pack_heads",
    )(*arrays, first)
    return dict(zip(ORDER[2:] + ORDER[:1], others)) | {ORDER[1]: first}


def choose_kernel(place_ref, gk_ref, gv_ref, own_ref, out_ref, held_ref, sems):
    head_size = out_ref.shape[2]
    columns = pl.ds(pl.multiple_of(place_ref[0] * head_size, head_size), head_size)
    copies = [
        pltpu.make_async_copy(
            ref.at[place_ref[1 + slot], :, columns],
            out_ref.at[2 * kind + slot],
            sems.at[2 * kind + slot],
        )
        for kind, ref in enumerate((gk_ref, gv_ref))
        for slot in range(2)
    ]
    copies.append(pltpu.make_async_copy(own_ref, held_ref, sems.at[4]))
    for copy in copies:
        copy.start()
    for copy in copies:
        copy.wait()


def choose(place, glob_keys, glob_values, own):
    head_size = own.shape[2]
    return pl.pallas_call(
        choose_kernel,
        in_specs=[pl.BlockSpec(memory_space=pltpu.SMEM)]
        + [pl.BlockSpec(memory_space=pltpu.HBM)] * 3,
        out_specs=in_vmem(2),
        out_shape=[
            jax.ShapeDtypeStruct((4, BLK, head_size), glob_keys.dtype),
            jax.ShapeDtypeStruct(own.shape, own.dtype),
        ],
        scratch_shapes=[pltpu.SemaphoreType.DMA((5,))],
        compiler_params=pltpu.CompilerParams(vmem_limit_bytes=SMALL_VMEM_BYTES),
        cost_estimate=pl.CostEstimate(
            flops=0, bytes_accessed=16 * BLK * head_size, transcendentals=0
        ),
        name="choose_blocks",
    )(place, glob_keys, glob_values, own)


def split_rows(block):
    empty = jnp.zeros((BLK, block.shape[1]), block.dtype)
    return jnp.concatenate(
        [
            jnp.concatenate([block[:BLK], empty], axis=0),
            jnp.concatenate([empty, block[BLK:]], axis=0),
        ],
        axis=1,
    )


def list_places(rand_ref, span, rand_count):
    return [
        [
            pl.multiple_of((rand_ref[(2 * span + half) * rand_count + slot] + 1) * BLK, BLK)
            for slot in range(rand_count)
        ]
        for half in range(2)
    ]


def gathered(pool, at, places, table_blocks):
    window = pool[at : at + 4 * BLK]
    lists = [
        jnp.concatenate([edge] + [pool[pl.ds(p, BLK)] for p in places[half]], axis=0)
        for half, edge in enumerate((window[:BLK], window[3 * BLK :]))
    ]
    both = jnp.concatenate([window[BLK : 3 * BLK]] + table_blocks, axis=0)
    return jnp.concatenate(lists, axis=1), both


def score_kernel(spans, place_ref, rand_ref, *refs):
    x_refs, g_ref = refs[:spans], refs[spans]
    q_all, k_all, o_all, p_all, ds_all = refs[spans + 1 : spans + 6]
    term_refs, v_all = refs[spans + 6 : spans + 8], refs[spans + 8]
    _, rows, head_size = x_refs[0].shape
    rand_count = rand_ref.shape[0] // (2 * spans)
    scaling = 1.0 / math.sqrt(head_size)
    me = place_ref[0]
    top = BLK + spans * rows
    for pool in (k_all, v_all):
        pool[:BLK] = jnp.zeros((BLK, head_size), pool.dtype)
        pool[top:] = jnp.zeros((BLK, head_size), pool.dtype)
    starts = [pl.multiple_of((me ^ flip) * rows, rows) for flip in ORDER]
    for at, ref in zip(starts, x_refs):
        q_all[pl.ds(at, rows)] = ref[0]
        k_all[pl.ds(pl.multiple_of(at + BLK, BLK), rows)] = ref[1]
        v_all[pl.ds(pl.multiple_of(at + BLK, BLK), rows)] = ref[2]
        o_all[pl.ds(at, rows)] = ref[3]
    gk = [g_ref[0], g_ref[1]]
    gv = [g_ref[2], g_ref[3]]
    own = (1 + rand_count) * BLK
    first = lax.broadcasted_iota(jnp.int32, (1, rows), 1) < BLK
    table_terms = [None, None]
    for group in range(0, spans, GROUP):
        members = range(group, min(group + GROUP, spans))
        made = []
        for span in members:
            at = span * rows
            q = q_all[at : at + rows]
            o = o_all[at : at + rows]
            places = list_places(rand_ref, span, rand_count)
            k_own, k_both = gathered(k_all, at, places, gk)
            v_own, v_both = gathered(v_all, at, places, gv)
            s_own = dot(k_own, split_rows(q), 1, 1) * scaling
            s_both = dot(k_both, q, 1, 1) * scaling
            g_own = dot(v_own, split_rows(o), 1, 1)
            g_both = dot(v_both, o, 1, 1)
            if span == 0 or span == spans - 1:
                row = lax.broadcasted_iota(jnp.int32, (own, 1), 0) < BLK
                outside = row & (first if span == 0 else jnp.logical_not(first))
                s_own = jnp.where(outside, MASKED, s_own)
            made.append((q, o, s_own, s_both, g_own, g_both))
        tops = [
            jnp.maximum(
                jnp.max(s_own, axis=0, keepdims=True), jnp.max(s_both, axis=0, keepdims=True)
            )
            for _, _, s_own, s_both, _, _ in made
        ]
        powers = [
            (jnp.exp(s_own - top_score), jnp.exp(s_both - top_score))
            for top_score, (_, _, s_own, s_both, _, _) in zip(tops, made)
        ]
        inverses = [
            1.0 / (jnp.sum(e_own, axis=0, keepdims=True) + jnp.sum(e_both, axis=0, keepdims=True))
            for e_own, e_both in powers
        ]
        weights = []
        for (e_own, e_both), inverse, (_, _, _, _, g_own, g_both) in zip(powers, inverses, made):
            p_own = e_own * inverse
            p_both = e_both * inverse
            pb_own = p_own.astype(jnp.bfloat16)
            pb_both = p_both.astype(jnp.bfloat16)
            row_dot = jnp.sum(
                pb_own.astype(jnp.float32) * g_own, axis=0, keepdims=True
            ) + jnp.sum(pb_both.astype(jnp.float32) * g_both, axis=0, keepdims=True)
            weights.append((p_own, p_both, pb_own, pb_both, row_dot))
        for span, (q, o, _, _, g_own, g_both), (p_own, p_both, pb_own, pb_both, row_dot) in zip(
            members, made, weights
        ):
            ds_own = (p_own * (g_own - row_dot) * scaling).astype(jnp.bfloat16)
            ds_both = (p_both * (g_both - row_dot) * scaling).astype(jnp.bfloat16)
            p_all[span, :own] = pb_own
            p_all[span, own:] = pb_both
            ds_all[span, :own] = ds_own
            ds_all[span, own:] = ds_both
            for kind, (weight, x) in enumerate(((ds_both, q), (pb_both, o))):
                term = dot(weight[2 * BLK :], x, 1, 0)
                so_far = table_terms[kind]
                table_terms[kind] = term if so_far is None else so_far + term
    mine = lax.axis_index("dp") % 2
    for flip, ref in enumerate(term_refs):
        ref[...] = jnp.zeros(ref.shape, ref.dtype)
        term = jnp.where(mine == flip, table_terms[0], table_terms[1]).astype(ref.dtype)
        for slot in range(2):
            at = pl.multiple_of(place_ref[1 + slot] * BLK, BLK)
            ref[pl.ds(at, BLK)] = term[slot * BLK : (slot + 1) * BLK]


def scores(chunks, chosen, place, rand_head, table_size):
    spans = len(chunks)
    _, rows, head_size = chunks[0].shape
    keys = 8 * BLK
    padded_rows = spans * rows + 2 * BLK
    keys_each = spans * rows * keys
    half = lambda *shape: jax.ShapeDtypeStruct(shape, jnp.bfloat16)
    outs = [
        half(spans * rows, head_size),
        half(padded_rows, head_size),
        half(spans * rows, head_size),
        half(spans, keys, rows),
        half(spans, keys, rows),
    ] + [half(table_size * BLK, head_size)] * 2
    results = pl.pallas_call(
        functools.partial(score_kernel, spans),
        in_specs=[pl.BlockSpec(memory_space=pltpu.SMEM)] * 2 + in_vmem(spans + 1),
        out_specs=in_vmem(len(outs)),
        out_shape=outs,
        scratch_shapes=[
            pltpu.VMEM((padded_rows, head_size), jnp.bfloat16),
        ],
        compiler_params=pltpu.CompilerParams(vmem_limit_bytes=VMEM_BYTES),
        cost_estimate=pl.CostEstimate(
            flops=4 * keys_each * head_size,
            bytes_accessed=8 * spans * rows * head_size,
            transcendentals=keys_each,
        ),
        name="scores",
    )(place, rand_head, *chunks, chosen)
    return results[:5], results[5:]


def added(left, right):
    return (left.astype(jnp.float32) + right.astype(jnp.float32)).astype(left.dtype)


def far_spans(spans, rand_count):
    return [(slot + 1) * spans // (rand_count + 1) for slot in range(rand_count)]


def grad_kernel(
    rand_ref, g_ref, q_all, k_all, o_all, p_all, ds_all, out_ref, made, sems
):
    spans, _, rows, head_size = made.shape
    rand_count = rand_ref.shape[0] // (2 * spans)
    own = (1 + rand_count) * BLK
    gk = [g_ref[0], g_ref[1]]
    offsets = far_spans(spans, rand_count)
    first = lax.broadcasted_iota(jnp.int32, (1, rows), 1) < BLK
    terms = []
    for span in range(spans):
        at = span * rows
        q = q_all[at : at + rows]
        o = o_all[at : at + rows]
        k_own, k_both = gathered(k_all, at, list_places(rand_ref, span, rand_count), gk)
        wide = dot(ds_all[span, :own], k_own, 0, 0)
        dq = jnp.concatenate([wide[:BLK, :head_size], wide[BLK:, head_size:]], axis=0)
        dq = dq + dot(ds_all[span, own:], k_both, 0, 0)
        made[span, 0] = dq.astype(made.dtype)
        keeps = [first]
        for slot, offset in enumerate(offsets):
            lower = [
                rand_ref[(2 * span + half) * rand_count + slot] == 2 * ((span + offset) % spans)
                for half in range(2)
            ]
            keeps.append((first & lower[0]) | (jnp.logical_not(first) & lower[1]))
        keeps = [jnp.where(keep, 1.0, 0.0).astype(made.dtype) for keep in keeps]
        pair = []
        for weights, x in ((ds_all, q), (p_all, o)):
            parts = [weights[span, own : own + 2 * BLK]]
            for place, keep in enumerate(keeps):
                block = weights[span, place * BLK : (place + 1) * BLK]
                lower = block * keep
                parts += [lower, block - lower]
            pair.append(dot(jnp.concatenate(parts, axis=0), x, 1, 0))
        terms.append(pair)
    copies = []
    for span in range(spans):
        for kind in range(2):
            part = lambda source, start, count: terms[source][kind][start : start + count]
            edges = [
                part(span - 1, 3 * BLK, BLK) if span > 0 else None,
                part(span + 1, 2 * BLK, BLK) if span < spans - 1 else None,
            ]
            edges = [jnp.zeros((BLK, head_size), jnp.float32) if e is None else e for e in edges]
            total = part(span, 0, 2 * BLK) + jnp.concatenate(edges, axis=0)
            for slot, offset in enumerate(offsets):
                total = total + part((span - offset) % spans, (4 + 2 * slot) * BLK, 2 * BLK)
            made[span, 1 + kind] = total.astype(made.dtype)
        copy = pltpu.make_async_copy(made.at[span], out_ref.at[span], sems.at[span])
        copy.start()
        copies.append(copy)
    for copy in copies:
        copy.wait()


def grads(rand_head, chosen, held):
    spans, keys, rows = held[3].shape
    head_size = held[1].shape[1]
    keys_each = spans * keys * rows
    shape = (spans, 3, rows, head_size)
    return pl.pallas_call(
        grad_kernel,
        in_specs=[pl.BlockSpec(memory_space=pltpu.SMEM)] + in_vmem(1 + len(held)),
        out_specs=pl.BlockSpec(memory_space=pltpu.HBM),
        out_shape=jax.ShapeDtypeStruct(shape, jnp.bfloat16),
        scratch_shapes=[
            pltpu.VMEM(shape, jnp.bfloat16),
            pltpu.SemaphoreType.DMA((spans,)),
        ],
        compiler_params=pltpu.CompilerParams(vmem_limit_bytes=VMEM_BYTES),
        cost_estimate=pl.CostEstimate(
            flops=6 * keys_each * head_size,
            bytes_accessed=8 * spans * rows * head_size,
            transcendentals=0,
        ),
        name="grads",
    )(rand_head, chosen, *held)


def early_kernel(sides, *refs):
    parts, out_ref = refs[:-1], refs[-1]
    head_size = parts[0].shape[2]
    head = lax.axis_index("ctx")
    share = lax.axis_index("dp") % 2
    for side, ref in zip(sides, parts):
        for place in range(ref.shape[0]):
            bits = side[place // len(COLUMN)]
            flip = COLUMN[place % len(COLUMN)]
            columns = pl.ds(pl.multiple_of((head ^ flip) * head_size, head_size), head_size)
            out_ref[share ^ bits, :, columns] = ref[place].astype(out_ref.dtype)


def early_table(head_count, sides, parts):
    _, rows, head_size = parts[0].shape
    shape = (2, rows, head_count * head_size)
    return pl.pallas_call(
        functools.partial(early_kernel, sides),
        in_specs=in_vmem(len(parts)),
        out_specs=pl.BlockSpec(memory_space=pltpu.VMEM),
        out_shape=jax.ShapeDtypeStruct(shape, jnp.float32),
        compiler_params=pltpu.CompilerParams(vmem_limit_bytes=VMEM_BYTES),
        cost_estimate=pl.CostEstimate(
            flops=EARLY_FLOPS, bytes_accessed=2**21, transcendentals=0
        ),
        name="early_table",
    )(*parts)


def finish_kernel(sides, *refs):
    count = len(sides)
    parts, x_ref = refs[:count], refs[count]
    grad_refs, table_ref = refs[count + 2 : count + 5], refs[count + 5]
    x_held, grad_made, table_made, x_sem, grad_sems, table_sems = refs[count + 6 :]
    heads, _, _, head_size = x_held.shape
    load = pltpu.make_async_copy(x_ref, x_held, x_sem)
    load.start()
    me = lax.axis_index("ctx")
    share = lax.axis_index("dp") % 2
    stores = []
    for side, ref in zip(sides, parts):
        for place in range(ref.shape[0]):
            at = len(stores)
            bits = side[place // len(COLUMN)]
            flip = COLUMN[place % len(COLUMN)] ^ 1
            columns = pl.ds(pl.multiple_of((me ^ flip) * head_size, head_size), head_size)
            table_made[at] = ref[place].astype(table_made.dtype)
            store = pltpu.make_async_copy(
                table_made.at[at], table_ref.at[share ^ bits, :, columns], table_sems.at[at]
            )
            store.start()
            stores.append(store)
    load.wait()
    for place, ref in enumerate(grad_refs):
        for head in range(heads):
            columns = slice(head * head_size, (head + 1) * head_size)
            grad_made[place, :, columns] = x_held[head, place]
        store = pltpu.make_async_copy(grad_made.at[place], ref.at[0], grad_sems.at[place])
        store.start()
        stores.append(store)
    for store in stores:
        store.wait()


def finish(x, table, sides, parts):
    heads, kinds, rows, head_size = x.shape
    blocks = sum(part.shape[0] for part in parts)
    in_hbm = pl.BlockSpec(memory_space=pltpu.HBM)
    grad = jax.ShapeDtypeStruct((1, rows, heads * head_size), x.dtype)
    return pl.pallas_call(
        functools.partial(finish_kernel, sides),
        in_specs=in_vmem(len(parts)) + [in_hbm] * 2,
        out_specs=[in_hbm] * (kinds + 1),
        out_shape=[grad] * kinds + [jax.ShapeDtypeStruct(table.shape, table.dtype)],
        scratch_shapes=[
            pltpu.VMEM(x.shape, x.dtype),
            pltpu.VMEM((kinds, rows, heads * head_size), x.dtype),
            pltpu.VMEM((blocks,) + parts[0].shape[1:], table.dtype),
            pltpu.SemaphoreType.DMA,
            pltpu.SemaphoreType.DMA((kinds,)),
            pltpu.SemaphoreType.DMA((blocks,)),
        ],
        input_output_aliases={len(parts) + 1: kinds},
        compiler_params=pltpu.CompilerParams(vmem_limit_bytes=FINISH_VMEM_BYTES),
        cost_estimate=pl.CostEstimate(flops=0, bytes_accessed=2**21, transcendentals=0),
        name="finish",
    )(*parts, x, table)


def flipped(array, axis, bits):
    if bits == 0:
        return array
    return lax.ppermute(array, axis, [(i, i ^ bits) for i in range(lax.axis_size(axis))])


def on_heads(query, key, value, dout, glob_keys, glob_values, glob_ids, rand_blocks):
    head_count, block_count, _ = rand_blocks.shape
    head_size = query.shape[2] // head_count
    table_size = glob_keys.shape[0]
    head = lax.axis_index("ctx").astype(jnp.int32)
    packed = pack(query, key, value, dout, head_count)
    chunks = [flipped(packed[flip], "ctx", flip) for flip in ORDER]
    place = jnp.concatenate([head[None], glob_ids[0]])
    rand_head = lax.dynamic_index_in_dim(rand_blocks, head, 0, keepdims=False).reshape(-1)
    rand_head = jnp.clip(rand_head, 0, block_count - 1)
    chosen, chunks[0] = choose(place, glob_keys, glob_values, packed[0])
    held, (kept, given) = scores(chunks, chosen, place, rand_head, table_size)
    given = flipped(given, "dp", 1)
    sent = grads(rand_head, chosen, held)
    given, sent = lax.optimization_barrier((given, sent))
    back = lax.all_to_all(sent, "ctx", 0, 0)
    chip = added(kept, given)
    column = jnp.stack([flipped(chip, "ctx", flip) for flip in COLUMN])
    even = added(column, flipped(column, "dp", 2))
    odd = flipped(even, "ctx", 1)
    beside_even = flipped(even, "dp", 1)
    beside_odd = flipped(odd, "dp", 1)
    d_table = early_table(head_count, ((0,), (1,)), [even, beside_even])
    d_query, d_key, d_value, d_table = finish(
        back, d_table, ((0,), (1,)), [odd, beside_odd]
    )
    return (d_query, d_key, d_value, d_table.reshape((2,) + glob_keys.shape))


def on_device(query, key, value, dout, glob_keys, glob_values, glob_ids, rand_blocks):
    head_count = rand_blocks.shape[0]
    one_head_each = lax.axis_size("ctx") == head_count == 8 and query.shape[1] == 2 * BLK
    if one_head_each and lax.axis_size("dp") == 4 and glob_keys.shape[0] % 2 == 0:
        plan = on_heads
    else:
        plan = on_ring
    return plan(query, key, value, dout, glob_keys, glob_values, glob_ids, rand_blocks)


def solution(mesh):
    placed = (
        P("dp", "ctx", None),
        P("dp", "ctx", None),
        P("dp", "ctx", None),
        P("dp", "ctx", None),
        P(),
        P(),
        P("dp", None),
        P(),
    )
    return jax.shard_map(
        on_device,
        mesh=mesh,
        in_specs=placed,
        out_specs=(P("dp", "ctx", None), P("dp", "ctx", None), P("dp", "ctx", None), P()),
        check_vma=False,
    )
```

```python
import functools
import math

import jax
import jax.numpy as jnp
from jax import lax
from jax.experimental import pallas as pl
from jax.experimental.pallas import tpu as pltpu
from jax.sharding import PartitionSpec as P

BLK = 64


def passed_along(shard, axis, by):
    length = lax.axis_size(axis)
    return lax.ppermute(shard, axis, [(i, (i + by) % length) for i in range(length)])


def padded(cells, sides, width):
    for axis, dim in sides:
        count = lax.axis_size(axis)
        ends = count - 1
        head = lax.slice_in_dim(cells, 0, width, axis=dim)
        tail = lax.slice_in_dim(cells, cells.shape[dim] - width, cells.shape[dim], axis=dim)
        cells = jnp.concatenate(
            [
                lax.ppermute(tail, axis, [(i, (i + 1) % count) for i in range(ends)]),
                cells,
                lax.ppermute(head, axis, [((i + 1) % count, i) for i in range(ends)]),
            ],
            axis=dim,
        )
    return cells


def passed_along_2(value, axis, steps):
    count = lax.axis_size(axis)
    leading, last = (max(0, -steps), min(count, count - steps))
    return lax.ppermute(value, axis, [(source, source + steps) for source in range(leading, last)])


def attend(
    q_head,
    o_grad,
    k_head,
    v_head,
    gk_head,
    gv_head,
    key_index,
    key_valid,
    scatter_count,
    rand_count,
):
    q_blocks = q_head.shape[0]
    head_size = q_head.shape[2]
    scaling = 1.0 / math.sqrt(head_size)
    local_lists = key_index.shape[1]
    keys_all = jnp.concatenate(
        [
            jnp.take(k_head, key_index, axis=0),
            jnp.broadcast_to(gk_head[None], (q_blocks,) + gk_head.shape),
        ],
        axis=1,
    ).reshape(q_blocks, -1, head_size)
    values_all = jnp.concatenate(
        [
            jnp.take(v_head, key_index, axis=0),
            jnp.broadcast_to(gv_head[None], (q_blocks,) + gv_head.shape),
        ],
        axis=1,
    ).reshape(q_blocks, -1, head_size)
    keep_mask = jnp.repeat(
        jnp.concatenate([key_valid, jnp.ones((q_blocks, 2), dtype=bool)], axis=1), BLK, axis=1
    )
    scores = (
        jnp.einsum("nqd,nkd->nqk", q_head, keys_all, preferred_element_type=jnp.float32) * scaling
    )
    scores = jnp.where(keep_mask[:, None, :], scores, -1e30)
    row_max = jnp.max(scores, axis=-1, keepdims=True)
    exp_scores = jnp.exp(scores - row_max)
    weights = exp_scores / jnp.sum(exp_scores, axis=-1, keepdims=True)
    weights_b = weights.astype(jnp.bfloat16)
    attn_out = jnp.einsum("nqk,nkd->nqd", weights_b, values_all, preferred_element_type=jnp.float32)
    row_dot = jnp.sum(o_grad.astype(jnp.float32) * attn_out, axis=-1, keepdims=True)
    prob_grad = jnp.einsum("nqd,nkd->nqk", o_grad, values_all, preferred_element_type=jnp.float32)
    score_grad = (weights * (prob_grad - row_dot) * scaling).astype(jnp.bfloat16)
    q_grad = jnp.einsum("nqk,nkd->nqd", score_grad, keys_all, preferred_element_type=jnp.float32)
    k_grad = jnp.einsum(
        "nqk,nqd->nkd", score_grad, q_head, preferred_element_type=jnp.float32
    ).reshape(q_blocks, local_lists + 2, BLK, head_size)
    v_grad = jnp.einsum(
        "nqk,nqd->nkd", weights_b, o_grad, preferred_element_type=jnp.float32
    ).reshape(q_blocks, local_lists + 2, BLK, head_size)
    flat_index = key_index.reshape(-1)
    k_local = (
        jnp.zeros(k_head.shape, jnp.float32)
        .at[flat_index]
        .add(k_grad[:, :scatter_count].reshape(-1, BLK, head_size))
    )
    v_local = (
        jnp.zeros(v_head.shape, jnp.float32)
        .at[flat_index]
        .add(v_grad[:, :scatter_count].reshape(-1, BLK, head_size))
    )
    grad_tiles = score_grad.reshape(q_blocks, BLK, local_lists + 2, BLK)[
        :, :, 3 : 3 + rand_count
    ].transpose(0, 2, 1, 3)
    prob_tiles = weights_b.reshape(q_blocks, BLK, local_lists + 2, BLK)[
        :, :, 3 : 3 + rand_count
    ].transpose(0, 2, 1, 3)
    return (
        q_grad,
        k_local,
        v_local,
        k_grad[:, local_lists:],
        v_grad[:, local_lists:],
        grad_tiles,
        prob_tiles,
    )


def by_heads(row_array, head_count):
    block_total = row_array.shape[0] // BLK
    return row_array.reshape(block_total, BLK, head_count, -1).transpose(2, 0, 1, 3)


def from_heads(head_array):
    head_count = head_array.shape[0]
    head_size = head_array.shape[3]
    return head_array.transpose(1, 2, 0, 3).reshape(-1, head_count * head_size)


def fetch_far(key_value, offset):
    return passed_along(key_value, "ctx", -offset)


def return_far(partials, offset):
    return passed_along(partials, "ctx", offset)


def on_ring(query, key, value, dout, glob_keys, glob_values, glob_ids, rand_blocks):
    row_count = query.shape[1]
    head_count = rand_blocks.shape[0]
    rand_count = rand_blocks.shape[2]
    head_size = query.shape[2] // head_count
    per_device = row_count // BLK
    span_count = lax.axis_size("ctx")
    device_pos = lax.axis_index("ctx")
    block_count = per_device * span_count
    offsets = [(slot + 1) * span_count // (rand_count + 1) for slot in range(rand_count)]
    key_value = jnp.stack([key[0], value[0]])
    extended = padded(key_value, (("ctx", 1),), row_count)
    far_spans = [fetch_far(key_value, offset) for offset in offsets]
    k_rows = jnp.concatenate([extended[0]] + [span[0] for span in far_spans], axis=0)
    v_rows = jnp.concatenate([extended[1]] + [span[1] for span in far_spans], axis=0)
    first_block = device_pos * per_device
    key_base = first_block - per_device
    query_ids = first_block + jnp.arange(per_device, dtype=jnp.int32)
    window = query_ids[:, None] + jnp.arange(-1, 2, dtype=jnp.int32)[None, :]
    key_valid = jnp.concatenate(
        [(window >= 0) & (window < block_count), jnp.ones((per_device, rand_count), dtype=bool)],
        axis=1,
    )
    window_local = jnp.clip(window - key_base, 0, 3 * per_device - 1)
    rand_rows = lax.dynamic_slice_in_dim(rand_blocks, first_block, per_device, 1)
    offset_table = jnp.array(offsets, dtype=jnp.int32)
    far_starts = (device_pos + offset_table) % span_count * per_device
    slot_base = (3 + jnp.arange(rand_count, dtype=jnp.int32)) * per_device
    rand_local = rand_rows - far_starts[None, None, :] + slot_base[None, None, :]
    all_lists = jnp.concatenate(
        [jnp.broadcast_to(window_local[None], (head_count,) + window_local.shape), rand_local],
        axis=2,
    )
    key_index = jnp.clip(all_lists, 0, (3 + rand_count) * per_device - 1)
    chosen = glob_ids[0]
    gk_heads = by_heads(jnp.take(glob_keys, chosen, axis=0).reshape(2 * BLK, -1), head_count)
    gv_heads = by_heads(jnp.take(glob_values, chosen, axis=0).reshape(2 * BLK, -1), head_count)
    scatter_count = 3 + rand_count

    def per_head(pieces):
        q_head, o_grad, k_head, v_head, gk_head, gv_head, index_head = pieces
        return attend(
            q_head,
            o_grad,
            k_head,
            v_head,
            gk_head,
            gv_head,
            index_head,
            key_valid,
            scatter_count,
            rand_count,
        )

    results = lax.map(
        per_head,
        (
            by_heads(query[0], head_count),
            by_heads(dout[0], head_count),
            by_heads(k_rows, head_count),
            by_heads(v_rows, head_count),
            gk_heads,
            gv_heads,
            key_index,
        ),
    )
    q_grad = results[0]
    kv_grads = jnp.stack([results[1], results[2]])
    lower_part = kv_grads[:, :, :per_device]
    upper_part = kv_grads[:, :, 2 * per_device : 3 * per_device]
    from_below = passed_along_2(upper_part.astype(jnp.bfloat16), "ctx", 1).astype(upper_part.dtype)
    from_above = passed_along_2(lower_part.astype(jnp.bfloat16), "ctx", -1).astype(lower_part.dtype)
    own_grads = kv_grads[:, :, per_device : 2 * per_device] + from_below + from_above
    for slot in range(rand_count):
        start = (3 + slot) * per_device
        own_grads = own_grads + return_far(
            kv_grads[:, :, start : start + per_device], offsets[slot]
        )
    global_part = jnp.stack([jnp.sum(results[3], axis=1), jnp.sum(results[4], axis=1)])
    global_part = global_part.transpose(0, 2, 3, 1, 4).reshape(2, 2, BLK, head_count * head_size)
    one_hot = (chosen[:, None] == jnp.arange(glob_keys.shape[0], dtype=jnp.int32)[None, :]).astype(
        jnp.float32
    )
    table_term = jnp.einsum("sg,ksbd->kgbd", one_hot, global_part, precision=lax.Precision.HIGHEST)
    table_grad = lax.psum(table_term, ("ctx", "dp"))
    d_query = from_heads(q_grad).astype(jnp.bfloat16)[None]
    d_key = from_heads(own_grads[0]).astype(jnp.bfloat16)[None]
    d_value = from_heads(own_grads[1]).astype(jnp.bfloat16)[None]
    return (d_query, d_key, d_value, table_grad)


VMEM_BYTES = 24 * 1024 * 1024
SMALL_VMEM_BYTES = 4 * 1024 * 1024
LARGE_VMEM_BYTES = 60 * 1024 * 1024
FINISH_VMEM_BYTES = 24 * 1024 * 1024
MASKED = -1e30
FIRST_BYTES = 60 * 1024 * 1024
PACK_FLOPS = 2 * 10**9
EARLY_FLOPS = 5 * 10**9
GROUP = 8
ORDER = (0, 4, 2, 5, 3, 6, 7, 1)
COLUMN = (0, 2, 4, 6)


def dot(left, right, left_dim, right_dim):
    dims = (((left_dim,), (right_dim,)), ((), ()))
    return lax.dot_general(left, right, dims, preferred_element_type=jnp.float32)


def in_vmem(count):
    return [pl.BlockSpec(memory_space=pltpu.VMEM)] * count


def first_kernel(q_ref, k_ref, v_ref, o_ref, out_ref, sems):
    head_size = out_ref.shape[2]
    at = pl.multiple_of((lax.axis_index("ctx") ^ ORDER[1]) * head_size, head_size)
    copies = [
        pltpu.make_async_copy(
            ref.at[0, :, pl.ds(at, head_size)], out_ref.at[place], sems.at[place]
        )
        for place, ref in enumerate((q_ref, k_ref, v_ref, o_ref))
    ]
    for copy in copies:
        copy.start()
    for copy in copies:
        copy.wait()


def pack_kernel(count, *refs):
    ins, outs = refs[:4], refs[5 : 5 + count]
    held, made, in_sems, out_sems = refs[5 + count :]
    head_size = made.shape[3]
    me = lax.axis_index("ctx")
    loads = [
        pltpu.make_async_copy(ref.at[0], held.at[place], in_sems.at[place])
        for place, ref in enumerate(ins)
    ]
    for load in loads:
        load.start()
    for load in loads:
        load.wait()
    stores = []
    for place, flip in enumerate(ORDER[2:] + ORDER[:1]):
        at = pl.multiple_of((me ^ flip) * head_size, head_size)
        made[place] = held[:, :, pl.ds(at, head_size)]
        store = pltpu.make_async_copy(made.at[place], outs[place], out_sems.at[place])
        store.start()
        stores.append(store)
    for store in stores:
        store.wait()


def pack(query, key, value, dout, head_count):
    _, rows, width = query.shape
    arrays = (query, key, value, dout)
    chunk = (4, rows, width // head_count)
    shape = jax.ShapeDtypeStruct(chunk, query.dtype)
    in_hbm = pl.BlockSpec(memory_space=pltpu.HBM)
    first = pl.pallas_call(
        first_kernel,
        in_specs=[in_hbm] * 4,
        out_specs=pl.BlockSpec(memory_space=pltpu.VMEM),
        out_shape=shape,
        scratch_shapes=[pltpu.SemaphoreType.DMA((4,))],
        compiler_params=pltpu.CompilerParams(vmem_limit_bytes=FIRST_BYTES),
        cost_estimate=pl.CostEstimate(flops=0, bytes_accessed=2 * rows * width, transcendentals=0),
        name="pack_first",
    )(*arrays)
    others = pl.pallas_call(
        functools.partial(pack_kernel, head_count - 1),
        in_specs=[in_hbm] * 5,
        out_specs=[in_hbm] * (head_count - 1),
        out_shape=[shape] * (head_count - 1),
        scratch_shapes=[
            pltpu.VMEM((4, rows, width), query.dtype),
            pltpu.VMEM((head_count - 1,) + chunk, query.dtype),
            pltpu.SemaphoreType.DMA((4,)),
            pltpu.SemaphoreType.DMA((head_count - 1,)),
        ],
        compiler_params=pltpu.CompilerParams(vmem_limit_bytes=LARGE_VMEM_BYTES),
        cost_estimate=pl.CostEstimate(
            flops=PACK_FLOPS, bytes_accessed=16 * rows * width, transcendentals=0
        ),
        name="pack_heads",
    )(*arrays, first)
    return dict(zip(ORDER[2:] + ORDER[:1], others)) | {ORDER[1]: first}


def choose_kernel(place_ref, gk_ref, gv_ref, own_ref, out_ref, held_ref, sems):
    head_size = out_ref.shape[2]
    columns = pl.ds(pl.multiple_of(place_ref[0] * head_size, head_size), head_size)
    copies = [
        pltpu.make_async_copy(
            ref.at[place_ref[1 + slot], :, columns],
            out_ref.at[2 * kind + slot],
            sems.at[2 * kind + slot],
        )
        for kind, ref in enumerate((gk_ref, gv_ref))
        for slot in range(2)
    ]
    copies.append(pltpu.make_async_copy(own_ref, held_ref, sems.at[4]))
    for copy in copies:
        copy.start()
    for copy in copies:
        copy.wait()


def choose(place, glob_keys, glob_values, own):
    head_size = own.shape[2]
    return pl.pallas_call(
        choose_kernel,
        in_specs=[pl.BlockSpec(memory_space=pltpu.SMEM)]
        + [pl.BlockSpec(memory_space=pltpu.HBM)] * 3,
        out_specs=in_vmem(2),
        out_shape=[
            jax.ShapeDtypeStruct((4, BLK, head_size), glob_keys.dtype),
            jax.ShapeDtypeStruct(own.shape, own.dtype),
        ],
        scratch_shapes=[pltpu.SemaphoreType.DMA((5,))],
        compiler_params=pltpu.CompilerParams(vmem_limit_bytes=SMALL_VMEM_BYTES),
        cost_estimate=pl.CostEstimate(
            flops=0, bytes_accessed=16 * BLK * head_size, transcendentals=0
        ),
        name="choose_blocks",
    )(place, glob_keys, glob_values, own)


def split_rows(block):
    empty = jnp.zeros((BLK, block.shape[1]), block.dtype)
    return jnp.concatenate(
        [
            jnp.concatenate([block[:BLK], empty], axis=0),
            jnp.concatenate([empty, block[BLK:]], axis=0),
        ],
        axis=1,
    )


def list_places(rand_ref, span, rand_count):
    return [
        [
            pl.multiple_of((rand_ref[(2 * span + half) * rand_count + slot] + 1) * BLK, BLK)
            for slot in range(rand_count)
        ]
        for half in range(2)
    ]


def gathered(pool, at, places, table_blocks):
    window = pool[at : at + 4 * BLK]
    lists = [
        jnp.concatenate([edge] + [pool[pl.ds(p, BLK)] for p in places[half]], axis=0)
        for half, edge in enumerate((window[:BLK], window[3 * BLK :]))
    ]
    both = jnp.concatenate([window[BLK : 3 * BLK]] + table_blocks, axis=0)
    return jnp.concatenate(lists, axis=1), both


def score_kernel(spans, place_ref, rand_ref, *refs):
    x_refs, g_ref = refs[:spans], refs[spans]
    q_all, k_all, o_all, p_all, ds_all = refs[spans + 1 : spans + 6]
    term_refs, v_all = refs[spans + 6 : spans + 8], refs[spans + 8]
    _, rows, head_size = x_refs[0].shape
    rand_count = rand_ref.shape[0] // (2 * spans)
    scaling = 1.0 / math.sqrt(head_size)
    rate = scaling * math.log2(math.e)
    me = place_ref[0]
    top = BLK + spans * rows
    for pool in (k_all, v_all):
        pool[:BLK] = jnp.zeros((BLK, head_size), pool.dtype)
        pool[top:] = jnp.zeros((BLK, head_size), pool.dtype)
    starts = [pl.multiple_of((me ^ flip) * rows, rows) for flip in ORDER]
    for at, ref in zip(starts, x_refs):
        q_all[pl.ds(at, rows)] = ref[0]
        k_all[pl.ds(pl.multiple_of(at + BLK, BLK), rows)] = ref[1]
        v_all[pl.ds(pl.multiple_of(at + BLK, BLK), rows)] = ref[2]
        o_all[pl.ds(at, rows)] = ref[3]
    gk = [g_ref[0], g_ref[1]]
    gv = [g_ref[2], g_ref[3]]
    own = (1 + rand_count) * BLK
    first = lax.broadcasted_iota(jnp.int32, (1, rows), 1) < BLK
    table_terms = [None, None]
    for group in range(0, spans, GROUP):
        members = range(group, min(group + GROUP, spans))
        made = []
        for span in members:
            at = span * rows
            q = q_all[at : at + rows]
            o = o_all[at : at + rows]
            places = list_places(rand_ref, span, rand_count)
            k_own, k_both = gathered(k_all, at, places, gk)
            s_own = dot(k_own, split_rows(q), 1, 1)
            s_both = dot(k_both, q, 1, 1)
            if span == 0 or span == spans - 1:
                row = lax.broadcasted_iota(jnp.int32, (own, 1), 0) < BLK
                outside = row & (first if span == 0 else jnp.logical_not(first))
                s_own = jnp.where(outside, MASKED / scaling, s_own)
            made.append((q, o, s_own, s_both))
        tops = [
            jnp.maximum(
                jnp.max(s_own, axis=0, keepdims=True), jnp.max(s_both, axis=0, keepdims=True)
            )
            for _, _, s_own, s_both in made
        ]
        powers = []
        values = []
        for span, top_score, (q, o, s_own, s_both) in zip(members, tops, made):
            places = list_places(rand_ref, span, rand_count)
            v_own, v_both = gathered(v_all, span * rows, places, gv)
            values.append((dot(v_own, split_rows(o), 1, 1), dot(v_both, o, 1, 1)))
            powers.append(
                (jnp.exp2((s_own - top_score) * rate), jnp.exp2((s_both - top_score) * rate))
            )
        inverses = [
            1.0 / (jnp.sum(e_own, axis=0, keepdims=True) + jnp.sum(e_both, axis=0, keepdims=True))
            for e_own, e_both in powers
        ]
        for span, (e_own, e_both), inverse, (q, o, _, _), (g_own, g_both) in zip(
            members, powers, inverses, made, values
        ):
            p_own = e_own * inverse
            p_both = e_both * inverse
            pb_own = p_own.astype(jnp.bfloat16)
            pb_both = p_both.astype(jnp.bfloat16)
            row_dot = jnp.sum(
                pb_own.astype(jnp.float32) * g_own, axis=0, keepdims=True
            ) + jnp.sum(pb_both.astype(jnp.float32) * g_both, axis=0, keepdims=True)
            ds_own = (p_own * (g_own - row_dot) * scaling).astype(jnp.bfloat16)
            ds_both = (p_both * (g_both - row_dot) * scaling).astype(jnp.bfloat16)
            p_all[span, :own] = pb_own
            p_all[span, own:] = pb_both
            ds_all[span, :own] = ds_own
            ds_all[span, own:] = ds_both
            for kind, (weight, x) in enumerate(((ds_both, q), (pb_both, o))):
                term = dot(weight[2 * BLK :], x, 1, 0)
                so_far = table_terms[kind]
                table_terms[kind] = term if so_far is None else so_far + term
    mine = lax.axis_index("dp") % 2
    for flip, ref in enumerate(term_refs):
        ref[...] = jnp.zeros(ref.shape, ref.dtype)
        term = jnp.where(mine == flip, table_terms[0], table_terms[1]).astype(ref.dtype)
        for slot in range(2):
            at = pl.multiple_of(place_ref[1 + slot] * BLK, BLK)
            ref[pl.ds(at, BLK)] = term[slot * BLK : (slot + 1) * BLK]


def scores(chunks, chosen, place, rand_head, table_size):
    spans = len(chunks)
    _, rows, head_size = chunks[0].shape
    keys = 8 * BLK
    padded_rows = spans * rows + 2 * BLK
    keys_each = spans * rows * keys
    half = lambda *shape: jax.ShapeDtypeStruct(shape, jnp.bfloat16)
    outs = [
        half(spans * rows, head_size),
        half(padded_rows, head_size),
        half(spans * rows, head_size),
        half(spans, keys, rows),
        half(spans, keys, rows),
    ] + [half(table_size * BLK, head_size)] * 2
    results = pl.pallas_call(
        functools.partial(score_kernel, spans),
        in_specs=[pl.BlockSpec(memory_space=pltpu.SMEM)] * 2 + in_vmem(spans + 1),
        out_specs=in_vmem(len(outs)),
        out_shape=outs,
        scratch_shapes=[
            pltpu.VMEM((padded_rows, head_size), jnp.bfloat16),
        ],
        compiler_params=pltpu.CompilerParams(vmem_limit_bytes=VMEM_BYTES),
        cost_estimate=pl.CostEstimate(
            flops=4 * keys_each * head_size,
            bytes_accessed=8 * spans * rows * head_size,
            transcendentals=keys_each,
        ),
        name="scores",
    )(place, rand_head, *chunks, chosen)
    return results[:5], results[5:]


def added(left, right):
    return (left.astype(jnp.float32) + right.astype(jnp.float32)).astype(left.dtype)


def far_spans(spans, rand_count):
    return [(slot + 1) * spans // (rand_count + 1) for slot in range(rand_count)]


def grad_kernel(
    rand_ref, g_ref, q_all, k_all, o_all, p_all, ds_all, out_ref, made, sems
):
    spans, _, rows, head_size = made.shape
    rand_count = rand_ref.shape[0] // (2 * spans)
    own = (1 + rand_count) * BLK
    gk = [g_ref[0], g_ref[1]]
    offsets = far_spans(spans, rand_count)
    first = lax.broadcasted_iota(jnp.int32, (1, rows), 1) < BLK
    terms = []
    for span in range(spans):
        at = span * rows
        q = q_all[at : at + rows]
        o = o_all[at : at + rows]
        keeps = [first]
        for slot, offset in enumerate(offsets):
            lower = [
                rand_ref[(2 * span + half) * rand_count + slot] == 2 * ((span + offset) % spans)
                for half in range(2)
            ]
            keeps.append((first & lower[0]) | (jnp.logical_not(first) & lower[1]))
        keeps = [jnp.where(keep, 1.0, 0.0).astype(made.dtype) for keep in keeps]
        pair = []
        for weights, x in ((ds_all, q), (p_all, o)):
            parts = [weights[span, own : own + 2 * BLK]]
            for place, keep in enumerate(keeps):
                block = weights[span, place * BLK : (place + 1) * BLK]
                lower = block * keep
                parts += [lower, block - lower]
            pair.append(dot(jnp.concatenate(parts, axis=0), x, 1, 0))
        terms.append(pair)
    copies = []
    for span in range(spans):
        at = span * rows
        k_own, k_both = gathered(k_all, at, list_places(rand_ref, span, rand_count), gk)
        wide = dot(ds_all[span, :own], k_own, 0, 0)
        dq = jnp.concatenate([wide[:BLK, :head_size], wide[BLK:, head_size:]], axis=0)
        dq = dq + dot(ds_all[span, own:], k_both, 0, 0)
        made[span, 0] = dq.astype(made.dtype)
        for kind in range(2):
            part = lambda source, start, count: terms[source][kind][start : start + count]
            edges = [
                part(span - 1, 3 * BLK, BLK) if span > 0 else None,
                part(span + 1, 2 * BLK, BLK) if span < spans - 1 else None,
            ]
            edges = [jnp.zeros((BLK, head_size), jnp.float32) if e is None else e for e in edges]
            total = part(span, 0, 2 * BLK) + jnp.concatenate(edges, axis=0)
            for slot, offset in enumerate(offsets):
                total = total + part((span - offset) % spans, (4 + 2 * slot) * BLK, 2 * BLK)
            made[span, 1 + kind] = total.astype(made.dtype)
        copy = pltpu.make_async_copy(made.at[span], out_ref.at[span], sems.at[span])
        copy.start()
        copies.append(copy)
    for copy in copies:
        copy.wait()


def grads(rand_head, chosen, held):
    spans, keys, rows = held[3].shape
    head_size = held[1].shape[1]
    keys_each = spans * keys * rows
    shape = (spans, 3, rows, head_size)
    return pl.pallas_call(
        grad_kernel,
        in_specs=[pl.BlockSpec(memory_space=pltpu.SMEM)] + in_vmem(1 + len(held)),
        out_specs=pl.BlockSpec(memory_space=pltpu.HBM),
        out_shape=jax.ShapeDtypeStruct(shape, jnp.bfloat16),
        scratch_shapes=[
            pltpu.VMEM(shape, jnp.bfloat16),
            pltpu.SemaphoreType.DMA((spans,)),
        ],
        compiler_params=pltpu.CompilerParams(vmem_limit_bytes=VMEM_BYTES),
        cost_estimate=pl.CostEstimate(
            flops=6 * keys_each * head_size,
            bytes_accessed=8 * spans * rows * head_size,
            transcendentals=0,
        ),
        name="grads",
    )(rand_head, chosen, *held)


def early_kernel(sides, *refs):
    parts, out_ref = refs[:-1], refs[-1]
    head_size = parts[0].shape[2]
    head = lax.axis_index("ctx")
    share = lax.axis_index("dp") % 2
    for side, ref in zip(sides, parts):
        for place in range(ref.shape[0]):
            bits = side[place // len(COLUMN)]
            flip = COLUMN[place % len(COLUMN)]
            columns = pl.ds(pl.multiple_of((head ^ flip) * head_size, head_size), head_size)
            out_ref[share ^ bits, :, columns] = ref[place].astype(out_ref.dtype)


def early_table(head_count, sides, parts):
    _, rows, head_size = parts[0].shape
    shape = (2, rows, head_count * head_size)
    return pl.pallas_call(
        functools.partial(early_kernel, sides),
        in_specs=in_vmem(len(parts)),
        out_specs=pl.BlockSpec(memory_space=pltpu.VMEM),
        out_shape=jax.ShapeDtypeStruct(shape, jnp.float32),
        compiler_params=pltpu.CompilerParams(vmem_limit_bytes=VMEM_BYTES),
        cost_estimate=pl.CostEstimate(
            flops=EARLY_FLOPS, bytes_accessed=2**21, transcendentals=0
        ),
        name="early_table",
    )(*parts)


def finish_kernel(sides, *refs):
    count = len(sides)
    parts, x_ref = refs[:count], refs[count]
    grad_refs, table_ref = refs[count + 2 : count + 5], refs[count + 5]
    x_held, grad_made, table_made, x_sem, grad_sems, table_sems = refs[count + 6 :]
    heads, _, _, head_size = x_held.shape
    load = pltpu.make_async_copy(x_ref, x_held, x_sem)
    load.start()
    me = lax.axis_index("ctx")
    share = lax.axis_index("dp") % 2
    stores = []
    for side, ref in zip(sides, parts):
        for place in range(ref.shape[0]):
            at = len(stores)
            bits = side[place // len(COLUMN)]
            flip = COLUMN[place % len(COLUMN)] ^ 1
            columns = pl.ds(pl.multiple_of((me ^ flip) * head_size, head_size), head_size)
            table_made[at] = ref[place].astype(table_made.dtype)
            store = pltpu.make_async_copy(
                table_made.at[at], table_ref.at[share ^ bits, :, columns], table_sems.at[at]
            )
            store.start()
            stores.append(store)
    load.wait()
    for place, ref in enumerate(grad_refs):
        for head in range(heads):
            columns = slice(head * head_size, (head + 1) * head_size)
            grad_made[place, :, columns] = x_held[head, place]
        store = pltpu.make_async_copy(grad_made.at[place], ref.at[0], grad_sems.at[place])
        store.start()
        stores.append(store)
    for store in stores:
        store.wait()


def finish(x, table, sides, parts):
    heads, kinds, rows, head_size = x.shape
    blocks = sum(part.shape[0] for part in parts)
    in_hbm = pl.BlockSpec(memory_space=pltpu.HBM)
    grad = jax.ShapeDtypeStruct((1, rows, heads * head_size), x.dtype)
    return pl.pallas_call(
        functools.partial(finish_kernel, sides),
        in_specs=in_vmem(len(parts)) + [in_hbm] * 2,
        out_specs=[in_hbm] * (kinds + 1),
        out_shape=[grad] * kinds + [jax.ShapeDtypeStruct(table.shape, table.dtype)],
        scratch_shapes=[
            pltpu.VMEM(x.shape, x.dtype),
            pltpu.VMEM((kinds, rows, heads * head_size), x.dtype),
            pltpu.VMEM((blocks,) + parts[0].shape[1:], table.dtype),
            pltpu.SemaphoreType.DMA,
            pltpu.SemaphoreType.DMA((kinds,)),
            pltpu.SemaphoreType.DMA((blocks,)),
        ],
        input_output_aliases={len(parts) + 1: kinds},
        compiler_params=pltpu.CompilerParams(vmem_limit_bytes=FINISH_VMEM_BYTES),
        cost_estimate=pl.CostEstimate(flops=0, bytes_accessed=2**21, transcendentals=0),
        name="finish",
    )(*parts, x, table)


def flipped(array, axis, bits):
    if bits == 0:
        return array
    return lax.ppermute(array, axis, [(i, i ^ bits) for i in range(lax.axis_size(axis))])


def on_heads(query, key, value, dout, glob_keys, glob_values, glob_ids, rand_blocks):
    head_count, block_count, _ = rand_blocks.shape
    head_size = query.shape[2] // head_count
    table_size = glob_keys.shape[0]
    head = lax.axis_index("ctx").astype(jnp.int32)
    packed = pack(query, key, value, dout, head_count)
    chunks = [flipped(packed[flip], "ctx", flip) for flip in ORDER]
    place = jnp.concatenate([head[None], glob_ids[0]])
    rand_head = lax.dynamic_index_in_dim(rand_blocks, head, 0, keepdims=False).reshape(-1)
    rand_head = jnp.clip(rand_head, 0, block_count - 1)
    chosen, chunks[0] = choose(place, glob_keys, glob_values, packed[0])
    held, (kept, given) = scores(chunks, chosen, place, rand_head, table_size)
    given = flipped(given, "dp", 1)
    sent = grads(rand_head, chosen, held)
    given, sent = lax.optimization_barrier((given, sent))
    back = lax.all_to_all(sent, "ctx", 0, 0)
    chip = added(kept, given)
    column = jnp.stack([flipped(chip, "ctx", flip) for flip in COLUMN])
    even = added(column, flipped(column, "dp", 2))
    odd = flipped(even, "ctx", 1)
    beside_even = flipped(even, "dp", 1)
    beside_odd = flipped(odd, "dp", 1)
    d_table = early_table(head_count, ((0,), (1,)), [even, beside_even])
    d_query, d_key, d_value, d_table = finish(
        back, d_table, ((0,), (1,)), [odd, beside_odd]
    )
    return (d_query, d_key, d_value, d_table.reshape((2,) + glob_keys.shape))


def on_device(query, key, value, dout, glob_keys, glob_values, glob_ids, rand_blocks):
    head_count = rand_blocks.shape[0]
    one_head_each = lax.axis_size("ctx") == head_count == 8 and query.shape[1] == 2 * BLK
    if one_head_each and lax.axis_size("dp") == 4 and glob_keys.shape[0] % 2 == 0:
        plan = on_heads
    else:
        plan = on_ring
    return plan(query, key, value, dout, glob_keys, glob_values, glob_ids, rand_blocks)


def solution(mesh):
    placed = (
        P("dp", "ctx", None),
        P("dp", "ctx", None),
        P("dp", "ctx", None),
        P("dp", "ctx", None),
        P(),
        P(),
        P("dp", None),
        P(),
    )
    return jax.shard_map(
        on_device,
        mesh=mesh,
        in_specs=placed,
        out_specs=(P("dp", "ctx", None), P("dp", "ctx", None), P("dp", "ctx", None), P()),
        check_vma=False,
    )
```

```python
import functools
import math

import jax
import jax.numpy as jnp
from jax import lax
from jax.experimental import pallas as pl
from jax.experimental.pallas import tpu as pltpu
from jax.sharding import PartitionSpec as P

BLK = 64


def passed_along(shard, axis, by):
    length = lax.axis_size(axis)
    return lax.ppermute(shard, axis, [(i, (i + by) % length) for i in range(length)])


def padded(cells, sides, width):
    for axis, dim in sides:
        count = lax.axis_size(axis)
        ends = count - 1
        head = lax.slice_in_dim(cells, 0, width, axis=dim)
        tail = lax.slice_in_dim(cells, cells.shape[dim] - width, cells.shape[dim], axis=dim)
        cells = jnp.concatenate(
            [
                lax.ppermute(tail, axis, [(i, (i + 1) % count) for i in range(ends)]),
                cells,
                lax.ppermute(head, axis, [((i + 1) % count, i) for i in range(ends)]),
            ],
            axis=dim,
        )
    return cells


def passed_along_2(value, axis, steps):
    count = lax.axis_size(axis)
    leading, last = (max(0, -steps), min(count, count - steps))
    return lax.ppermute(value, axis, [(source, source + steps) for source in range(leading, last)])


def attend(
    q_head,
    o_grad,
    k_head,
    v_head,
    gk_head,
    gv_head,
    key_index,
    key_valid,
    scatter_count,
    rand_count,
):
    q_blocks = q_head.shape[0]
    head_size = q_head.shape[2]
    scaling = 1.0 / math.sqrt(head_size)
    local_lists = key_index.shape[1]
    keys_all = jnp.concatenate(
        [
            jnp.take(k_head, key_index, axis=0),
            jnp.broadcast_to(gk_head[None], (q_blocks,) + gk_head.shape),
        ],
        axis=1,
    ).reshape(q_blocks, -1, head_size)
    values_all = jnp.concatenate(
        [
            jnp.take(v_head, key_index, axis=0),
            jnp.broadcast_to(gv_head[None], (q_blocks,) + gv_head.shape),
        ],
        axis=1,
    ).reshape(q_blocks, -1, head_size)
    keep_mask = jnp.repeat(
        jnp.concatenate([key_valid, jnp.ones((q_blocks, 2), dtype=bool)], axis=1), BLK, axis=1
    )
    scores = (
        jnp.einsum("nqd,nkd->nqk", q_head, keys_all, preferred_element_type=jnp.float32) * scaling
    )
    scores = jnp.where(keep_mask[:, None, :], scores, -1e30)
    row_max = jnp.max(scores, axis=-1, keepdims=True)
    exp_scores = jnp.exp(scores - row_max)
    weights = exp_scores / jnp.sum(exp_scores, axis=-1, keepdims=True)
    weights_b = weights.astype(jnp.bfloat16)
    attn_out = jnp.einsum("nqk,nkd->nqd", weights_b, values_all, preferred_element_type=jnp.float32)
    row_dot = jnp.sum(o_grad.astype(jnp.float32) * attn_out, axis=-1, keepdims=True)
    prob_grad = jnp.einsum("nqd,nkd->nqk", o_grad, values_all, preferred_element_type=jnp.float32)
    score_grad = (weights * (prob_grad - row_dot) * scaling).astype(jnp.bfloat16)
    q_grad = jnp.einsum("nqk,nkd->nqd", score_grad, keys_all, preferred_element_type=jnp.float32)
    k_grad = jnp.einsum(
        "nqk,nqd->nkd", score_grad, q_head, preferred_element_type=jnp.float32
    ).reshape(q_blocks, local_lists + 2, BLK, head_size)
    v_grad = jnp.einsum(
        "nqk,nqd->nkd", weights_b, o_grad, preferred_element_type=jnp.float32
    ).reshape(q_blocks, local_lists + 2, BLK, head_size)
    flat_index = key_index.reshape(-1)
    k_local = (
        jnp.zeros(k_head.shape, jnp.float32)
        .at[flat_index]
        .add(k_grad[:, :scatter_count].reshape(-1, BLK, head_size))
    )
    v_local = (
        jnp.zeros(v_head.shape, jnp.float32)
        .at[flat_index]
        .add(v_grad[:, :scatter_count].reshape(-1, BLK, head_size))
    )
    grad_tiles = score_grad.reshape(q_blocks, BLK, local_lists + 2, BLK)[
        :, :, 3 : 3 + rand_count
    ].transpose(0, 2, 1, 3)
    prob_tiles = weights_b.reshape(q_blocks, BLK, local_lists + 2, BLK)[
        :, :, 3 : 3 + rand_count
    ].transpose(0, 2, 1, 3)
    return (
        q_grad,
        k_local,
        v_local,
        k_grad[:, local_lists:],
        v_grad[:, local_lists:],
        grad_tiles,
        prob_tiles,
    )


def by_heads(row_array, head_count):
    block_total = row_array.shape[0] // BLK
    return row_array.reshape(block_total, BLK, head_count, -1).transpose(2, 0, 1, 3)


def from_heads(head_array):
    head_count = head_array.shape[0]
    head_size = head_array.shape[3]
    return head_array.transpose(1, 2, 0, 3).reshape(-1, head_count * head_size)


def fetch_far(key_value, offset):
    return passed_along(key_value, "ctx", -offset)


def return_far(partials, offset):
    return passed_along(partials, "ctx", offset)


def on_ring(query, key, value, dout, glob_keys, glob_values, glob_ids, rand_blocks):
    row_count = query.shape[1]
    head_count = rand_blocks.shape[0]
    rand_count = rand_blocks.shape[2]
    head_size = query.shape[2] // head_count
    per_device = row_count // BLK
    span_count = lax.axis_size("ctx")
    device_pos = lax.axis_index("ctx")
    block_count = per_device * span_count
    offsets = [(slot + 1) * span_count // (rand_count + 1) for slot in range(rand_count)]
    key_value = jnp.stack([key[0], value[0]])
    extended = padded(key_value, (("ctx", 1),), row_count)
    far_spans = [fetch_far(key_value, offset) for offset in offsets]
    k_rows = jnp.concatenate([extended[0]] + [span[0] for span in far_spans], axis=0)
    v_rows = jnp.concatenate([extended[1]] + [span[1] for span in far_spans], axis=0)
    first_block = device_pos * per_device
    key_base = first_block - per_device
    query_ids = first_block + jnp.arange(per_device, dtype=jnp.int32)
    window = query_ids[:, None] + jnp.arange(-1, 2, dtype=jnp.int32)[None, :]
    key_valid = jnp.concatenate(
        [(window >= 0) & (window < block_count), jnp.ones((per_device, rand_count), dtype=bool)],
        axis=1,
    )
    window_local = jnp.clip(window - key_base, 0, 3 * per_device - 1)
    rand_rows = lax.dynamic_slice_in_dim(rand_blocks, first_block, per_device, 1)
    offset_table = jnp.array(offsets, dtype=jnp.int32)
    far_starts = (device_pos + offset_table) % span_count * per_device
    slot_base = (3 + jnp.arange(rand_count, dtype=jnp.int32)) * per_device
    rand_local = rand_rows - far_starts[None, None, :] + slot_base[None, None, :]
    all_lists = jnp.concatenate(
        [jnp.broadcast_to(window_local[None], (head_count,) + window_local.shape), rand_local],
        axis=2,
    )
    key_index = jnp.clip(all_lists, 0, (3 + rand_count) * per_device - 1)
    chosen = glob_ids[0]
    gk_heads = by_heads(jnp.take(glob_keys, chosen, axis=0).reshape(2 * BLK, -1), head_count)
    gv_heads = by_heads(jnp.take(glob_values, chosen, axis=0).reshape(2 * BLK, -1), head_count)
    scatter_count = 3 + rand_count

    def per_head(pieces):
        q_head, o_grad, k_head, v_head, gk_head, gv_head, index_head = pieces
        return attend(
            q_head,
            o_grad,
            k_head,
            v_head,
            gk_head,
            gv_head,
            index_head,
            key_valid,
            scatter_count,
            rand_count,
        )

    results = lax.map(
        per_head,
        (
            by_heads(query[0], head_count),
            by_heads(dout[0], head_count),
            by_heads(k_rows, head_count),
            by_heads(v_rows, head_count),
            gk_heads,
            gv_heads,
            key_index,
        ),
    )
    q_grad = results[0]
    kv_grads = jnp.stack([results[1], results[2]])
    lower_part = kv_grads[:, :, :per_device]
    upper_part = kv_grads[:, :, 2 * per_device : 3 * per_device]
    from_below = passed_along_2(upper_part.astype(jnp.bfloat16), "ctx", 1).astype(upper_part.dtype)
    from_above = passed_along_2(lower_part.astype(jnp.bfloat16), "ctx", -1).astype(lower_part.dtype)
    own_grads = kv_grads[:, :, per_device : 2 * per_device] + from_below + from_above
    for slot in range(rand_count):
        start = (3 + slot) * per_device
        own_grads = own_grads + return_far(
            kv_grads[:, :, start : start + per_device], offsets[slot]
        )
    global_part = jnp.stack([jnp.sum(results[3], axis=1), jnp.sum(results[4], axis=1)])
    global_part = global_part.transpose(0, 2, 3, 1, 4).reshape(2, 2, BLK, head_count * head_size)
    one_hot = (chosen[:, None] == jnp.arange(glob_keys.shape[0], dtype=jnp.int32)[None, :]).astype(
        jnp.float32
    )
    table_term = jnp.einsum("sg,ksbd->kgbd", one_hot, global_part, precision=lax.Precision.HIGHEST)
    table_grad = lax.psum(table_term, ("ctx", "dp"))
    d_query = from_heads(q_grad).astype(jnp.bfloat16)[None]
    d_key = from_heads(own_grads[0]).astype(jnp.bfloat16)[None]
    d_value = from_heads(own_grads[1]).astype(jnp.bfloat16)[None]
    return (d_query, d_key, d_value, table_grad)


VMEM_BYTES = 24 * 1024 * 1024
SMALL_VMEM_BYTES = 4 * 1024 * 1024
LARGE_VMEM_BYTES = 60 * 1024 * 1024
FINISH_VMEM_BYTES = 24 * 1024 * 1024
MASKED = -1e30
FIRST_BYTES = 60 * 1024 * 1024
PACK_FLOPS = 2 * 10**9
EARLY_FLOPS = 5 * 10**9
GROUP = 8
ORDER = (0, 4, 2, 5, 3, 6, 7, 1)
COLUMN = (0, 2, 4, 6)


def dot(left, right, left_dim, right_dim):
    dims = (((left_dim,), (right_dim,)), ((), ()))
    return lax.dot_general(left, right, dims, preferred_element_type=jnp.float32)


def in_vmem(count):
    return [pl.BlockSpec(memory_space=pltpu.VMEM)] * count


def first_kernel(q_ref, k_ref, v_ref, o_ref, out_ref, sems):
    head_size = out_ref.shape[2]
    at = pl.multiple_of((lax.axis_index("ctx") ^ ORDER[1]) * head_size, head_size)
    copies = [
        pltpu.make_async_copy(
            ref.at[0, :, pl.ds(at, head_size)], out_ref.at[place], sems.at[place]
        )
        for place, ref in enumerate((q_ref, k_ref, v_ref, o_ref))
    ]
    for copy in copies:
        copy.start()
    for copy in copies:
        copy.wait()


def pack_kernel(count, *refs):
    ins, outs = refs[:4], refs[5 : 5 + count]
    held, made, in_sems, out_sems = refs[5 + count :]
    head_size = made.shape[3]
    me = lax.axis_index("ctx")
    loads = [
        pltpu.make_async_copy(ref.at[0], held.at[place], in_sems.at[place])
        for place, ref in enumerate(ins)
    ]
    for load in loads:
        load.start()
    for load in loads:
        load.wait()
    stores = []
    for place, flip in enumerate(ORDER[2:] + ORDER[:1]):
        at = pl.multiple_of((me ^ flip) * head_size, head_size)
        made[place] = held[:, :, pl.ds(at, head_size)]
        store = pltpu.make_async_copy(made.at[place], outs[place], out_sems.at[place])
        store.start()
        stores.append(store)
    for store in stores:
        store.wait()


def pack(query, key, value, dout, head_count):
    _, rows, width = query.shape
    arrays = (query, key, value, dout)
    chunk = (4, rows, width // head_count)
    shape = jax.ShapeDtypeStruct(chunk, query.dtype)
    in_hbm = pl.BlockSpec(memory_space=pltpu.HBM)
    first = pl.pallas_call(
        first_kernel,
        in_specs=[in_hbm] * 4,
        out_specs=pl.BlockSpec(memory_space=pltpu.VMEM),
        out_shape=shape,
        scratch_shapes=[pltpu.SemaphoreType.DMA((4,))],
        compiler_params=pltpu.CompilerParams(vmem_limit_bytes=FIRST_BYTES),
        cost_estimate=pl.CostEstimate(flops=0, bytes_accessed=2 * rows * width, transcendentals=0),
        name="pack_first",
    )(*arrays)
    others = pl.pallas_call(
        functools.partial(pack_kernel, head_count - 1),
        in_specs=[in_hbm] * 5,
        out_specs=[in_hbm] * (head_count - 1),
        out_shape=[shape] * (head_count - 1),
        scratch_shapes=[
            pltpu.VMEM((4, rows, width), query.dtype),
            pltpu.VMEM((head_count - 1,) + chunk, query.dtype),
            pltpu.SemaphoreType.DMA((4,)),
            pltpu.SemaphoreType.DMA((head_count - 1,)),
        ],
        compiler_params=pltpu.CompilerParams(vmem_limit_bytes=LARGE_VMEM_BYTES),
        cost_estimate=pl.CostEstimate(
            flops=PACK_FLOPS, bytes_accessed=16 * rows * width, transcendentals=0
        ),
        name="pack_heads",
    )(*arrays, first)
    return dict(zip(ORDER[2:] + ORDER[:1], others)) | {ORDER[1]: first}


def choose_kernel(place_ref, gk_ref, gv_ref, own_ref, out_ref, held_ref, sems):
    head_size = out_ref.shape[2]
    columns = pl.ds(pl.multiple_of(place_ref[0] * head_size, head_size), head_size)
    copies = [
        pltpu.make_async_copy(
            ref.at[place_ref[1 + slot], :, columns],
            out_ref.at[2 * kind + slot],
            sems.at[2 * kind + slot],
        )
        for kind, ref in enumerate((gk_ref, gv_ref))
        for slot in range(2)
    ]
    copies.append(pltpu.make_async_copy(own_ref, held_ref, sems.at[4]))
    for copy in copies:
        copy.start()
    for copy in copies:
        copy.wait()


def choose(place, glob_keys, glob_values, own):
    head_size = own.shape[2]
    return pl.pallas_call(
        choose_kernel,
        in_specs=[pl.BlockSpec(memory_space=pltpu.SMEM)]
        + [pl.BlockSpec(memory_space=pltpu.HBM)] * 3,
        out_specs=in_vmem(2),
        out_shape=[
            jax.ShapeDtypeStruct((4, BLK, head_size), glob_keys.dtype),
            jax.ShapeDtypeStruct(own.shape, own.dtype),
        ],
        scratch_shapes=[pltpu.SemaphoreType.DMA((5,))],
        compiler_params=pltpu.CompilerParams(vmem_limit_bytes=SMALL_VMEM_BYTES),
        cost_estimate=pl.CostEstimate(
            flops=0, bytes_accessed=16 * BLK * head_size, transcendentals=0
        ),
        name="choose_blocks",
    )(place, glob_keys, glob_values, own)


def split_rows(block):
    empty = jnp.zeros((BLK, block.shape[1]), block.dtype)
    return jnp.concatenate(
        [
            jnp.concatenate([block[:BLK], empty], axis=0),
            jnp.concatenate([empty, block[BLK:]], axis=0),
        ],
        axis=1,
    )


def list_places(rand_ref, span, rand_count):
    return [
        [
            pl.multiple_of((rand_ref[(2 * span + half) * rand_count + slot] + 1) * BLK, BLK)
            for slot in range(rand_count)
        ]
        for half in range(2)
    ]


def gathered(pool, at, places, table_blocks):
    window = pool[at : at + 4 * BLK]
    lists = [
        jnp.concatenate([edge] + [pool[pl.ds(p, BLK)] for p in places[half]], axis=0)
        for half, edge in enumerate((window[:BLK], window[3 * BLK :]))
    ]
    both = jnp.concatenate([window[BLK : 3 * BLK]] + table_blocks, axis=0)
    return jnp.concatenate(lists, axis=1), both


def score_kernel(spans, place_ref, rand_ref, *refs):
    x_refs, g_ref = refs[:spans], refs[spans]
    q_all, k_all, o_all, p_all, ds_all = refs[spans + 1 : spans + 6]
    term_refs, v_all = refs[spans + 6 : spans + 8], refs[spans + 8]
    _, rows, head_size = x_refs[0].shape
    rand_count = rand_ref.shape[0] // (2 * spans)
    scaling = 1.0 / math.sqrt(head_size)
    rate = scaling * math.log2(math.e)
    me = place_ref[0]
    top = BLK + spans * rows
    for pool in (k_all, v_all):
        pool[:BLK] = jnp.zeros((BLK, head_size), pool.dtype)
        pool[top:] = jnp.zeros((BLK, head_size), pool.dtype)
    starts = [pl.multiple_of((me ^ flip) * rows, rows) for flip in ORDER]
    for at, ref in zip(starts, x_refs):
        q_all[pl.ds(at, rows)] = ref[0]
        k_all[pl.ds(pl.multiple_of(at + BLK, BLK), rows)] = ref[1]
        v_all[pl.ds(pl.multiple_of(at + BLK, BLK), rows)] = ref[2]
        o_all[pl.ds(at, rows)] = ref[3]
    gk = [g_ref[0], g_ref[1]]
    gv = [g_ref[2], g_ref[3]]
    own = (1 + rand_count) * BLK
    first = lax.broadcasted_iota(jnp.int32, (1, rows), 1) < BLK
    table_terms = [None, None]
    for group in range(0, spans, GROUP):
        members = range(group, min(group + GROUP, spans))
        made = []
        for span in members:
            at = span * rows
            q = q_all[at : at + rows]
            o = o_all[at : at + rows]
            places = list_places(rand_ref, span, rand_count)
            k_own, k_both = gathered(k_all, at, places, gk)
            s_own = dot(k_own, split_rows(q), 1, 1)
            s_both = dot(k_both, q, 1, 1)
            if span == 0 or span == spans - 1:
                row = lax.broadcasted_iota(jnp.int32, (own, 1), 0) < BLK
                outside = row & (first if span == 0 else jnp.logical_not(first))
                s_own = jnp.where(outside, MASKED / scaling, s_own)
            made.append((q, o, s_own, s_both))
        tops = [
            jnp.maximum(
                jnp.max(s_own, axis=0, keepdims=True), jnp.max(s_both, axis=0, keepdims=True)
            )
            for _, _, s_own, s_both in made
        ]
        powers = []
        values = []
        for span, top_score, (q, o, s_own, s_both) in zip(members, tops, made):
            places = list_places(rand_ref, span, rand_count)
            v_own, v_both = gathered(v_all, span * rows, places, gv)
            values.append((dot(v_own, split_rows(o), 1, 1), dot(v_both, o, 1, 1)))
            powers.append(
                (jnp.exp2((s_own - top_score) * rate), jnp.exp2((s_both - top_score) * rate))
            )
        inverses = [
            1.0 / (jnp.sum(e_own, axis=0, keepdims=True) + jnp.sum(e_both, axis=0, keepdims=True))
            for e_own, e_both in powers
        ]
        for span, (e_own, e_both), inverse, (q, o, _, _), (g_own, g_both) in zip(
            members, powers, inverses, made, values
        ):
            p_own = e_own * inverse
            p_both = e_both * inverse
            pb_own = p_own.astype(jnp.bfloat16)
            pb_both = p_both.astype(jnp.bfloat16)
            row_dot = jnp.sum(
                pb_own.astype(jnp.float32) * g_own, axis=0, keepdims=True
            ) + jnp.sum(pb_both.astype(jnp.float32) * g_both, axis=0, keepdims=True)
            ds_own = (p_own * (g_own - row_dot) * scaling).astype(jnp.bfloat16)
            ds_both = (p_both * (g_both - row_dot) * scaling).astype(jnp.bfloat16)
            p_all[span, :own] = pb_own
            p_all[span, own:] = pb_both
            ds_all[span, :own] = ds_own
            ds_all[span, own:] = ds_both
            for kind, (weight, x) in enumerate(((ds_both, q), (pb_both, o))):
                term = dot(weight[2 * BLK :], x, 1, 0)
                so_far = table_terms[kind]
                table_terms[kind] = term if so_far is None else so_far + term
    mine = lax.axis_index("dp") % 2
    for flip, ref in enumerate(term_refs):
        ref[...] = jnp.zeros(ref.shape, ref.dtype)
        term = jnp.where(mine == flip, table_terms[0], table_terms[1]).astype(ref.dtype)
        for slot in range(2):
            at = pl.multiple_of(place_ref[1 + slot] * BLK, BLK)
            ref[pl.ds(at, BLK)] = term[slot * BLK : (slot + 1) * BLK]


def scores(chunks, chosen, place, rand_head, table_size):
    spans = len(chunks)
    _, rows, head_size = chunks[0].shape
    keys = 8 * BLK
    padded_rows = spans * rows + 2 * BLK
    keys_each = spans * rows * keys
    half = lambda *shape: jax.ShapeDtypeStruct(shape, jnp.bfloat16)
    outs = [
        half(spans * rows, head_size),
        half(padded_rows, head_size),
        half(spans * rows, head_size),
        half(spans, keys, rows),
        half(spans, keys, rows),
    ] + [half(table_size * BLK, head_size)] * 2
    results = pl.pallas_call(
        functools.partial(score_kernel, spans),
        in_specs=[pl.BlockSpec(memory_space=pltpu.SMEM)] * 2 + in_vmem(spans + 1),
        out_specs=in_vmem(len(outs)),
        out_shape=outs,
        scratch_shapes=[
            pltpu.VMEM((padded_rows, head_size), jnp.bfloat16),
        ],
        compiler_params=pltpu.CompilerParams(vmem_limit_bytes=VMEM_BYTES),
        cost_estimate=pl.CostEstimate(
            flops=4 * keys_each * head_size,
            bytes_accessed=8 * spans * rows * head_size,
            transcendentals=keys_each,
        ),
        name="scores",
    )(place, rand_head, *chunks, chosen)
    return results[:5], results[5:]


def added(left, right):
    return (left.astype(jnp.float32) + right.astype(jnp.float32)).astype(left.dtype)


def far_spans(spans, rand_count):
    return [(slot + 1) * spans // (rand_count + 1) for slot in range(rand_count)]


def grad_kernel(
    rand_ref, g_ref, q_all, k_all, o_all, p_all, ds_all, out_ref, made, sems
):
    spans, _, rows, head_size = made.shape
    rand_count = rand_ref.shape[0] // (2 * spans)
    own = (1 + rand_count) * BLK
    gk = [g_ref[0], g_ref[1]]
    offsets = far_spans(spans, rand_count)
    first = lax.broadcasted_iota(jnp.int32, (1, rows), 1) < BLK
    terms = []
    for span in range(spans):
        at = span * rows
        q = q_all[at : at + rows]
        o = o_all[at : at + rows]
        keeps = [first]
        for slot, offset in enumerate(offsets):
            lower = [
                rand_ref[(2 * span + half) * rand_count + slot] == 2 * ((span + offset) % spans)
                for half in range(2)
            ]
            keeps.append((first & lower[0]) | (jnp.logical_not(first) & lower[1]))
        keeps = [jnp.where(keep, 1.0, 0.0).astype(made.dtype) for keep in keeps]
        pair = []
        for weights, x in ((ds_all, q), (p_all, o)):
            parts = [weights[span, own : own + 2 * BLK]]
            for place, keep in enumerate(keeps):
                block = weights[span, place * BLK : (place + 1) * BLK]
                lower = block * keep
                parts += [lower, block - lower]
            pair.append(dot(jnp.concatenate(parts, axis=0), x, 1, 0))
        terms.append(pair)
    copies = []
    for span in range(spans):
        at = span * rows
        k_own, k_both = gathered(k_all, at, list_places(rand_ref, span, rand_count), gk)
        wide = dot(ds_all[span, :own], k_own, 0, 0)
        dq = jnp.concatenate([wide[:BLK, :head_size], wide[BLK:, head_size:]], axis=0)
        dq = dq + dot(ds_all[span, own:], k_both, 0, 0)
        made[span, 0] = dq.astype(made.dtype)
        for kind in range(2):
            part = lambda source, start, count: terms[source][kind][start : start + count]
            edges = [
                part(span - 1, 3 * BLK, BLK) if span > 0 else None,
                part(span + 1, 2 * BLK, BLK) if span < spans - 1 else None,
            ]
            edges = [jnp.zeros((BLK, head_size), jnp.float32) if e is None else e for e in edges]
            total = part(span, 0, 2 * BLK) + jnp.concatenate(edges, axis=0)
            for slot, offset in enumerate(offsets):
                total = total + part((span - offset) % spans, (4 + 2 * slot) * BLK, 2 * BLK)
            made[span, 1 + kind] = total.astype(made.dtype)
        copy = pltpu.make_async_copy(made.at[span], out_ref.at[span], sems.at[span])
        copy.start()
        copies.append(copy)
    for copy in copies:
        copy.wait()


def grads(rand_head, chosen, held):
    spans, keys, rows = held[3].shape
    head_size = held[1].shape[1]
    keys_each = spans * keys * rows
    shape = (spans, 3, rows, head_size)
    return pl.pallas_call(
        grad_kernel,
        in_specs=[pl.BlockSpec(memory_space=pltpu.SMEM)] + in_vmem(1 + len(held)),
        out_specs=pl.BlockSpec(memory_space=pltpu.HBM),
        out_shape=jax.ShapeDtypeStruct(shape, jnp.bfloat16),
        scratch_shapes=[
            pltpu.VMEM(shape, jnp.bfloat16),
            pltpu.SemaphoreType.DMA((spans,)),
        ],
        compiler_params=pltpu.CompilerParams(vmem_limit_bytes=VMEM_BYTES),
        cost_estimate=pl.CostEstimate(
            flops=6 * keys_each * head_size,
            bytes_accessed=8 * spans * rows * head_size,
            transcendentals=0,
        ),
        name="grads",
    )(rand_head, chosen, *held)


def early_kernel(sides, *refs):
    parts, out_ref = refs[:-1], refs[-1]
    head_size = parts[0].shape[2]
    head = lax.axis_index("ctx")
    share = lax.axis_index("dp") % 2
    for side, ref in zip(sides, parts):
        for place in range(ref.shape[0]):
            bits = side[place // len(COLUMN)]
            flip = COLUMN[place % len(COLUMN)]
            columns = pl.ds(pl.multiple_of((head ^ flip) * head_size, head_size), head_size)
            out_ref[share ^ bits, :, columns] = ref[place].astype(out_ref.dtype)


def early_table(head_count, sides, parts):
    _, rows, head_size = parts[0].shape
    shape = (2, rows, head_count * head_size)
    return pl.pallas_call(
        functools.partial(early_kernel, sides),
        in_specs=in_vmem(len(parts)),
        out_specs=pl.BlockSpec(memory_space=pltpu.VMEM),
        out_shape=jax.ShapeDtypeStruct(shape, jnp.float32),
        compiler_params=pltpu.CompilerParams(vmem_limit_bytes=VMEM_BYTES),
        cost_estimate=pl.CostEstimate(
            flops=EARLY_FLOPS, bytes_accessed=2**21, transcendentals=0
        ),
        name="early_table",
    )(*parts)


def finish_kernel(sides, *refs):
    count = len(sides)
    parts, x_ref = refs[:count], refs[count]
    grad_refs, table_ref = refs[count + 2 : count + 5], refs[count + 5]
    grad_made, table_made, grad_sems, table_sems = refs[count + 6 :]
    heads, _, _, head_size = x_ref.shape
    me = lax.axis_index("ctx")
    share = lax.axis_index("dp") % 2
    stores = []
    for side, ref in zip(sides, parts):
        for place in range(ref.shape[0]):
            at = len(stores)
            bits = side[place // len(COLUMN)]
            flip = COLUMN[place % len(COLUMN)] ^ 1
            columns = pl.ds(pl.multiple_of((me ^ flip) * head_size, head_size), head_size)
            table_made[at] = ref[place].astype(table_made.dtype)
            store = pltpu.make_async_copy(
                table_made.at[at], table_ref.at[share ^ bits, :, columns], table_sems.at[at]
            )
            store.start()
            stores.append(store)
    for place, ref in enumerate(grad_refs):
        for head in range(heads):
            columns = slice(head * head_size, (head + 1) * head_size)
            grad_made[place, :, columns] = x_ref[head, place]
        store = pltpu.make_async_copy(grad_made.at[place], ref.at[0], grad_sems.at[place])
        store.start()
        stores.append(store)
    for store in stores:
        store.wait()


def finish(x, table, sides, parts):
    heads, kinds, rows, head_size = x.shape
    blocks = sum(part.shape[0] for part in parts)
    in_hbm = pl.BlockSpec(memory_space=pltpu.HBM)
    grad = jax.ShapeDtypeStruct((1, rows, heads * head_size), x.dtype)
    return pl.pallas_call(
        functools.partial(finish_kernel, sides),
        in_specs=in_vmem(len(parts) + 1) + [in_hbm],
        out_specs=[in_hbm] * (kinds + 1),
        out_shape=[grad] * kinds + [jax.ShapeDtypeStruct(table.shape, table.dtype)],
        scratch_shapes=[
            pltpu.VMEM((kinds, rows, heads * head_size), x.dtype),
            pltpu.VMEM((blocks,) + parts[0].shape[1:], table.dtype),
            pltpu.SemaphoreType.DMA((kinds,)),
            pltpu.SemaphoreType.DMA((blocks,)),
        ],
        input_output_aliases={len(parts) + 1: kinds},
        compiler_params=pltpu.CompilerParams(vmem_limit_bytes=FINISH_VMEM_BYTES),
        cost_estimate=pl.CostEstimate(flops=0, bytes_accessed=2**21, transcendentals=0),
        name="finish",
    )(*parts, x, table)


def flipped(array, axis, bits):
    if bits == 0:
        return array
    return lax.ppermute(array, axis, [(i, i ^ bits) for i in range(lax.axis_size(axis))])


def on_heads(query, key, value, dout, glob_keys, glob_values, glob_ids, rand_blocks):
    head_count, block_count, _ = rand_blocks.shape
    head_size = query.shape[2] // head_count
    table_size = glob_keys.shape[0]
    head = lax.axis_index("ctx").astype(jnp.int32)
    packed = pack(query, key, value, dout, head_count)
    chunks = [flipped(packed[flip], "ctx", flip) for flip in ORDER]
    place = jnp.concatenate([head[None], glob_ids[0]])
    rand_head = lax.dynamic_index_in_dim(rand_blocks, head, 0, keepdims=False).reshape(-1)
    rand_head = jnp.clip(rand_head, 0, block_count - 1)
    chosen, chunks[0] = choose(place, glob_keys, glob_values, packed[0])
    held, (kept, given) = scores(chunks, chosen, place, rand_head, table_size)
    given = flipped(given, "dp", 1)
    sent = grads(rand_head, chosen, held)
    given, sent = lax.optimization_barrier((given, sent))
    back = lax.all_to_all(sent, "ctx", 0, 0)
    chip = added(kept, given)
    column = jnp.stack([flipped(chip, "ctx", flip) for flip in COLUMN])
    even = added(column, flipped(column, "dp", 2))
    odd = flipped(even, "ctx", 1)
    beside_even = flipped(even, "dp", 1)
    beside_odd = flipped(odd, "dp", 1)
    d_table = early_table(head_count, ((0,), (1,)), [even, beside_even])
    d_query, d_key, d_value, d_table = finish(
        back, d_table, ((0,), (1,)), [odd, beside_odd]
    )
    return (d_query, d_key, d_value, d_table.reshape((2,) + glob_keys.shape))


def on_device(query, key, value, dout, glob_keys, glob_values, glob_ids, rand_blocks):
    head_count = rand_blocks.shape[0]
    one_head_each = lax.axis_size("ctx") == head_count == 8 and query.shape[1] == 2 * BLK
    if one_head_each and lax.axis_size("dp") == 4 and glob_keys.shape[0] % 2 == 0:
        plan = on_heads
    else:
        plan = on_ring
    return plan(query, key, value, dout, glob_keys, glob_values, glob_ids, rand_blocks)


def solution(mesh):
    placed = (
        P("dp", "ctx", None),
        P("dp", "ctx", None),
        P("dp", "ctx", None),
        P("dp", "ctx", None),
        P(),
        P(),
        P("dp", None),
        P(),
    )
    return jax.shard_map(
        on_device,
        mesh=mesh,
        in_specs=placed,
        out_specs=(P("dp", "ctx", None), P("dp", "ctx", None), P("dp", "ctx", None), P()),
        check_vma=False,
    )
```

```python
import functools
import math

import jax
import jax.numpy as jnp
from jax import lax
from jax.experimental import pallas as pl
from jax.experimental.pallas import tpu as pltpu
from jax.sharding import PartitionSpec as P

BLK = 64


def passed_along(shard, axis, by):
    length = lax.axis_size(axis)
    return lax.ppermute(shard, axis, [(i, (i + by) % length) for i in range(length)])


def padded(cells, sides, width):
    for axis, dim in sides:
        count = lax.axis_size(axis)
        ends = count - 1
        head = lax.slice_in_dim(cells, 0, width, axis=dim)
        tail = lax.slice_in_dim(cells, cells.shape[dim] - width, cells.shape[dim], axis=dim)
        cells = jnp.concatenate(
            [
                lax.ppermute(tail, axis, [(i, (i + 1) % count) for i in range(ends)]),
                cells,
                lax.ppermute(head, axis, [((i + 1) % count, i) for i in range(ends)]),
            ],
            axis=dim,
        )
    return cells


def passed_along_2(value, axis, steps):
    count = lax.axis_size(axis)
    leading, last = (max(0, -steps), min(count, count - steps))
    return lax.ppermute(value, axis, [(source, source + steps) for source in range(leading, last)])


def attend(
    q_head,
    o_grad,
    k_head,
    v_head,
    gk_head,
    gv_head,
    key_index,
    key_valid,
    scatter_count,
    rand_count,
):
    q_blocks = q_head.shape[0]
    head_size = q_head.shape[2]
    scaling = 1.0 / math.sqrt(head_size)
    local_lists = key_index.shape[1]
    keys_all = jnp.concatenate(
        [
            jnp.take(k_head, key_index, axis=0),
            jnp.broadcast_to(gk_head[None], (q_blocks,) + gk_head.shape),
        ],
        axis=1,
    ).reshape(q_blocks, -1, head_size)
    values_all = jnp.concatenate(
        [
            jnp.take(v_head, key_index, axis=0),
            jnp.broadcast_to(gv_head[None], (q_blocks,) + gv_head.shape),
        ],
        axis=1,
    ).reshape(q_blocks, -1, head_size)
    keep_mask = jnp.repeat(
        jnp.concatenate([key_valid, jnp.ones((q_blocks, 2), dtype=bool)], axis=1), BLK, axis=1
    )
    scores = (
        jnp.einsum("nqd,nkd->nqk", q_head, keys_all, preferred_element_type=jnp.float32) * scaling
    )
    scores = jnp.where(keep_mask[:, None, :], scores, -1e30)
    row_max = jnp.max(scores, axis=-1, keepdims=True)
    exp_scores = jnp.exp(scores - row_max)
    weights = exp_scores / jnp.sum(exp_scores, axis=-1, keepdims=True)
    weights_b = weights.astype(jnp.bfloat16)
    attn_out = jnp.einsum("nqk,nkd->nqd", weights_b, values_all, preferred_element_type=jnp.float32)
    row_dot = jnp.sum(o_grad.astype(jnp.float32) * attn_out, axis=-1, keepdims=True)
    prob_grad = jnp.einsum("nqd,nkd->nqk", o_grad, values_all, preferred_element_type=jnp.float32)
    score_grad = (weights * (prob_grad - row_dot) * scaling).astype(jnp.bfloat16)
    q_grad = jnp.einsum("nqk,nkd->nqd", score_grad, keys_all, preferred_element_type=jnp.float32)
    k_grad = jnp.einsum(
        "nqk,nqd->nkd", score_grad, q_head, preferred_element_type=jnp.float32
    ).reshape(q_blocks, local_lists + 2, BLK, head_size)
    v_grad = jnp.einsum(
        "nqk,nqd->nkd", weights_b, o_grad, preferred_element_type=jnp.float32
    ).reshape(q_blocks, local_lists + 2, BLK, head_size)
    flat_index = key_index.reshape(-1)
    k_local = (
        jnp.zeros(k_head.shape, jnp.float32)
        .at[flat_index]
        .add(k_grad[:, :scatter_count].reshape(-1, BLK, head_size))
    )
    v_local = (
        jnp.zeros(v_head.shape, jnp.float32)
        .at[flat_index]
        .add(v_grad[:, :scatter_count].reshape(-1, BLK, head_size))
    )
    grad_tiles = score_grad.reshape(q_blocks, BLK, local_lists + 2, BLK)[
        :, :, 3 : 3 + rand_count
    ].transpose(0, 2, 1, 3)
    prob_tiles = weights_b.reshape(q_blocks, BLK, local_lists + 2, BLK)[
        :, :, 3 : 3 + rand_count
    ].transpose(0, 2, 1, 3)
    return (
        q_grad,
        k_local,
        v_local,
        k_grad[:, local_lists:],
        v_grad[:, local_lists:],
        grad_tiles,
        prob_tiles,
    )


def by_heads(row_array, head_count):
    block_total = row_array.shape[0] // BLK
    return row_array.reshape(block_total, BLK, head_count, -1).transpose(2, 0, 1, 3)


def from_heads(head_array):
    head_count = head_array.shape[0]
    head_size = head_array.shape[3]
    return head_array.transpose(1, 2, 0, 3).reshape(-1, head_count * head_size)


def fetch_far(key_value, offset):
    return passed_along(key_value, "ctx", -offset)


def return_far(partials, offset):
    return passed_along(partials, "ctx", offset)


def on_ring(query, key, value, dout, glob_keys, glob_values, glob_ids, rand_blocks):
    row_count = query.shape[1]
    head_count = rand_blocks.shape[0]
    rand_count = rand_blocks.shape[2]
    head_size = query.shape[2] // head_count
    per_device = row_count // BLK
    span_count = lax.axis_size("ctx")
    device_pos = lax.axis_index("ctx")
    block_count = per_device * span_count
    offsets = [(slot + 1) * span_count // (rand_count + 1) for slot in range(rand_count)]
    key_value = jnp.stack([key[0], value[0]])
    extended = padded(key_value, (("ctx", 1),), row_count)
    far_spans = [fetch_far(key_value, offset) for offset in offsets]
    k_rows = jnp.concatenate([extended[0]] + [span[0] for span in far_spans], axis=0)
    v_rows = jnp.concatenate([extended[1]] + [span[1] for span in far_spans], axis=0)
    first_block = device_pos * per_device
    key_base = first_block - per_device
    query_ids = first_block + jnp.arange(per_device, dtype=jnp.int32)
    window = query_ids[:, None] + jnp.arange(-1, 2, dtype=jnp.int32)[None, :]
    key_valid = jnp.concatenate(
        [(window >= 0) & (window < block_count), jnp.ones((per_device, rand_count), dtype=bool)],
        axis=1,
    )
    window_local = jnp.clip(window - key_base, 0, 3 * per_device - 1)
    rand_rows = lax.dynamic_slice_in_dim(rand_blocks, first_block, per_device, 1)
    offset_table = jnp.array(offsets, dtype=jnp.int32)
    far_starts = (device_pos + offset_table) % span_count * per_device
    slot_base = (3 + jnp.arange(rand_count, dtype=jnp.int32)) * per_device
    rand_local = rand_rows - far_starts[None, None, :] + slot_base[None, None, :]
    all_lists = jnp.concatenate(
        [jnp.broadcast_to(window_local[None], (head_count,) + window_local.shape), rand_local],
        axis=2,
    )
    key_index = jnp.clip(all_lists, 0, (3 + rand_count) * per_device - 1)
    chosen = glob_ids[0]
    gk_heads = by_heads(jnp.take(glob_keys, chosen, axis=0).reshape(2 * BLK, -1), head_count)
    gv_heads = by_heads(jnp.take(glob_values, chosen, axis=0).reshape(2 * BLK, -1), head_count)
    scatter_count = 3 + rand_count

    def per_head(pieces):
        q_head, o_grad, k_head, v_head, gk_head, gv_head, index_head = pieces
        return attend(
            q_head,
            o_grad,
            k_head,
            v_head,
            gk_head,
            gv_head,
            index_head,
            key_valid,
            scatter_count,
            rand_count,
        )

    results = lax.map(
        per_head,
        (
            by_heads(query[0], head_count),
            by_heads(dout[0], head_count),
            by_heads(k_rows, head_count),
            by_heads(v_rows, head_count),
            gk_heads,
            gv_heads,
            key_index,
        ),
    )
    q_grad = results[0]
    kv_grads = jnp.stack([results[1], results[2]])
    lower_part = kv_grads[:, :, :per_device]
    upper_part = kv_grads[:, :, 2 * per_device : 3 * per_device]
    from_below = passed_along_2(upper_part.astype(jnp.bfloat16), "ctx", 1).astype(upper_part.dtype)
    from_above = passed_along_2(lower_part.astype(jnp.bfloat16), "ctx", -1).astype(lower_part.dtype)
    own_grads = kv_grads[:, :, per_device : 2 * per_device] + from_below + from_above
    for slot in range(rand_count):
        start = (3 + slot) * per_device
        own_grads = own_grads + return_far(
            kv_grads[:, :, start : start + per_device], offsets[slot]
        )
    global_part = jnp.stack([jnp.sum(results[3], axis=1), jnp.sum(results[4], axis=1)])
    global_part = global_part.transpose(0, 2, 3, 1, 4).reshape(2, 2, BLK, head_count * head_size)
    one_hot = (chosen[:, None] == jnp.arange(glob_keys.shape[0], dtype=jnp.int32)[None, :]).astype(
        jnp.float32
    )
    table_term = jnp.einsum("sg,ksbd->kgbd", one_hot, global_part, precision=lax.Precision.HIGHEST)
    table_grad = lax.psum(table_term, ("ctx", "dp"))
    d_query = from_heads(q_grad).astype(jnp.bfloat16)[None]
    d_key = from_heads(own_grads[0]).astype(jnp.bfloat16)[None]
    d_value = from_heads(own_grads[1]).astype(jnp.bfloat16)[None]
    return (d_query, d_key, d_value, table_grad)


VMEM_BYTES = 24 * 1024 * 1024
SMALL_VMEM_BYTES = 4 * 1024 * 1024
LARGE_VMEM_BYTES = 60 * 1024 * 1024
FINISH_VMEM_BYTES = 24 * 1024 * 1024
MASKED = -1e30
FIRST_BYTES = 60 * 1024 * 1024
PACK_FLOPS = 2 * 10**9
EARLY_FLOPS = 5 * 10**9
GROUP = 8
ORDER = (0, 4, 3, 5, 2, 6, 7, 1)
COLUMN = (0, 2, 4, 6)


def dot(left, right, left_dim, right_dim):
    dims = (((left_dim,), (right_dim,)), ((), ()))
    return lax.dot_general(left, right, dims, preferred_element_type=jnp.float32)


def in_vmem(count):
    return [pl.BlockSpec(memory_space=pltpu.VMEM)] * count


def first_kernel(q_ref, k_ref, v_ref, o_ref, out_ref, held, in_sems, out_sems):
    head_size = out_ref.shape[2]
    at = pl.multiple_of((lax.axis_index("ctx") ^ ORDER[1]) * head_size, head_size)
    loads = [
        pltpu.make_async_copy(
            ref.at[0, :, pl.ds(at, head_size)], held.at[place], in_sems.at[place]
        )
        for place, ref in enumerate((q_ref, k_ref, v_ref, o_ref))
    ]
    stores = [
        pltpu.make_async_copy(held.at[place], out_ref.at[place], out_sems.at[place])
        for place in range(len(loads))
    ]
    for load in loads:
        load.start()
    for load, store in zip(loads, stores):
        load.wait()
        store.start()
    for store in stores:
        store.wait()


def pack_kernel(count, *refs):
    ins, outs = refs[:4], refs[5 : 5 + count]
    held, made, in_sems, out_sems = refs[5 + count :]
    head_size = made.shape[3]
    me = lax.axis_index("ctx")
    loads = [
        pltpu.make_async_copy(ref.at[0], held.at[place], in_sems.at[place])
        for place, ref in enumerate(ins)
    ]
    for load in loads:
        load.start()
    for load in loads:
        load.wait()
    stores = []
    for place, flip in enumerate(ORDER[2:] + ORDER[:1]):
        at = pl.multiple_of((me ^ flip) * head_size, head_size)
        made[place] = held[:, :, pl.ds(at, head_size)]
        store = pltpu.make_async_copy(made.at[place], outs[place], out_sems.at[place])
        store.start()
        stores.append(store)
    for store in stores:
        store.wait()


def pack(query, key, value, dout, head_count):
    _, rows, width = query.shape
    arrays = (query, key, value, dout)
    chunk = (4, rows, width // head_count)
    shape = jax.ShapeDtypeStruct(chunk, query.dtype)
    in_hbm = pl.BlockSpec(memory_space=pltpu.HBM)
    first = pl.pallas_call(
        first_kernel,
        in_specs=[in_hbm] * 4,
        out_specs=in_hbm,
        out_shape=shape,
        scratch_shapes=[
            pltpu.VMEM(chunk, query.dtype),
            pltpu.SemaphoreType.DMA((4,)),
            pltpu.SemaphoreType.DMA((4,)),
        ],
        compiler_params=pltpu.CompilerParams(vmem_limit_bytes=FIRST_BYTES),
        cost_estimate=pl.CostEstimate(flops=0, bytes_accessed=2 * rows * width, transcendentals=0),
        name="pack_first",
    )(*arrays)
    others = pl.pallas_call(
        functools.partial(pack_kernel, head_count - 1),
        in_specs=[in_hbm] * 5,
        out_specs=[in_hbm] * (head_count - 1),
        out_shape=[shape] * (head_count - 1),
        scratch_shapes=[
            pltpu.VMEM((4, rows, width), query.dtype),
            pltpu.VMEM((head_count - 1,) + chunk, query.dtype),
            pltpu.SemaphoreType.DMA((4,)),
            pltpu.SemaphoreType.DMA((head_count - 1,)),
        ],
        compiler_params=pltpu.CompilerParams(vmem_limit_bytes=LARGE_VMEM_BYTES),
        cost_estimate=pl.CostEstimate(
            flops=PACK_FLOPS, bytes_accessed=16 * rows * width, transcendentals=0
        ),
        name="pack_heads",
    )(*arrays, first)
    return dict(zip(ORDER[2:] + ORDER[:1], others)) | {ORDER[1]: first}


def choose_kernel(place_ref, gk_ref, gv_ref, own_ref, out_ref, held_ref, sems):
    head_size = out_ref.shape[2]
    columns = pl.ds(pl.multiple_of(place_ref[0] * head_size, head_size), head_size)
    copies = [
        pltpu.make_async_copy(
            ref.at[place_ref[1 + slot], :, columns],
            out_ref.at[2 * kind + slot],
            sems.at[2 * kind + slot],
        )
        for kind, ref in enumerate((gk_ref, gv_ref))
        for slot in range(2)
    ]
    copies.append(pltpu.make_async_copy(own_ref, held_ref, sems.at[4]))
    for copy in copies:
        copy.start()
    for copy in copies:
        copy.wait()


def choose(place, glob_keys, glob_values, own):
    head_size = own.shape[2]
    return pl.pallas_call(
        choose_kernel,
        in_specs=[pl.BlockSpec(memory_space=pltpu.SMEM)]
        + [pl.BlockSpec(memory_space=pltpu.HBM)] * 3,
        out_specs=in_vmem(2),
        out_shape=[
            jax.ShapeDtypeStruct((4, BLK, head_size), glob_keys.dtype),
            jax.ShapeDtypeStruct(own.shape, own.dtype),
        ],
        scratch_shapes=[pltpu.SemaphoreType.DMA((5,))],
        compiler_params=pltpu.CompilerParams(vmem_limit_bytes=SMALL_VMEM_BYTES),
        cost_estimate=pl.CostEstimate(
            flops=0, bytes_accessed=16 * BLK * head_size, transcendentals=0
        ),
        name="choose_blocks",
    )(place, glob_keys, glob_values, own)


def split_rows(block):
    empty = jnp.zeros((BLK, block.shape[1]), block.dtype)
    return jnp.concatenate(
        [
            jnp.concatenate([block[:BLK], empty], axis=0),
            jnp.concatenate([empty, block[BLK:]], axis=0),
        ],
        axis=1,
    )


def list_places(rand_ref, span, rand_count):
    return [
        [
            pl.multiple_of((rand_ref[(2 * span + half) * rand_count + slot] + 1) * BLK, BLK)
            for slot in range(rand_count)
        ]
        for half in range(2)
    ]


def gathered(pool, at, places, table_blocks):
    window = pool[at : at + 4 * BLK]
    lists = [
        jnp.concatenate([edge] + [pool[pl.ds(p, BLK)] for p in places[half]], axis=0)
        for half, edge in enumerate((window[:BLK], window[3 * BLK :]))
    ]
    both = jnp.concatenate([window[BLK : 3 * BLK]] + table_blocks, axis=0)
    return jnp.concatenate(lists, axis=1), both


def score_kernel(spans, place_ref, rand_ref, *refs):
    x_refs, g_ref = refs[:spans], refs[spans]
    q_all, k_all, o_all, p_all, ds_all = refs[spans + 1 : spans + 6]
    term_refs, v_all = refs[spans + 6 : spans + 8], refs[spans + 8]
    _, rows, head_size = x_refs[0].shape
    rand_count = rand_ref.shape[0] // (2 * spans)
    scaling = 1.0 / math.sqrt(head_size)
    rate = scaling * math.log2(math.e)
    me = place_ref[0]
    top = BLK + spans * rows
    for pool in (k_all, v_all):
        pool[:BLK] = jnp.zeros((BLK, head_size), pool.dtype)
        pool[top:] = jnp.zeros((BLK, head_size), pool.dtype)
    starts = [pl.multiple_of((me ^ flip) * rows, rows) for flip in ORDER]
    for at, ref in zip(starts, x_refs):
        q_all[pl.ds(at, rows)] = ref[0]
        k_all[pl.ds(pl.multiple_of(at + BLK, BLK), rows)] = ref[1]
        v_all[pl.ds(pl.multiple_of(at + BLK, BLK), rows)] = ref[2]
        o_all[pl.ds(at, rows)] = ref[3]
    gk = [g_ref[0], g_ref[1]]
    gv = [g_ref[2], g_ref[3]]
    own = (1 + rand_count) * BLK
    first = lax.broadcasted_iota(jnp.int32, (1, rows), 1) < BLK
    table_terms = [None, None]
    for group in range(0, spans, GROUP):
        members = range(group, min(group + GROUP, spans))
        made = []
        for span in members:
            at = span * rows
            q = q_all[at : at + rows]
            o = o_all[at : at + rows]
            places = list_places(rand_ref, span, rand_count)
            k_own, k_both = gathered(k_all, at, places, gk)
            s_own = dot(k_own, split_rows(q), 1, 1)
            s_both = dot(k_both, q, 1, 1)
            if span == 0 or span == spans - 1:
                row = lax.broadcasted_iota(jnp.int32, (own, 1), 0) < BLK
                outside = row & (first if span == 0 else jnp.logical_not(first))
                s_own = jnp.where(outside, MASKED / scaling, s_own)
            made.append((q, o, s_own, s_both))
        tops = [
            jnp.maximum(
                jnp.max(s_own, axis=0, keepdims=True), jnp.max(s_both, axis=0, keepdims=True)
            )
            for _, _, s_own, s_both in made
        ]
        powers = []
        values = []
        for span, top_score, (q, o, s_own, s_both) in zip(members, tops, made):
            places = list_places(rand_ref, span, rand_count)
            v_own, v_both = gathered(v_all, span * rows, places, gv)
            values.append((dot(v_own, split_rows(o), 1, 1), dot(v_both, o, 1, 1)))
            powers.append(
                (jnp.exp2((s_own - top_score) * rate), jnp.exp2((s_both - top_score) * rate))
            )
        inverses = [
            1.0 / (jnp.sum(e_own, axis=0, keepdims=True) + jnp.sum(e_both, axis=0, keepdims=True))
            for e_own, e_both in powers
        ]
        for span, (e_own, e_both), inverse, (q, o, _, _), (g_own, g_both) in zip(
            members, powers, inverses, made, values
        ):
            p_own = e_own * inverse
            p_both = e_both * inverse
            pb_own = p_own.astype(jnp.bfloat16)
            pb_both = p_both.astype(jnp.bfloat16)
            row_dot = jnp.sum(
                pb_own.astype(jnp.float32) * g_own, axis=0, keepdims=True
            ) + jnp.sum(pb_both.astype(jnp.float32) * g_both, axis=0, keepdims=True)
            ds_own = (p_own * (g_own - row_dot) * scaling).astype(jnp.bfloat16)
            ds_both = (p_both * (g_both - row_dot) * scaling).astype(jnp.bfloat16)
            p_all[span, :own] = pb_own
            p_all[span, own:] = pb_both
            ds_all[span, :own] = ds_own
            ds_all[span, own:] = ds_both
            for kind, (weight, x) in enumerate(((ds_both, q), (pb_both, o))):
                term = dot(weight[2 * BLK :], x, 1, 0)
                so_far = table_terms[kind]
                table_terms[kind] = term if so_far is None else so_far + term
    mine = lax.axis_index("dp") % 2
    for flip, ref in enumerate(term_refs):
        ref[...] = jnp.zeros(ref.shape, ref.dtype)
        term = jnp.where(mine == flip, table_terms[0], table_terms[1]).astype(ref.dtype)
        for slot in range(2):
            at = pl.multiple_of(place_ref[1 + slot] * BLK, BLK)
            ref[pl.ds(at, BLK)] = term[slot * BLK : (slot + 1) * BLK]


def scores(chunks, chosen, place, rand_head, table_size):
    spans = len(chunks)
    _, rows, head_size = chunks[0].shape
    keys = 8 * BLK
    padded_rows = spans * rows + 2 * BLK
    keys_each = spans * rows * keys
    half = lambda *shape: jax.ShapeDtypeStruct(shape, jnp.bfloat16)
    outs = [
        half(spans * rows, head_size),
        half(padded_rows, head_size),
        half(spans * rows, head_size),
        half(spans, keys, rows),
        half(spans, keys, rows),
    ] + [half(table_size * BLK, head_size)] * 2
    results = pl.pallas_call(
        functools.partial(score_kernel, spans),
        in_specs=[pl.BlockSpec(memory_space=pltpu.SMEM)] * 2 + in_vmem(spans + 1),
        out_specs=in_vmem(len(outs)),
        out_shape=outs,
        scratch_shapes=[
            pltpu.VMEM((padded_rows, head_size), jnp.bfloat16),
        ],
        compiler_params=pltpu.CompilerParams(vmem_limit_bytes=VMEM_BYTES),
        cost_estimate=pl.CostEstimate(
            flops=4 * keys_each * head_size,
            bytes_accessed=8 * spans * rows * head_size,
            transcendentals=keys_each,
        ),
        name="scores",
    )(place, rand_head, *chunks, chosen)
    return results[:5], results[5:]


def added(left, right):
    return (left.astype(jnp.float32) + right.astype(jnp.float32)).astype(left.dtype)


def far_spans(spans, rand_count):
    return [(slot + 1) * spans // (rand_count + 1) for slot in range(rand_count)]


def grad_kernel(
    rand_ref, g_ref, q_all, k_all, o_all, p_all, ds_all, out_ref, made, sems
):
    spans, _, rows, head_size = made.shape
    rand_count = rand_ref.shape[0] // (2 * spans)
    own = (1 + rand_count) * BLK
    gk = [g_ref[0], g_ref[1]]
    offsets = far_spans(spans, rand_count)
    first = lax.broadcasted_iota(jnp.int32, (1, rows), 1) < BLK
    terms = []
    for span in range(spans):
        at = span * rows
        q = q_all[at : at + rows]
        o = o_all[at : at + rows]
        keeps = [first]
        for slot, offset in enumerate(offsets):
            lower = [
                rand_ref[(2 * span + half) * rand_count + slot] == 2 * ((span + offset) % spans)
                for half in range(2)
            ]
            keeps.append((first & lower[0]) | (jnp.logical_not(first) & lower[1]))
        keeps = [jnp.where(keep, 1.0, 0.0).astype(made.dtype) for keep in keeps]
        pair = []
        for weights, x in ((ds_all, q), (p_all, o)):
            parts = [weights[span, own : own + 2 * BLK]]
            for place, keep in enumerate(keeps):
                block = weights[span, place * BLK : (place + 1) * BLK]
                lower = block * keep
                parts += [lower, block - lower]
            pair.append(dot(jnp.concatenate(parts, axis=0), x, 1, 0))
        terms.append(pair)
    copies = []
    for span in range(spans):
        at = span * rows
        k_own, k_both = gathered(k_all, at, list_places(rand_ref, span, rand_count), gk)
        wide = dot(ds_all[span, :own], k_own, 0, 0)
        dq = jnp.concatenate([wide[:BLK, :head_size], wide[BLK:, head_size:]], axis=0)
        dq = dq + dot(ds_all[span, own:], k_both, 0, 0)
        made[span, 0] = dq.astype(made.dtype)
        for kind in range(2):
            part = lambda source, start, count: terms[source][kind][start : start + count]
            edges = [
                part(span - 1, 3 * BLK, BLK) if span > 0 else None,
                part(span + 1, 2 * BLK, BLK) if span < spans - 1 else None,
            ]
            edges = [jnp.zeros((BLK, head_size), jnp.float32) if e is None else e for e in edges]
            total = part(span, 0, 2 * BLK) + jnp.concatenate(edges, axis=0)
            for slot, offset in enumerate(offsets):
                total = total + part((span - offset) % spans, (4 + 2 * slot) * BLK, 2 * BLK)
            made[span, 1 + kind] = total.astype(made.dtype)
        copy = pltpu.make_async_copy(made.at[span], out_ref.at[span], sems.at[span])
        copy.start()
        copies.append(copy)
    for copy in copies:
        copy.wait()


def grads(rand_head, chosen, held):
    spans, keys, rows = held[3].shape
    head_size = held[1].shape[1]
    keys_each = spans * keys * rows
    shape = (spans, 3, rows, head_size)
    return pl.pallas_call(
        grad_kernel,
        in_specs=[pl.BlockSpec(memory_space=pltpu.SMEM)] + in_vmem(1 + len(held)),
        out_specs=pl.BlockSpec(memory_space=pltpu.HBM),
        out_shape=jax.ShapeDtypeStruct(shape, jnp.bfloat16),
        scratch_shapes=[
            pltpu.VMEM(shape, jnp.bfloat16),
            pltpu.SemaphoreType.DMA((spans,)),
        ],
        compiler_params=pltpu.CompilerParams(vmem_limit_bytes=VMEM_BYTES),
        cost_estimate=pl.CostEstimate(
            flops=6 * keys_each * head_size,
            bytes_accessed=8 * spans * rows * head_size,
            transcendentals=0,
        ),
        name="grads",
    )(rand_head, chosen, *held)


def early_kernel(sides, *refs):
    parts, out_ref = refs[:-1], refs[-1]
    head_size = parts[0].shape[2]
    head = lax.axis_index("ctx")
    share = lax.axis_index("dp") % 2
    for side, ref in zip(sides, parts):
        for place in range(ref.shape[0]):
            bits = side[place // len(COLUMN)]
            flip = COLUMN[place % len(COLUMN)]
            columns = pl.ds(pl.multiple_of((head ^ flip) * head_size, head_size), head_size)
            out_ref[share ^ bits, :, columns] = ref[place].astype(out_ref.dtype)


def early_table(head_count, sides, parts):
    _, rows, head_size = parts[0].shape
    shape = (2, rows, head_count * head_size)
    return pl.pallas_call(
        functools.partial(early_kernel, sides),
        in_specs=in_vmem(len(parts)),
        out_specs=pl.BlockSpec(memory_space=pltpu.VMEM),
        out_shape=jax.ShapeDtypeStruct(shape, jnp.float32),
        compiler_params=pltpu.CompilerParams(vmem_limit_bytes=VMEM_BYTES),
        cost_estimate=pl.CostEstimate(
            flops=EARLY_FLOPS, bytes_accessed=2**21, transcendentals=0
        ),
        name="early_table",
    )(*parts)


def finish_kernel(sides, *refs):
    count = len(sides)
    parts, x_ref = refs[:count], refs[count]
    grad_refs, table_ref = refs[count + 2 : count + 5], refs[count + 5]
    grad_made, table_made, grad_sems, table_sems = refs[count + 6 :]
    heads, _, _, head_size = x_ref.shape
    me = lax.axis_index("ctx")
    share = lax.axis_index("dp") % 2
    stores = []
    for side, ref in zip(sides, parts):
        for place in range(ref.shape[0]):
            at = len(stores)
            bits = side[place // len(COLUMN)]
            flip = COLUMN[place % len(COLUMN)] ^ 1
            columns = pl.ds(pl.multiple_of((me ^ flip) * head_size, head_size), head_size)
            table_made[at] = ref[place].astype(table_made.dtype)
            store = pltpu.make_async_copy(
                table_made.at[at], table_ref.at[share ^ bits, :, columns], table_sems.at[at]
            )
            store.start()
            stores.append(store)
    for place, ref in enumerate(grad_refs):
        for head in range(heads):
            columns = slice(head * head_size, (head + 1) * head_size)
            grad_made[place, :, columns] = x_ref[head, place]
        store = pltpu.make_async_copy(grad_made.at[place], ref.at[0], grad_sems.at[place])
        store.start()
        stores.append(store)
    for store in stores:
        store.wait()


def finish(x, table, sides, parts):
    heads, kinds, rows, head_size = x.shape
    blocks = sum(part.shape[0] for part in parts)
    in_hbm = pl.BlockSpec(memory_space=pltpu.HBM)
    grad = jax.ShapeDtypeStruct((1, rows, heads * head_size), x.dtype)
    return pl.pallas_call(
        functools.partial(finish_kernel, sides),
        in_specs=in_vmem(len(parts) + 1) + [in_hbm],
        out_specs=[in_hbm] * (kinds + 1),
        out_shape=[grad] * kinds + [jax.ShapeDtypeStruct(table.shape, table.dtype)],
        scratch_shapes=[
            pltpu.VMEM((kinds, rows, heads * head_size), x.dtype),
            pltpu.VMEM((blocks,) + parts[0].shape[1:], table.dtype),
            pltpu.SemaphoreType.DMA((kinds,)),
            pltpu.SemaphoreType.DMA((blocks,)),
        ],
        input_output_aliases={len(parts) + 1: kinds},
        compiler_params=pltpu.CompilerParams(vmem_limit_bytes=FINISH_VMEM_BYTES),
        cost_estimate=pl.CostEstimate(flops=0, bytes_accessed=2**21, transcendentals=0),
        name="finish",
    )(*parts, x, table)


def flipped(array, axis, bits):
    if bits == 0:
        return array
    return lax.ppermute(array, axis, [(i, i ^ bits) for i in range(lax.axis_size(axis))])


def on_heads(query, key, value, dout, glob_keys, glob_values, glob_ids, rand_blocks):
    head_count, block_count, _ = rand_blocks.shape
    head_size = query.shape[2] // head_count
    table_size = glob_keys.shape[0]
    head = lax.axis_index("ctx").astype(jnp.int32)
    packed = pack(query, key, value, dout, head_count)
    chunks = [flipped(packed[flip], "ctx", flip) for flip in ORDER]
    place = jnp.concatenate([head[None], glob_ids[0]])
    rand_head = lax.dynamic_index_in_dim(rand_blocks, head, 0, keepdims=False).reshape(-1)
    rand_head = jnp.clip(rand_head, 0, block_count - 1)
    chosen, chunks[0] = choose(place, glob_keys, glob_values, packed[0])
    held, (kept, given) = scores(chunks, chosen, place, rand_head, table_size)
    given = flipped(given, "dp", 1)
    sent = grads(rand_head, chosen, held)
    given, sent = lax.optimization_barrier((given, sent))
    back = lax.all_to_all(sent, "ctx", 0, 0)
    chip = added(kept, given)
    column = jnp.stack([flipped(chip, "ctx", flip) for flip in COLUMN])
    even = added(column, flipped(column, "dp", 2))
    odd = flipped(even, "ctx", 1)
    beside_even = flipped(even, "dp", 1)
    beside_odd = flipped(odd, "dp", 1)
    d_table = early_table(head_count, ((0,), (1,)), [even, beside_even])
    d_query, d_key, d_value, d_table = finish(
        back, d_table, ((0,), (1,)), [odd, beside_odd]
    )
    return (d_query, d_key, d_value, d_table.reshape((2,) + glob_keys.shape))


def on_device(query, key, value, dout, glob_keys, glob_values, glob_ids, rand_blocks):
    head_count = rand_blocks.shape[0]
    one_head_each = lax.axis_size("ctx") == head_count == 8 and query.shape[1] == 2 * BLK
    if one_head_each and lax.axis_size("dp") == 4 and glob_keys.shape[0] % 2 == 0:
        plan = on_heads
    else:
        plan = on_ring
    return plan(query, key, value, dout, glob_keys, glob_values, glob_ids, rand_blocks)


def solution(mesh):
    placed = (
        P("dp", "ctx", None),
        P("dp", "ctx", None),
        P("dp", "ctx", None),
        P("dp", "ctx", None),
        P(),
        P(),
        P("dp", None),
        P(),
    )
    return jax.shard_map(
        on_device,
        mesh=mesh,
        in_specs=placed,
        out_specs=(P("dp", "ctx", None), P("dp", "ctx", None), P("dp", "ctx", None), P()),
        check_vma=False,
    )
```
